32 devices in a mesh: groups: 2 (over y), dp: 16 (over z, x, core).
Axes of the slice: x: 2, y: 2, z: 4, core: 2. Of those that a mesh axis runs over, the one named last changes fastest.
Arguments:
- teacher_post: bfloat16 [32, 3, 2048], P(('groups', 'dp')), parts along dimension 0, may hold values from 0 to 1, as said below
- assignment: int32 [32], P('groups'), parts along dimension 0, may hold values from 0 to 15, each once
- encoder_out: bfloat16 [32, 64, 640], P(('groups', 'dp')), parts along dimension 0, may hold values from -5 to 5
- predictor_out: bfloat16 [32, 32, 640], P(('groups', 'dp')), parts along dimension 0, may hold values from -5 to 5
- frame_lengths: int32 [32], P(('groups', 'dp')), parts along dimension 0, may hold values from 16 to 64, as said below
- token_lengths: int32 [32], P(('groups', 'dp')), parts along dimension 0, may hold values from 1 to 31, as said below
- labels: int32 [32, 31], P(('groups', 'dp')), parts along dimension 0, may hold values from 1 to 1023
- out_weight: bfloat16 [640, 1024], replicated, may hold values from -1 to 1
- out_bias: float32 [1024], replicated, may hold values from -5 to 5
Outputs:
- utt_loss: float32 [32], P(('groups', 'dp')), parts along dimension 0
- grad_weight: float32 [1280, 1024], P('groups'), parts along dimension 0
- grad_bias: float32 [2048], P('groups'), parts along dimension 0
- grad_encoder: bfloat16 [32, 64, 640], P(('groups', 'dp')), parts along dimension 0
- grad_predictor: bfloat16 [32, 32, 640], P(('groups', 'dp')), parts along dimension 0
The draws below stay inside these ranges and needn't reach their ends.
There are 2 independent parts, one for each index of `groups`. The reference program is written for one: setup_inputs(seed, part) draws one part's arguments, and reference() takes and returns one part's arrays. A program takes and returns all parts, laid end to end along the dimension named above; an argument that names none is the same for every part. Nothing has to cross between parts.
Inputs may be any that keep to these rules, and one draw needn't show every extreme that they name: `frame_lengths`: one utterance of each group has exactly 64 frames. `token_lengths`: one utterance of each group has exactly 31 labels. `teacher_post`: each cell's three posteriors are positive and sum to about one.
All inputs are finite; a program needn't handle non-finite values.
Results may differ from the reference program's by a relative error of at most 0.0042.
Values may be sent and summed in bfloat16 or wider, within the bound.
No kernel may reach another device: no remote copies, remote signals or barrier semaphores. Data moves between devices by JAX's collectives and lax.ppermute only.
A program may use at most 64 MiB of HBM per device.

```python
import jax
import jax.numpy as jnp
from jax import lax

H = 640
V = 1024
FR = 64
TOK = 31
FB = 16
TOKP = 32
CELLS = 2048
UTT = 16


def draw_teacher_post(key, part):
    key = jax.random.fold_in(key, 11)
    logit_draw = 1.5 * jax.random.normal(key, (UTT, 3, CELLS), jnp.float32)
    return jax.nn.softmax(logit_draw, axis=1).astype(jnp.bfloat16)


def draw_frame_lengths(key, part):
    key = jax.random.fold_in(key, 12)
    lengths_key, place_key = jax.random.split(key)
    drawn = jax.random.randint(lengths_key, (UTT,), FB, FR + 1)
    longest = jax.random.randint(place_key, (), 0, UTT)
    return jnp.where(jnp.arange(UTT) == longest, FR, drawn).astype(jnp.int32)


def draw_token_lengths(key, part):
    key = jax.random.fold_in(key, 13)
    lengths_key, place_key = jax.random.split(key)
    drawn = jax.random.randint(lengths_key, (UTT,), 1, TOK + 1)
    longest = jax.random.randint(place_key, (), 0, UTT)
    return jnp.where(jnp.arange(UTT) == longest, TOK, drawn).astype(jnp.int32)


def draw_encoder_out(key, part):
    key = jax.random.fold_in(key, 14)
    return jnp.clip(0.7 * jax.random.normal(key, (UTT, FR, H), jnp.float32), -5.0, 5.0).astype(jnp.bfloat16)


def draw_out_weight(key, part):
    key = jax.random.fold_in(key, 21)
    spread = 1.0 / H ** 0.5
    return jnp.clip(spread * jax.random.normal(key, (H, V), jnp.float32), -6.0 * spread, 6.0 * spread).astype(jnp.bfloat16)


def draw_out_bias(key, part):
    key = jax.random.fold_in(key, 23)
    return jnp.clip(jax.random.normal(key, (V,), jnp.float32), -5.0, 5.0).astype(jnp.float32)


def touch_ends(result, key, smallest, high):
    longest = result.shape.index(max(result.shape))
    spots = []
    for shift in (0, 1):
        where = [jax.random.randint(jax.random.fold_in(key, axis), (), 0, length) for axis, length in enumerate(result.shape)]
        where[longest] = (where[longest] + shift) % result.shape[longest]
        spots.append(tuple(where))
    return result.at[spots[0]].set(smallest).at[spots[1]].set(high)


def levels(key, extent, shards, low, high):
    factor_of, own = 1.0, jax.random.fold_in(key, 6)
    for dim, shards_of in shards:
        heights = jnp.exp(jax.random.uniform(jax.random.fold_in(own, dim), (shards_of,), jnp.float32, low / len(shards), high / len(shards)))
        factor_of = factor_of * jnp.repeat(heights, extent[dim] // shards_of).reshape([-1 if axis == dim else 1 for axis in range(len(extent))])
    return factor_of


def gaussian(rng, extent, width, most, pieces=(), held_as=jnp.bfloat16):
    values = width * jax.random.normal(rng, extent, jnp.float32)
    if pieces:
        values = values * levels(rng, extent, pieces, -0.22, 0.18)
    return jnp.clip(values, -most, most).astype(held_as)


def setup_inputs(seed: int = 0, part: int = 0) -> dict:
    splits = jax.random.split(jax.random.key(seed), 10)
    part_splits = jax.random.split(jax.random.fold_in(splits[9], part), 10)
    teacher_post = draw_teacher_post(jax.random.fold_in(jax.random.fold_in(splits[9], part), 71), part)
    assignment = jax.random.permutation(part_splits[1], UTT).astype(jnp.int32)
    encoder_out = draw_encoder_out(jax.random.fold_in(jax.random.fold_in(splits[9], part), 71), part)
    predictor_out = gaussian(part_splits[3], (UTT, TOKP, H), 0.7, 5.0, ((0, 16),))
    frame_lengths = draw_frame_lengths(jax.random.fold_in(jax.random.fold_in(splits[9], part), 71), part)
    token_lengths = draw_token_lengths(jax.random.fold_in(jax.random.fold_in(splits[9], part), 71), part)
    labels = touch_ends(jax.random.randint(part_splits[6], (UTT, TOK), 1, V), jax.random.fold_in(part_splits[6], 1), 1, V - 1).astype(jnp.int32)
    out_weight = draw_out_weight(jax.random.fold_in(splits[9], 71), part)
    out_bias = draw_out_bias(jax.random.fold_in(splits[9], 71), part)
    return {"teacher_post": teacher_post, "assignment": assignment, "encoder_out": encoder_out, "predictor_out": predictor_out, "frame_lengths": frame_lengths, "token_lengths": token_lengths, "labels": labels, "out_weight": out_weight, "out_bias": out_bias}


def collapse(logits, q_blank, q_label, q_rest, label_hot, weight_cell):
    vocab_ids = lax.broadcasted_iota(jnp.int32, logits.shape, 1)
    blank_hot = (vocab_ids == 0).astype(logits.dtype)
    rest_mask = (1.0 - blank_hot) * (1.0 - label_hot)
    row_max = jnp.max(logits, axis=1, keepdims=True)
    shifted = jnp.exp(logits - row_max)
    exp_total = jnp.sum(shifted, axis=1)
    rest_sum = jnp.sum(shifted * rest_mask, axis=1)
    log_norm = row_max[:, 0] + jnp.log(exp_total)
    label_logit = jnp.sum(logits * label_hot, axis=1)
    cell_loss = -(q_blank * (logits[:, 0] - log_norm) + q_label * (label_logit - log_norm)
                  + q_rest * (jnp.log(rest_sum) - jnp.log(exp_total)))
    soft_probs = shifted / exp_total[:, None]
    q_total = q_blank + q_label + q_rest
    d_logits = weight_cell[:, None] * (q_total[:, None] * soft_probs - q_blank[:, None] * blank_hot
                                       - q_label[:, None] * label_hot
                                       - q_rest[:, None] * rest_mask * shifted / rest_sum[:, None])
    return jnp.sum(cell_loss * weight_cell), d_logits


def reference(teacher_post, assignment, encoder_out, predictor_out, frame_lengths, token_lengths, labels, out_weight, out_bias):
    routed = jnp.take(teacher_post, assignment, axis=0)
    cell_ids = jnp.arange(CELLS, dtype=jnp.int32)
    frame_of = cell_ids // TOKP
    token_of = cell_ids % TOKP
    vocab_ids = lax.broadcasted_iota(jnp.int32, (CELLS, V), 1)

    def one_slot(state_carry, inputs):
        grad_w, grad_b = state_carry
        post_slot, enc_slot, pred_slot, frame_len, token_len, label_row = inputs
        joint_act = jnp.tanh(enc_slot.astype(jnp.float32)[:, None, :] + pred_slot.astype(jnp.float32)[None, :, :]).reshape(CELLS, H)
        joint_in = joint_act.astype(jnp.bfloat16)
        logits = jnp.dot(joint_in, out_weight, preferred_element_type=jnp.float32) + out_bias
        padded_lab = jnp.concatenate([label_row, jnp.zeros((1,), jnp.int32)])
        target = padded_lab[token_of]
        label_ok = token_of < token_len
        valid_cell = (frame_of < frame_len) & (token_of <= token_len)
        cell_count = (frame_len * (token_len + 1)).astype(jnp.float32)
        weight_cell = valid_cell.astype(jnp.float32) / cell_count
        label_hot = ((vocab_ids == target[:, None]) & label_ok[:, None]).astype(jnp.float32)
        post_f32 = post_slot.astype(jnp.float32)
        q_label = post_f32[1] * label_ok.astype(jnp.float32)
        slot_loss, d_logits = collapse(logits, post_f32[0], q_label, post_f32[2], label_hot, weight_cell)
        d_low = d_logits.astype(jnp.bfloat16)
        grad_w = grad_w + jnp.dot(joint_in.T, d_low, preferred_element_type=jnp.float32)
        grad_b = grad_b + jnp.sum(d_logits, axis=0)
        d_hidden = jnp.dot(d_low, out_weight.T, preferred_element_type=jnp.float32)
        d_pre = (d_hidden * (1.0 - joint_act * joint_act)).reshape(FR, TOKP, H)
        return (grad_w, grad_b), (slot_loss, jnp.sum(d_pre, axis=1).astype(jnp.bfloat16), jnp.sum(d_pre, axis=0).astype(jnp.bfloat16))

    initial = (jnp.zeros((H, V), jnp.float32), jnp.zeros((V,), jnp.float32))
    (grad_weight, grad_bias), (utt_loss, grad_encoder, grad_predictor) = lax.scan(
        one_slot, initial, (routed, encoder_out, predictor_out, frame_lengths, token_lengths, labels))
    return utt_loss, grad_weight, grad_bias, grad_encoder, grad_predictor
```

```python
import functools

import jax
import jax.numpy as jnp
from jax import lax
from jax.experimental import pallas as pl
from jax.experimental.pallas import tpu as pltpu
from jax.sharding import PartitionSpec as P

F32 = jnp.float32
BF16 = jnp.bfloat16
LANES = 128
EXTRA = 16
VMEM_LIMIT = 56 * 1024 * 1024


def params():
    return pltpu.CompilerParams(
        dimension_semantics=("arbitrary",), vmem_limit_bytes=VMEM_LIMIT
    )


def target_column(labels_ref, token_len, tok_slots, reps):
    tok = labels_ref.shape[1]
    row = lax.broadcasted_iota(jnp.int32, (tok_slots, tok), 0)
    lane = lax.broadcasted_iota(jnp.int32, (tok_slots, tok), 1)
    picked = jnp.where(row == lane, labels_ref[...].astype(F32), 0.0)
    column = jnp.sum(picked, axis=1, keepdims=True)
    token = lax.broadcasted_iota(jnp.int32, (tok_slots, 1), 0)
    column = jnp.where(token < token_len, column, -1.0).astype(jnp.int32)
    whole = jnp.broadcast_to(column[None], (reps, tok_slots, 1))
    return whole.reshape(reps * tok_slots, 1)


def forward_kernel(tlen_ref, labels_ref, enc_ref, pred_ref, w_ref, b_ref, e_ref, st_ref, jt_ref, enc_scr):
    step = pl.program_id(0)
    rows, vocab = e_ref.shape
    tok_slots, width = pred_ref.shape
    block_frames = rows // tok_slots

    @pl.when(step == 0)
    def _():
        enc_scr[...] = enc_ref[...].astype(F32)

    first = pl.multiple_of(step * block_frames, block_frames)
    enc = enc_scr[pl.ds(first, block_frames), :]
    pred = pred_ref[...].astype(F32)
    act = jnp.tanh(enc[:, None, :] + pred[None, :, :]).reshape(rows, width)
    joint_in = act.astype(BF16)
    jt_ref[...] = joint_in.T
    logits = jnp.dot(joint_in, w_ref[...], preferred_element_type=F32) + b_ref[...]
    row_max = jnp.max(logits, axis=1, keepdims=True)
    target = target_column(labels_ref, tlen_ref[0], tok_slots, block_frames)
    lane = lax.broadcasted_iota(jnp.int32, (rows, LANES), 1)
    rest_acc = jnp.zeros((rows, LANES), F32)
    label_acc = jnp.zeros((rows, LANES), F32)
    for j in range(vocab // LANES):
        shifted = logits[:, j * LANES : (j + 1) * LANES] - row_max
        e = jnp.exp(shifted)
        e_ref[:, j * LANES : (j + 1) * LANES] = e
        hot = lane == target - j * LANES
        rest = jnp.where(hot, 0.0, e)
        if j == 0:
            z_blank = shifted[:, 0:1]
            rest = jnp.where(lane == 0, 0.0, rest)
        rest_acc = rest_acc + rest
        label_acc = label_acc + jnp.where(hot, shifted, 0.0)
    rest_sum = jnp.sum(rest_acc, axis=1, keepdims=True)
    z_label = jnp.sum(label_acc, axis=1, keepdims=True)
    e_label = jnp.where(target >= 0, jnp.exp(z_label), 0.0)
    total = rest_sum + jnp.exp(z_blank) + e_label
    st_ref[...] = jnp.concatenate([total, rest_sum, z_blank, z_label], axis=1)


def grad_kernel(
    pick_ref, flen_ref, tlen_ref, labels_ref, qa_ref, qb_ref, e_ref, st_ref, jt_ref,
    d_ref, loss_ref, send_ref, keep_ref, keepb_ref, d_scr, gb_scr, loss_scr,
):
    step = pl.program_id(0)
    steps = pl.num_programs(0)
    rows, vocab = e_ref.shape
    tok_slots = labels_ref.shape[1] + 1
    block_frames = rows // tok_slots
    width = jt_ref.shape[0]

    @pl.when(step == 0)
    def _():
        gb_scr[...] = jnp.zeros_like(gb_scr)
        loss_scr[...] = jnp.zeros_like(loss_scr)

    half_count = pick_ref[1]
    chosen = jnp.where(pick_ref[0] < half_count, qa_ref[0].astype(F32), qb_ref[0].astype(F32))
    padded = jnp.concatenate([chosen, jnp.zeros((5, rows), F32)], axis=0)
    q = padded.T
    frame_len, token_len = flen_ref[0], tlen_ref[0]
    row = lax.broadcasted_iota(jnp.int32, (block_frames, tok_slots, 1), 0).reshape(rows, 1)
    frame = row + step * block_frames
    token = lax.broadcasted_iota(jnp.int32, (block_frames, tok_slots, 1), 1).reshape(rows, 1)
    count = (frame_len * (token_len + 1)).astype(F32)
    weight = jnp.where((frame < frame_len) & (token <= token_len), 1.0 / count, 0.0)
    q_blank = q[:, 0:1]
    q_label = jnp.where(token < token_len, q[:, 1:2], 0.0)
    q_rest = q[:, 2:3]
    total = st_ref[:, 0:1]
    rest_sum = st_ref[:, 1:2]
    z_blank = st_ref[:, 2:3]
    z_label = st_ref[:, 3:4]
    log_total = jnp.log(total)
    cell_loss = -(
        q_blank * (z_blank - log_total)
        + q_label * (z_label - log_total)
        + q_rest * (jnp.log(rest_sum) - log_total)
    )
    loss_scr[...] += jnp.sum((cell_loss * weight).reshape(rows // 8, 8, 1), axis=0)
    soft = weight * (q_blank + q_label + q_rest) / total
    scale = soft - weight * q_rest / rest_sum
    d_blank = soft * jnp.exp(z_blank) - weight * q_blank
    d_label = soft * jnp.exp(z_label) - weight * q_label
    target = target_column(labels_ref, token_len, tok_slots, block_frames)
    lane = lax.broadcasted_iota(jnp.int32, (rows, LANES), 1)
    base = pl.multiple_of(step * rows, rows)
    for j in range(vocab // LANES):
        cols = slice(j * LANES, (j + 1) * LANES)
        d = jnp.where(lane == target - j * LANES, d_label, e_ref[:, cols] * scale)
        if j == 0:
            d = jnp.where(lane == 0, d_blank, d)
        low = d.astype(BF16)
        d_ref[:, cols] = low
        d_scr[pl.ds(base, rows), cols] = low
        gb_scr[:, cols] += jnp.sum(d.reshape(rows // 8, 8, LANES), axis=0)

    @pl.when(step == steps - 1)
    def _():
        loss_ref[...] = jnp.broadcast_to(jnp.sum(loss_scr[...], axis=0, keepdims=True), loss_ref.shape)
        part = vocab // 2
        tile = part // 2
        core = pick_ref[2]
        for j in range(2):
            col = pl.multiple_of((1 - core) * part + j * tile, tile)
            dw = jnp.dot(jt_ref[...], d_scr[:, pl.ds(col, tile)], preferred_element_type=F32)
            send_ref[:width, j * tile : (j + 1) * tile] = dw.astype(BF16)
        for j in range(2):
            col = pl.multiple_of(core * part + j * tile, tile)
            dw = jnp.dot(jt_ref[...], d_scr[:, pl.ds(col, tile)], preferred_element_type=F32)
            keep_ref[:, j * tile : (j + 1) * tile] = dw
        bias = jnp.sum(gb_scr[...], axis=0, keepdims=True)
        first, second = bias[:, :part], bias[:, part:]
        mine = jnp.where(core == 0, first, second)
        other = jnp.where(core == 0, second, first)
        keepb_ref[...] = mine
        high = other.astype(BF16)
        low = (other - high.astype(F32)).astype(BF16)
        place = lax.broadcasted_iota(jnp.int32, (EXTRA, part), 0)
        packed = jnp.where(place == 0, high.astype(F32), jnp.where(place == 1, low.astype(F32), 0.0))
        send_ref[width:, :] = packed.astype(BF16)


def input_kernel(enc_ref, pred_ref, d_ref, w_ref, ge_ref, gp_ref, enc_scr, ge_scr, gp_scr):
    step = pl.program_id(0)
    steps = pl.num_programs(0)
    rows = d_ref.shape[0]
    tok_slots, width = pred_ref.shape
    block_frames = rows // tok_slots

    @pl.when(step == 0)
    def _():
        enc_scr[...] = enc_ref[...].astype(F32)
        gp_scr[...] = jnp.zeros_like(gp_scr)

    first = pl.multiple_of(step * block_frames, block_frames)
    d_hidden = lax.dot_general(
        d_ref[...], w_ref[...], (((1,), (1,)), ((), ())), preferred_element_type=F32
    )
    enc = enc_scr[pl.ds(first, block_frames), :]
    act = jnp.tanh(enc[:, None, :] + pred_ref[...].astype(F32)[None, :, :])
    d_pre = d_hidden.reshape(block_frames, tok_slots, width) * (1.0 - act * act)
    ge_scr[pl.ds(first, block_frames), :] = jnp.sum(d_pre, axis=1)
    gp_scr[...] += jnp.sum(d_pre, axis=0)

    @pl.when(step == steps - 1)
    def _():
        ge_ref[...] = ge_scr[...].astype(BF16)
        gp_ref[...] = gp_scr[...].astype(BF16)


def whole(shape):
    return pl.BlockSpec(shape, lambda *_: (0,) * len(shape))


SMEM_SPEC = pl.BlockSpec(memory_space=pltpu.SMEM)


def forward(tlen, labels, enc, pred, w, bias, rows):
    frames, width = enc.shape
    tok_slots = pred.shape[0]
    vocab = w.shape[1]
    cells = frames * tok_slots
    return pl.pallas_call(
        forward_kernel,
        grid=(cells // rows,),
        in_specs=[
            SMEM_SPEC, whole(labels.shape), whole(enc.shape), whole(pred.shape),
            whole(w.shape), whole(bias.shape),
        ],
        out_specs=[
            pl.BlockSpec((rows, vocab), lambda i: (i, 0)),
            pl.BlockSpec((rows, 4), lambda i: (i, 0)),
            pl.BlockSpec((width, rows), lambda i: (0, i)),
        ],
        out_shape=[
            jax.ShapeDtypeStruct((cells, vocab), F32),
            jax.ShapeDtypeStruct((cells, 4), F32),
            jax.ShapeDtypeStruct((width, cells), BF16),
        ],
        scratch_shapes=[pltpu.VMEM((frames, width), F32)],
        compiler_params=params(),
        cost_estimate=pl.CostEstimate(
            flops=2 * cells * width * vocab, bytes_accessed=16 * 1024 * 1024,
            transcendentals=cells * (width + vocab),
        ),
    )(tlen, labels, enc, pred, w, bias)


def gradients(pick, flen, tlen, labels, qa, qb, e, st, jt, rows):
    cells, vocab = e.shape
    width = jt.shape[0]
    part = vocab // 2
    smem = pl.BlockSpec(memory_space=pltpu.SMEM)
    grid_spec = pltpu.PrefetchScalarGridSpec(
        num_scalar_prefetch=1,
        grid=(cells // rows,),
        in_specs=[
            smem, smem, whole(labels.shape),
            pl.BlockSpec((1, 3, rows), lambda i, pick: (lax.rem(pick[0], pick[1]), 0, i)),
            pl.BlockSpec((1, 3, rows), lambda i, pick: (lax.rem(pick[0], pick[1]), 0, i)),
            pl.BlockSpec((rows, vocab), lambda i, pick: (i, 0)),
            pl.BlockSpec((rows, 4), lambda i, pick: (i, 0)),
            whole(jt.shape),
        ],
        out_specs=[
            pl.BlockSpec((rows, vocab), lambda i, pick: (i, 0)),
            whole((8, LANES)),
            whole((width + EXTRA, part)),
            whole((width, part)),
            whole((1, part)),
        ],
        scratch_shapes=[
            pltpu.VMEM((cells, vocab), BF16),
            pltpu.VMEM((8, vocab), F32),
            pltpu.VMEM((8, 1), F32),
        ],
    )
    return pl.pallas_call(
        grad_kernel,
        grid_spec=grid_spec,
        out_shape=[
            jax.ShapeDtypeStruct((cells, vocab), BF16),
            jax.ShapeDtypeStruct((8, LANES), F32),
            jax.ShapeDtypeStruct((width + EXTRA, part), BF16),
            jax.ShapeDtypeStruct((width, part), F32),
            jax.ShapeDtypeStruct((1, part), F32),
        ],
        compiler_params=params(),
        cost_estimate=pl.CostEstimate(
            flops=2 * cells * width * vocab, bytes_accessed=16 * 1024 * 1024, transcendentals=cells * 8
        ),
    )(pick, flen, tlen, labels, qa, qb, e, st, jt)


def input_gradients(enc, pred, d_low, w, rows):
    cells, vocab = d_low.shape
    return pl.pallas_call(
        input_kernel,
        grid=(cells // rows,),
        in_specs=[
            whole(enc.shape), whole(pred.shape),
            pl.BlockSpec((rows, vocab), lambda i: (i, 0)), whole(w.shape),
        ],
        out_specs=[whole(enc.shape), whole(pred.shape)],
        out_shape=[
            jax.ShapeDtypeStruct(enc.shape, BF16),
            jax.ShapeDtypeStruct(pred.shape, BF16),
        ],
        scratch_shapes=[
            pltpu.VMEM(enc.shape, F32), pltpu.VMEM(enc.shape, F32), pltpu.VMEM(pred.shape, F32)
        ],
        compiler_params=params(),
        cost_estimate=pl.CostEstimate(
            flops=2 * cells * w.shape[0] * vocab, bytes_accessed=6 * 1024 * 1024,
            transcendentals=cells * w.shape[0],
        ),
    )(enc, pred, d_low, w)


def split_two(value):
    high = lax.reduce_precision(value, 8, 7)
    return high, lax.reduce_precision(value - high, 8, 7)


def on_device(
    dp, teacher_post, assignment, encoder_out, predictor_out, frame_lengths, token_lengths,
    labels, out_weight, out_bias,
):
    own = lax.axis_index("dp")
    core = own & 1
    masks = [1 << k for k in range(dp.bit_length() - 1)]
    enc, pred = encoder_out[0], predictor_out[0]
    rows = 8 * pred.shape[0]
    width, vocab = out_weight.shape
    part = vocab // 2

    def exchange(value, even, odd):
        pairs = [(k, k ^ (odd if k & 1 else even)) for k in range(dp)]
        return lax.ppermute(value, "dp", pairs)

    held = teacher_post
    for mask in masks[:-1]:
        held = jnp.concatenate([held, exchange(held, mask, mask)], axis=0)
    far = exchange(held, masks[-1], masks[-1])
    place = lax.dynamic_index_in_dim(assignment, own, keepdims=False) ^ own
    pick = jnp.stack([place, jnp.int32(dp // 2), core]).astype(jnp.int32)

    e, st, jt = forward(
        token_lengths, labels, enc, pred, out_weight, out_bias.reshape(1, vocab), rows
    )
    d_low, loss, send, keep, bias = gradients(
        pick, frame_lengths, token_lengths, labels, held, far, e, st, jt, rows
    )
    got = exchange(send, 1, 1)
    grad_enc, grad_pred = input_gradients(enc, pred, d_low, out_weight, rows)

    def got_bias(rows_of):
        return rows_of[0:1].astype(F32) + rows_of[1:2].astype(F32)

    def bias_rows(high, low):
        filler = jnp.zeros((EXTRA - 2, part), BF16)
        return jnp.concatenate([high.astype(BF16), low.astype(BF16), filler], axis=0)

    acc = keep + got[:width].astype(F32)
    bias = bias + got_bias(got[width:])
    rest = masks[1:]
    even_order = rest[:1] + rest[1:][::-1]
    odd_order = rest[1:2] + rest[:1] + rest[2:]
    sides = []
    count = width
    for even, odd in zip(even_order, odd_order):
        side = (own & jnp.where(core == 0, even, odd)) != 0
        sides.append(side)
        count //= 2
        top, bottom = acc[:count], acc[count:]
        high, low = split_two(bias)
        send = jnp.where(side, top, bottom).astype(BF16)
        got = exchange(jnp.concatenate([send, bias_rows(high, low)], axis=0), even, odd)
        acc = jnp.where(side, bottom, top) + got[:count].astype(F32)
        bias = (high + low) + got_bias(got[count:])
    have = acc.astype(BF16)
    for even, odd, side in list(zip(even_order, odd_order, sides))[::-1]:
        got = exchange(have, even, odd)
        have = jnp.where(
            side, jnp.concatenate([got, have], axis=0), jnp.concatenate([have, got], axis=0)
        )
    high, low = split_two(bias)
    got = exchange(jnp.concatenate([have, bias_rows(high, low)], axis=0), 1, 1)
    other = got[:width]
    grad_weight = jnp.where(
        core == 0, jnp.concatenate([have, other], axis=1), jnp.concatenate([other, have], axis=1)
    ).astype(F32)
    bias, other_bias = high + low, got_bias(got[width:])
    grad_bias = jnp.where(
        core == 0,
        jnp.concatenate([bias, other_bias], axis=1),
        jnp.concatenate([other_bias, bias], axis=1),
    ).reshape(vocab)
    return (loss[0, 0:1], grad_weight, grad_bias, grad_enc[None], grad_pred[None])


def solution(mesh):
    in_specs = (
        P(("groups", "dp"), None, None),
        P("groups"),
        P(("groups", "dp"), None, None),
        P(("groups", "dp"), None, None),
        P(("groups", "dp")),
        P(("groups", "dp")),
        P(("groups", "dp"), None),
        P(),
        P(),
    )
    out_specs = (
        P(("groups", "dp")),
        P("groups", None),
        P("groups"),
        P(("groups", "dp"), None, None),
        P(("groups", "dp"), None, None),
    )
    return jax.shard_map(
        functools.partial(on_device, mesh.shape["dp"]),
        mesh=mesh, in_specs=in_specs, out_specs=out_specs, check_vma=False,
    )
```

```python
import functools

import jax
import jax.numpy as jnp
from jax import lax
from jax.experimental import pallas as pl
from jax.experimental.pallas import tpu as pltpu
from jax.sharding import PartitionSpec as P

F32 = jnp.float32
BF16 = jnp.bfloat16
LANES = 128
EXTRA = 16
VMEM_LIMIT = 56 * 1024 * 1024


def params():
    return pltpu.CompilerParams(
        dimension_semantics=("arbitrary",), vmem_limit_bytes=VMEM_LIMIT
    )


def target_column(labels_ref, token_len, tok_slots, reps):
    tok = labels_ref.shape[1]
    row = lax.broadcasted_iota(jnp.int32, (tok_slots, tok), 0)
    lane = lax.broadcasted_iota(jnp.int32, (tok_slots, tok), 1)
    picked = jnp.where(row == lane, labels_ref[...].astype(F32), 0.0)
    column = jnp.sum(picked, axis=1, keepdims=True)
    token = lax.broadcasted_iota(jnp.int32, (tok_slots, 1), 0)
    column = jnp.where(token < token_len, column, -1.0).astype(jnp.int32)
    whole = jnp.broadcast_to(column[None], (reps, tok_slots, 1))
    return whole.reshape(reps * tok_slots, 1)


def forward_kernel(begin, tlen_ref, labels_ref, enc_ref, pred_ref, w_ref, b_ref, *refs):
    e_ref, st_ref, jt_ref, enc_scr = refs[-4:]
    step = pl.program_id(0)
    rows, vocab = e_ref.shape
    tok_slots, width = pred_ref.shape
    block_frames = rows // tok_slots

    @pl.when(step == 0)
    def _():
        enc_scr[...] = enc_ref[...].astype(F32)

    first = pl.multiple_of((begin + step) * block_frames, block_frames)
    enc = enc_scr[pl.ds(first, block_frames), :]
    pred = pred_ref[...].astype(F32)
    act = jnp.tanh(enc[:, None, :] + pred[None, :, :]).reshape(rows, width)
    joint_in = act.astype(BF16)
    jt_ref[...] = joint_in.T
    logits = jnp.dot(joint_in, w_ref[...], preferred_element_type=F32) + b_ref[...]
    row_max = jnp.max(logits, axis=1, keepdims=True)
    target = target_column(labels_ref, tlen_ref[0], tok_slots, block_frames)
    lane = lax.broadcasted_iota(jnp.int32, (rows, LANES), 1)
    rest_acc = jnp.zeros((rows, LANES), F32)
    label_acc = jnp.zeros((rows, LANES), F32)
    for j in range(vocab // LANES):
        shifted = logits[:, j * LANES : (j + 1) * LANES] - row_max
        e = jnp.exp(shifted)
        e_ref[:, j * LANES : (j + 1) * LANES] = e
        hot = lane == target - j * LANES
        rest = jnp.where(hot, 0.0, e)
        if j == 0:
            z_blank = shifted[:, 0:1]
            rest = jnp.where(lane == 0, 0.0, rest)
        rest_acc = rest_acc + rest
        label_acc = label_acc + jnp.where(hot, shifted, 0.0)
    rest_sum = jnp.sum(rest_acc, axis=1, keepdims=True)
    z_label = jnp.sum(label_acc, axis=1, keepdims=True)
    e_label = jnp.where(target >= 0, jnp.exp(z_label), 0.0)
    total = rest_sum + jnp.exp(z_blank) + e_label
    st_ref[...] = jnp.concatenate([total, rest_sum, z_blank, z_label], axis=1)


def grad_kernel(
    pick_ref, flen_ref, tlen_ref, labels_ref, qa_ref, qb_ref, e_ref, st_ref, jt_ref,
    d_ref, loss_ref, send_ref, keep_ref, keepb_ref, d_scr, gb_scr, loss_scr,
):
    step = pl.program_id(0)
    steps = pl.num_programs(0)
    rows, vocab = e_ref.shape
    tok_slots = labels_ref.shape[1] + 1
    block_frames = rows // tok_slots
    width = jt_ref.shape[0]

    @pl.when(step == 0)
    def _():
        gb_scr[...] = jnp.zeros_like(gb_scr)
        loss_scr[...] = jnp.zeros_like(loss_scr)

    half_count = pick_ref[1]
    chosen = jnp.where(pick_ref[0] < half_count, qa_ref[0].astype(F32), qb_ref[0].astype(F32))
    padded = jnp.concatenate([chosen, jnp.zeros((5, rows), F32)], axis=0)
    q = padded.T
    frame_len, token_len = flen_ref[0], tlen_ref[0]
    row = lax.broadcasted_iota(jnp.int32, (block_frames, tok_slots, 1), 0).reshape(rows, 1)
    frame = row + step * block_frames
    token = lax.broadcasted_iota(jnp.int32, (block_frames, tok_slots, 1), 1).reshape(rows, 1)
    count = (frame_len * (token_len + 1)).astype(F32)
    weight = jnp.where((frame < frame_len) & (token <= token_len), 1.0 / count, 0.0)
    q_blank = q[:, 0:1]
    q_label = jnp.where(token < token_len, q[:, 1:2], 0.0)
    q_rest = q[:, 2:3]
    total = st_ref[:, 0:1]
    rest_sum = st_ref[:, 1:2]
    z_blank = st_ref[:, 2:3]
    z_label = st_ref[:, 3:4]
    log_total = jnp.log(total)
    cell_loss = -(
        q_blank * (z_blank - log_total)
        + q_label * (z_label - log_total)
        + q_rest * (jnp.log(rest_sum) - log_total)
    )
    loss_scr[...] += jnp.sum((cell_loss * weight).reshape(rows // 8, 8, 1), axis=0)
    soft = weight * (q_blank + q_label + q_rest) / total
    scale = soft - weight * q_rest / rest_sum
    d_blank = soft * jnp.exp(z_blank) - weight * q_blank
    d_label = soft * jnp.exp(z_label) - weight * q_label
    target = target_column(labels_ref, token_len, tok_slots, block_frames)
    lane = lax.broadcasted_iota(jnp.int32, (rows, LANES), 1)
    base = pl.multiple_of(step * rows, rows)
    for j in range(vocab // LANES):
        cols = slice(j * LANES, (j + 1) * LANES)
        d = jnp.where(lane == target - j * LANES, d_label, e_ref[:, cols] * scale)
        if j == 0:
            d = jnp.where(lane == 0, d_blank, d)
        low = d.astype(BF16)
        d_ref[:, cols] = low
        d_scr[pl.ds(base, rows), cols] = low
        gb_scr[:, cols] += jnp.sum(d.reshape(rows // 8, 8, LANES), axis=0)

    @pl.when(step == steps - 1)
    def _():
        loss_ref[...] = jnp.broadcast_to(jnp.sum(loss_scr[...], axis=0, keepdims=True), loss_ref.shape)
        part = vocab // 2
        tile = part // 2
        core = pick_ref[2]
        for j in range(2):
            col = pl.multiple_of((1 - core) * part + j * tile, tile)
            dw = jnp.dot(jt_ref[...], d_scr[:, pl.ds(col, tile)], preferred_element_type=F32)
            send_ref[:width, j * tile : (j + 1) * tile] = dw.astype(BF16)
        for j in range(2):
            col = pl.multiple_of(core * part + j * tile, tile)
            dw = jnp.dot(jt_ref[...], d_scr[:, pl.ds(col, tile)], preferred_element_type=F32)
            keep_ref[:, j * tile : (j + 1) * tile] = dw
        bias = jnp.sum(gb_scr[...], axis=0, keepdims=True)
        first, second = bias[:, :part], bias[:, part:]
        mine = jnp.where(core == 0, first, second)
        other = jnp.where(core == 0, second, first)
        keepb_ref[...] = mine
        high = other.astype(BF16)
        low = (other - high.astype(F32)).astype(BF16)
        place = lax.broadcasted_iota(jnp.int32, (EXTRA, part), 0)
        packed = jnp.where(place == 0, high.astype(F32), jnp.where(place == 1, low.astype(F32), 0.0))
        send_ref[width:, :] = packed.astype(BF16)


def input_kernel(enc_ref, pred_ref, d_ref, w_ref, base_ref, ge_ref, gp_ref, enc_scr, ge_scr):
    step = pl.program_id(0)
    steps = pl.num_programs(0)
    rows = d_ref.shape[0]
    tok_slots, width = pred_ref.shape
    block_frames = rows // tok_slots

    @pl.when(step == 0)
    def _():
        enc_scr[...] = enc_ref[...].astype(F32)
        gp_ref[...] = base_ref[...]

    first = pl.multiple_of(step * block_frames, block_frames)
    d_hidden = lax.dot_general(
        d_ref[...], w_ref[...], (((1,), (1,)), ((), ())), preferred_element_type=F32
    )
    enc = enc_scr[pl.ds(first, block_frames), :]
    act = jnp.tanh(enc[:, None, :] + pred_ref[...].astype(F32)[None, :, :])
    d_pre = d_hidden.reshape(block_frames, tok_slots, width) * (1.0 - act * act)
    ge_scr[pl.ds(first, block_frames), :] = jnp.sum(d_pre, axis=1)
    gp_ref[...] += jnp.sum(d_pre, axis=0)

    @pl.when(step == steps - 1)
    def _():
        ge_ref[...] = ge_scr[...].astype(BF16)


def whole(shape):
    return pl.BlockSpec(shape, lambda *_: (0,) * len(shape))


SMEM_SPEC = pl.BlockSpec(memory_space=pltpu.SMEM)


def forward(tlen, labels, enc, pred, w, bias, rows, begin, blocks, before):
    frames, width = enc.shape
    tok_slots = pred.shape[0]
    vocab = w.shape[1]
    cells = frames * tok_slots
    return pl.pallas_call(
        functools.partial(forward_kernel, begin),
        grid=(blocks,),
        in_specs=[
            SMEM_SPEC, whole(labels.shape), whole(enc.shape), whole(pred.shape),
            whole(w.shape), whole(bias.shape),
        ] + [pl.BlockSpec(memory_space=pl.ANY)] * len(before),
        out_specs=[
            pl.BlockSpec((rows, vocab), lambda i: (i + begin, 0)),
            pl.BlockSpec((rows, 4), lambda i: (i + begin, 0)),
            pl.BlockSpec((width, rows), lambda i: (0, i + begin)),
        ],
        out_shape=[
            jax.ShapeDtypeStruct((cells, vocab), F32),
            jax.ShapeDtypeStruct((cells, 4), F32),
            jax.ShapeDtypeStruct((width, cells), BF16),
        ],
        scratch_shapes=[pltpu.VMEM((frames, width), F32)],
        input_output_aliases={6 + k: k for k in range(len(before))},
        compiler_params=params(),
        cost_estimate=pl.CostEstimate(
            flops=2 * blocks * rows * width * vocab, bytes_accessed=blocks * rows * vocab * 8,
            transcendentals=blocks * rows * (width + vocab),
        ),
    )(tlen, labels, enc, pred, w, bias, *before)


def gradients(pick, flen, tlen, labels, qa, qb, e, st, jt, rows):
    cells, vocab = e.shape
    width = jt.shape[0]
    part = vocab // 2
    smem = pl.BlockSpec(memory_space=pltpu.SMEM)
    grid_spec = pltpu.PrefetchScalarGridSpec(
        num_scalar_prefetch=1,
        grid=(cells // rows,),
        in_specs=[
            smem, smem, whole(labels.shape),
            pl.BlockSpec((1, 3, rows), lambda i, pick: (lax.rem(pick[0], pick[1]), 0, i)),
            pl.BlockSpec((1, 3, rows), lambda i, pick: (lax.rem(pick[0], pick[1]), 0, i)),
            pl.BlockSpec((rows, vocab), lambda i, pick: (i, 0)),
            pl.BlockSpec((rows, 4), lambda i, pick: (i, 0)),
            whole(jt.shape),
        ],
        out_specs=[
            pl.BlockSpec((rows, vocab), lambda i, pick: (i, 0)),
            whole((8, LANES)),
            whole((width + EXTRA, part)),
            whole((width, part)),
            whole((1, part)),
        ],
        scratch_shapes=[
            pltpu.VMEM((cells, vocab), BF16),
            pltpu.VMEM((8, vocab), F32),
            pltpu.VMEM((8, 1), F32),
        ],
    )
    return pl.pallas_call(
        grad_kernel,
        grid_spec=grid_spec,
        out_shape=[
            jax.ShapeDtypeStruct((cells, vocab), BF16),
            jax.ShapeDtypeStruct((8, LANES), F32),
            jax.ShapeDtypeStruct((width + EXTRA, part), BF16),
            jax.ShapeDtypeStruct((width, part), F32),
            jax.ShapeDtypeStruct((1, part), F32),
        ],
        compiler_params=params(),
        cost_estimate=pl.CostEstimate(
            flops=2 * cells * width * vocab, bytes_accessed=16 * 1024 * 1024, transcendentals=cells * 8
        ),
    )(pick, flen, tlen, labels, qa, qb, e, st, jt)


def input_gradients(enc, pred, d_low, w, base, rows, begin):
    vocab = d_low.shape[1]
    cells = enc.shape[0] * pred.shape[0]
    return pl.pallas_call(
        input_kernel,
        grid=(cells // rows,),
        in_specs=[
            whole(enc.shape), whole(pred.shape),
            pl.BlockSpec((rows, vocab), lambda i: (i + begin, 0)), whole(w.shape), whole(base.shape),
        ],
        out_specs=[whole(enc.shape), whole(pred.shape)],
        out_shape=[
            jax.ShapeDtypeStruct(enc.shape, BF16),
            jax.ShapeDtypeStruct(pred.shape, F32),
        ],
        scratch_shapes=[pltpu.VMEM(enc.shape, F32), pltpu.VMEM(enc.shape, F32)],
        compiler_params=params(),
        cost_estimate=pl.CostEstimate(
            flops=2 * cells * w.shape[0] * vocab, bytes_accessed=cells * vocab * 4,
            transcendentals=cells * w.shape[0],
        ),
    )(enc, pred, d_low, w, base)


def split_two(value):
    high = lax.reduce_precision(value, 8, 7)
    return high, lax.reduce_precision(value - high, 8, 7)


def on_device(
    dp, teacher_post, assignment, encoder_out, predictor_out, frame_lengths, token_lengths,
    labels, out_weight, out_bias,
):
    own = lax.axis_index("dp")
    core = own & 1
    masks = [1 << k for k in range(dp.bit_length() - 1)]
    enc, pred = encoder_out[0], predictor_out[0]
    rows = 8 * pred.shape[0]
    width, vocab = out_weight.shape
    part = vocab // 2

    def exchange(value, even, odd):
        pairs = [(k, k ^ (odd if k & 1 else even)) for k in range(dp)]
        return lax.ppermute(value, "dp", pairs)

    blocks = enc.shape[0] * pred.shape[0] // rows
    quarter = blocks // 4
    shares = [(0, quarter), (quarter, quarter), (2 * quarter, blocks - 2 * quarter)]
    bias_row = out_bias.reshape(1, vocab)
    held, made = teacher_post, ()
    for k, mask in enumerate(masks):
        got = exchange(held, mask, mask)
        part_no = k - (len(masks) - len(shares))
        if part_no >= 0:
            begin, number = shares[part_no]
            made = tuple(forward(
                token_lengths, labels, enc, pred, out_weight, bias_row, rows, begin, number, made
            ))
        if k < len(masks) - 1:
            held = jnp.concatenate([held, got], axis=0)
            held, made = lax.optimization_barrier((held, made))
    far = got
    e, st, jt = made
    place = lax.dynamic_index_in_dim(assignment, own, keepdims=False) ^ own
    pick = jnp.stack([place, jnp.int32(dp // 2), core]).astype(jnp.int32)
    d_low, loss, send, keep, bias = gradients(
        pick, frame_lengths, token_lengths, labels, held, far, e, st, jt, rows
    )
    got = exchange(send, 1, 1)

    def got_bias(rows_of):
        return rows_of[0:1].astype(F32) + rows_of[1:2].astype(F32)

    def bias_rows(high, low):
        filler = jnp.zeros((EXTRA - 2, part), BF16)
        return jnp.concatenate([high.astype(BF16), low.astype(BF16), filler], axis=0)

    acc = keep + got[:width].astype(F32)
    bias = bias + got_bias(got[width:])
    rest = masks[1:]
    even_order = rest
    odd_order = rest[1:2] + rest[:1] + rest[2:]
    orders = list(zip(even_order, odd_order))
    sides = []
    count = width
    frames = enc.shape[0]
    grad_enc, grad_pred = [], jnp.zeros(pred.shape, F32)
    for k, (even, odd) in enumerate(orders):
        high, low = split_two(bias)
        if k < len(orders) - 1:
            side = (own & jnp.where(core == 0, even, odd)) != 0
            sides.append(side)
            count //= 2
            top, bottom = acc[:count], acc[count:]
            send = jnp.where(side, top, bottom).astype(BF16)
            acc = jnp.where(side, bottom, top)
        else:
            send = acc.astype(BF16)
            acc = lax.reduce_precision(acc, 8, 7)
        send = jnp.concatenate([send, bias_rows(high, low)], axis=0)
        if k < 2:
            send, d_low = lax.optimization_barrier((send, d_low))
        got = exchange(send, even, odd)
        if k < 2:
            piece = enc[k * (frames // 2) : (k + 1) * (frames // 2)]
            grad_rows, grad_pred = input_gradients(
                piece, pred, d_low, out_weight, grad_pred, rows, k * (blocks // 2)
            )
            got, grad_rows, grad_pred = lax.optimization_barrier((got, grad_rows, grad_pred))
            grad_enc.append(grad_rows)
        acc = acc + got[:count].astype(F32)
        bias = (high + low) + got_bias(got[count:])
    have = acc.astype(BF16)
    for (even, odd), side in list(zip(orders, sides))[::-1]:
        got = exchange(have, even, odd)
        have = jnp.where(
            side, jnp.concatenate([got, have], axis=0), jnp.concatenate([have, got], axis=0)
        )
    high, low = split_two(bias)
    got = exchange(jnp.concatenate([have, bias_rows(high, low)], axis=0), 1, 1)
    other = got[:width]
    grad_weight = jnp.where(
        core == 0, jnp.concatenate([have, other], axis=1), jnp.concatenate([other, have], axis=1)
    ).astype(F32)
    bias, other_bias = high + low, got_bias(got[width:])
    grad_bias = jnp.where(
        core == 0,
        jnp.concatenate([bias, other_bias], axis=1),
        jnp.concatenate([other_bias, bias], axis=1),
    ).reshape(vocab)
    return (
        loss[0, 0:1], grad_weight, grad_bias, jnp.concatenate(grad_enc, axis=0)[None],
        grad_pred.astype(BF16)[None],
    )


def solution(mesh):
    in_specs = (
        P(("groups", "dp"), None, None),
        P("groups"),
        P(("groups", "dp"), None, None),
        P(("groups", "dp"), None, None),
        P(("groups", "dp")),
        P(("groups", "dp")),
        P(("groups", "dp"), None),
        P(),
        P(),
    )
    out_specs = (
        P(("groups", "dp")),
        P("groups", None),
        P("groups"),
        P(("groups", "dp"), None, None),
        P(("groups", "dp"), None, None),
    )
    return jax.shard_map(
        functools.partial(on_device, mesh.shape["dp"]),
        mesh=mesh, in_specs=in_specs, out_specs=out_specs, check_vma=False,
    )
```

```python
import functools

import jax
import jax.numpy as jnp
from jax import lax
from jax.experimental import pallas as pl
from jax.experimental.pallas import tpu as pltpu
from jax.sharding import PartitionSpec as P

F32 = jnp.float32
BF16 = jnp.bfloat16
LANES = 128
EXTRA = 16
VMEM_LIMIT = 24 * 1024 * 1024


def params():
    return pltpu.CompilerParams(
        dimension_semantics=("arbitrary",), vmem_limit_bytes=VMEM_LIMIT
    )


def target_column(labels_ref, token_len, tok_slots, reps):
    tok = labels_ref.shape[1]
    row = lax.broadcasted_iota(jnp.int32, (tok_slots, tok), 0)
    lane = lax.broadcasted_iota(jnp.int32, (tok_slots, tok), 1)
    picked = jnp.where(row == lane, labels_ref[...].astype(F32), 0.0)
    column = jnp.sum(picked, axis=1, keepdims=True)
    token = lax.broadcasted_iota(jnp.int32, (tok_slots, 1), 0)
    column = jnp.where(token < token_len, column, -1.0).astype(jnp.int32)
    whole = jnp.broadcast_to(column[None], (reps, tok_slots, 1))
    return whole.reshape(reps * tok_slots, 1)


SUB = 256


def forward_kernel(begin, tlen_ref, labels_ref, enc_ref, pred_ref, w_ref, b_ref, *refs):
    e_ref, st_ref, jt_ref, enc_scr, logit_scr = refs[-5:]
    step = pl.program_id(0)
    rows, vocab = e_ref.shape
    tok_slots, width = pred_ref.shape
    block_frames = rows // tok_slots

    @pl.when(step == 0)
    def _():
        enc_scr[...] = enc_ref[...].astype(F32)

    first = pl.multiple_of((begin + step) * block_frames, block_frames)
    enc = enc_scr[pl.ds(first, block_frames), :]
    pred = pred_ref[...].astype(F32)
    sub_frames = SUB // tok_slots
    target = target_column(labels_ref, tlen_ref[0], tok_slots, sub_frames)
    lane = lax.broadcasted_iota(jnp.int32, (SUB, LANES), 1)
    parts = rows // SUB

    def multiply(k):
        place = slice(k * SUB, (k + 1) * SUB)
        act = jnp.tanh(enc[k * sub_frames : (k + 1) * sub_frames, None, :] + pred[None, :, :])
        joint_in = act.reshape(SUB, width).astype(BF16)
        jt_ref[:, place] = joint_in.T
        logit_scr[k % 2] = jnp.dot(joint_in, w_ref[...], preferred_element_type=F32)

    def collapse(k):
        place = slice(k * SUB, (k + 1) * SUB)
        tops = jnp.full((SUB, LANES), -jnp.inf, F32)
        for j in range(vocab // LANES):
            cols = slice(j * LANES, (j + 1) * LANES)
            tops = jnp.maximum(tops, logit_scr[k % 2, :, cols] + b_ref[:, cols])
        row_max = jnp.max(tops, axis=1, keepdims=True)
        rest_acc = jnp.zeros((SUB, LANES), F32)
        label_acc = jnp.zeros((SUB, LANES), F32)
        for j in range(vocab // LANES):
            cols = slice(j * LANES, (j + 1) * LANES)
            shifted = logit_scr[k % 2, :, cols] + b_ref[:, cols] - row_max
            e = jnp.exp(shifted)
            e_ref[place, cols] = e
            hot = lane == target - j * LANES
            rest = jnp.where(hot, 0.0, e)
            if j == 0:
                z_blank = shifted[:, 0:1]
                rest = jnp.where(lane == 0, 0.0, rest)
            rest_acc = rest_acc + rest
            label_acc = label_acc + jnp.where(hot, shifted, 0.0)
        rest_sum = jnp.sum(rest_acc, axis=1, keepdims=True)
        z_label = jnp.sum(label_acc, axis=1, keepdims=True)
        packed = jnp.where(lane == 0, rest_sum, jnp.where(lane == 1, z_blank, z_label))
        st_ref[:, place] = packed.T[:8]

    multiply(0)
    for k in range(parts):
        if k + 1 < parts:
            multiply(k + 1)
        collapse(k)


def grad_kernel(
    pick_ref, flen_ref, tlen_ref, labels_ref, qa_ref, qb_ref, e_ref, st_ref, jt_ref,
    d_ref, loss_ref, send_ref, keep_ref, keepb_ref, d_scr, gb_scr, loss_scr, target_scr,
):
    step = pl.program_id(0)
    steps = pl.num_programs(0)
    rows, vocab = e_ref.shape
    tok_slots = labels_ref.shape[1] + 1
    block_frames = rows // tok_slots
    width = jt_ref.shape[0]
    frame_len, token_len = flen_ref[0], tlen_ref[0]

    @pl.when(step == 0)
    def _():
        gb_scr[...] = jnp.zeros_like(gb_scr)
        loss_scr[...] = jnp.zeros_like(loss_scr)
        column = target_column(labels_ref, token_len, tok_slots, block_frames)
        target_scr[...] = jnp.broadcast_to(column, (rows, LANES))

    half_count = pick_ref[1]
    q = jnp.where(pick_ref[0] < half_count, qa_ref[0].astype(F32), qb_ref[0].astype(F32))
    cell = lax.broadcasted_iota(jnp.int32, (1, rows), 1)
    frame = lax.div(cell, tok_slots) + step * block_frames
    token = lax.rem(cell, tok_slots)
    has_label = token < token_len
    count = jnp.full((1, rows), frame_len * (token_len + 1), jnp.int32).astype(F32)
    weight = jnp.where((frame < frame_len) & (token <= token_len), 1.0 / count, 0.0)
    q_blank = q[0:1]
    q_label = jnp.where(has_label, q[1:2], 0.0)
    q_rest = q[2:3]
    rest_sum = st_ref[0:1]
    z_blank = st_ref[1:2]
    z_label = st_ref[2:3]
    e_blank = jnp.exp(z_blank)
    e_label = jnp.exp(z_label)
    total = rest_sum + e_blank + jnp.where(has_label, e_label, 0.0)
    log_total = jnp.log(total)
    cell_loss = -(
        q_blank * (z_blank - log_total)
        + q_label * (z_label - log_total)
        + q_rest * (jnp.log(rest_sum) - log_total)
    )
    loss_scr[...] += cell_loss * weight
    soft = weight * (q_blank + q_label + q_rest) / total
    scale = soft - weight * q_rest / rest_sum
    d_blank = soft * e_blank - weight * q_blank
    d_label = soft * e_label - weight * q_label
    place = lax.broadcasted_iota(jnp.int32, (8, rows), 0)
    packed = jnp.where(place == 0, scale, jnp.where(place == 1, d_label, d_blank))
    columns = packed.T
    scale = jnp.broadcast_to(columns[:, 0:1], (rows, LANES))
    d_label = jnp.broadcast_to(columns[:, 1:2], (rows, LANES))
    lane = lax.broadcasted_iota(jnp.int32, (rows, LANES), 1)
    base = pl.multiple_of(step * rows, rows)
    for j in range(vocab // LANES):
        cols = slice(j * LANES, (j + 1) * LANES)
        d = jnp.where(lane + j * LANES == target_scr[...], d_label, e_ref[:, cols] * scale)
        if j == 0:
            d = jnp.where(lane == 0, columns[:, 2:3], d)
        low = d.astype(BF16)
        d_ref[:, cols] = low
        d_scr[pl.ds(base, rows), cols] = low
        gb_scr[:, cols] += jnp.sum(d.reshape(rows // 8, 8, LANES), axis=0)

    @pl.when(step == steps - 1)
    def _():
        loss_ref[...] = jnp.broadcast_to(jnp.sum(loss_scr[...], axis=1, keepdims=True), loss_ref.shape)
        part = vocab // 2
        core = pick_ref[2]
        col = pl.multiple_of((1 - core) * part, part)
        dw = jnp.dot(jt_ref[...], d_scr[:, pl.ds(col, part)], preferred_element_type=F32)
        send_ref[:width, :] = dw.astype(BF16)
        col = pl.multiple_of(core * part, part)
        keep_ref[...] = jnp.dot(jt_ref[...], d_scr[:, pl.ds(col, part)], preferred_element_type=F32)
        bias = jnp.sum(gb_scr[...], axis=0, keepdims=True)
        first, second = bias[:, :part], bias[:, part:]
        mine = jnp.where(core == 0, first, second)
        other = jnp.where(core == 0, second, first)
        keepb_ref[...] = mine
        high = other.astype(BF16)
        low = (other - high.astype(F32)).astype(BF16)
        place = lax.broadcasted_iota(jnp.int32, (EXTRA, part), 0)
        packed = jnp.where(place == 0, high.astype(F32), jnp.where(place == 1, low.astype(F32), 0.0))
        send_ref[width:, :] = packed.astype(BF16)


def input_kernel(enc_ref, pred_ref, d_ref, w_ref, base_ref, ge_ref, gp_ref, enc_scr, ge_scr):
    step = pl.program_id(0)
    steps = pl.num_programs(0)
    rows = d_ref.shape[0]
    tok_slots, width = pred_ref.shape
    block_frames = rows // tok_slots

    @pl.when(step == 0)
    def _():
        enc_scr[...] = enc_ref[...].astype(F32)
        gp_ref[...] = base_ref[...]

    first = pl.multiple_of(step * block_frames, block_frames)
    d_hidden = lax.dot_general(
        d_ref[...], w_ref[...], (((1,), (1,)), ((), ())), preferred_element_type=F32
    )
    enc = enc_scr[pl.ds(first, block_frames), :]
    act = jnp.tanh(enc[:, None, :] + pred_ref[...].astype(F32)[None, :, :])
    d_pre = d_hidden.reshape(block_frames, tok_slots, width) * (1.0 - act * act)
    ge_scr[pl.ds(first, block_frames), :] = jnp.sum(d_pre, axis=1)
    gp_ref[...] += jnp.sum(d_pre, axis=0)

    @pl.when(step == steps - 1)
    def _():
        ge_ref[...] = ge_scr[...].astype(BF16)


def whole(shape):
    return pl.BlockSpec(shape, lambda *_: (0,) * len(shape))


SMEM_SPEC = pl.BlockSpec(memory_space=pltpu.SMEM)


def forward(tlen, labels, enc, pred, w, bias, rows, begin, blocks, before):
    frames, width = enc.shape
    tok_slots = pred.shape[0]
    vocab = w.shape[1]
    cells = frames * tok_slots
    return pl.pallas_call(
        functools.partial(forward_kernel, begin),
        grid=(blocks,),
        in_specs=[
            SMEM_SPEC, whole(labels.shape), whole(enc.shape), whole(pred.shape),
            whole(w.shape), whole(bias.shape),
        ] + [pl.BlockSpec(memory_space=pl.ANY)] * len(before),
        out_specs=[
            pl.BlockSpec((rows, vocab), lambda i: (i + begin, 0)),
            pl.BlockSpec((8, rows), lambda i: (0, i + begin)),
            pl.BlockSpec((width, rows), lambda i: (0, i + begin)),
        ],
        out_shape=[
            jax.ShapeDtypeStruct((cells, vocab), F32),
            jax.ShapeDtypeStruct((8, cells), F32),
            jax.ShapeDtypeStruct((width, cells), BF16),
        ],
        scratch_shapes=[pltpu.VMEM((frames, width), F32), pltpu.VMEM((2, SUB, vocab), F32)],
        input_output_aliases={6 + k: k for k in range(len(before))},
        compiler_params=params(),
        cost_estimate=pl.CostEstimate(
            flops=2 * blocks * rows * width * vocab, bytes_accessed=blocks * rows * vocab * 8,
            transcendentals=blocks * rows * (width + vocab),
        ),
    )(tlen, labels, enc, pred, w, bias, *before)


def gradients(pick, flen, tlen, labels, qa, qb, e, st, jt, rows):
    cells, vocab = e.shape
    width = jt.shape[0]
    part = vocab // 2
    smem = pl.BlockSpec(memory_space=pltpu.SMEM)
    grid_spec = pltpu.PrefetchScalarGridSpec(
        num_scalar_prefetch=1,
        grid=(cells // rows,),
        in_specs=[
            smem, smem, whole(labels.shape),
            pl.BlockSpec((1, 3, rows), lambda i, pick: (lax.rem(pick[0], pick[1]), 0, i)),
            pl.BlockSpec((1, 3, rows), lambda i, pick: (lax.rem(pick[0], pick[1]), 0, i)),
            pl.BlockSpec((rows, vocab), lambda i, pick: (i, 0)),
            pl.BlockSpec((8, rows), lambda i, pick: (0, i)),
            whole(jt.shape),
        ],
        out_specs=[
            pl.BlockSpec((rows, vocab), lambda i, pick: (i, 0)),
            whole((8, LANES)),
            whole((width + EXTRA, part)),
            whole((width, part)),
            whole((1, part)),
        ],
        scratch_shapes=[
            pltpu.VMEM((cells, vocab), BF16),
            pltpu.VMEM((8, vocab), F32),
            pltpu.VMEM((1, rows), F32),
            pltpu.VMEM((rows, LANES), jnp.int32),
        ],
    )
    return pl.pallas_call(
        grad_kernel,
        grid_spec=grid_spec,
        out_shape=[
            jax.ShapeDtypeStruct((cells, vocab), BF16),
            jax.ShapeDtypeStruct((8, LANES), F32),
            jax.ShapeDtypeStruct((width + EXTRA, part), BF16),
            jax.ShapeDtypeStruct((width, part), F32),
            jax.ShapeDtypeStruct((1, part), F32),
        ],
        compiler_params=params(),
        cost_estimate=pl.CostEstimate(
            flops=2 * cells * width * vocab, bytes_accessed=16 * 1024 * 1024, transcendentals=cells * 8
        ),
    )(pick, flen, tlen, labels, qa, qb, e, st, jt)


def input_gradients(enc, pred, d_low, w, base, rows, begin):
    vocab = d_low.shape[1]
    cells = enc.shape[0] * pred.shape[0]
    return pl.pallas_call(
        input_kernel,
        grid=(cells // rows,),
        in_specs=[
            whole(enc.shape), whole(pred.shape),
            pl.BlockSpec((rows, vocab), lambda i: (i + begin, 0)), whole(w.shape), whole(base.shape),
        ],
        out_specs=[whole(enc.shape), whole(pred.shape)],
        out_shape=[
            jax.ShapeDtypeStruct(enc.shape, BF16),
            jax.ShapeDtypeStruct(pred.shape, F32),
        ],
        scratch_shapes=[pltpu.VMEM(enc.shape, F32), pltpu.VMEM(enc.shape, F32)],
        compiler_params=params(),
        cost_estimate=pl.CostEstimate(
            flops=2 * cells * w.shape[0] * vocab, bytes_accessed=cells * vocab * 4,
            transcendentals=cells * w.shape[0],
        ),
    )(enc, pred, d_low, w, base)


def split_two(value):
    high = lax.reduce_precision(value, 8, 7)
    return high, lax.reduce_precision(value - high, 8, 7)


def on_device(
    dp, teacher_post, assignment, encoder_out, predictor_out, frame_lengths, token_lengths,
    labels, out_weight, out_bias,
):
    own = lax.axis_index("dp")
    core = own & 1
    masks = [1 << k for k in range(dp.bit_length() - 1)]
    enc, pred = encoder_out[0], predictor_out[0]
    rows = 16 * pred.shape[0]
    width, vocab = out_weight.shape
    part = vocab // 2

    def exchange(value, even, odd):
        pairs = [(k, k ^ (odd if k & 1 else even)) for k in range(dp)]
        return lax.ppermute(value, "dp", pairs)

    blocks = enc.shape[0] * pred.shape[0] // rows
    quarter = blocks // 4
    shares = [(0, quarter), (quarter, quarter), (2 * quarter, blocks - 2 * quarter)]
    bias_row = out_bias.reshape(1, vocab)
    held, made = teacher_post, ()
    for k, mask in enumerate(masks):
        got = exchange(held, mask, mask)
        part_no = k - (len(masks) - len(shares))
        if part_no >= 0:
            begin, number = shares[part_no]
            made = tuple(forward(
                token_lengths, labels, enc, pred, out_weight, bias_row, rows, begin, number, made
            ))
        if k < len(masks) - 1:
            held = jnp.concatenate([held, got], axis=0)
            held, made = lax.optimization_barrier((held, made))
    far = got
    e, st, jt = made
    place = lax.dynamic_index_in_dim(assignment, own, keepdims=False) ^ own
    pick = jnp.stack([place, jnp.int32(dp // 2), core]).astype(jnp.int32)
    d_low, loss, send, keep, bias = gradients(
        pick, frame_lengths, token_lengths, labels, held, far, e, st, jt, rows
    )
    got = exchange(send, 1, 1)

    def got_bias(rows_of):
        return rows_of[0:1].astype(F32) + rows_of[1:2].astype(F32)

    def bias_rows(high, low):
        filler = jnp.zeros((EXTRA - 2, part), BF16)
        return jnp.concatenate([high.astype(BF16), low.astype(BF16), filler], axis=0)

    acc = keep + got[:width].astype(F32)
    bias = bias + got_bias(got[width:])
    rest = masks[1:]
    even_order = rest
    odd_order = rest[1:2] + rest[:1] + rest[2:]
    orders = list(zip(even_order, odd_order))
    sides = []
    count = width
    frames = enc.shape[0]
    grad_enc, grad_pred = [], jnp.zeros(pred.shape, F32)
    for k, (even, odd) in enumerate(orders):
        high, low = split_two(bias)
        if k < len(orders) - 1:
            side = (own & jnp.where(core == 0, even, odd)) != 0
            sides.append(side)
            count //= 2
            top, bottom = acc[:count], acc[count:]
            send = jnp.where(side, top, bottom).astype(BF16)
            acc = jnp.where(side, bottom, top)
        else:
            send = acc.astype(BF16)
            acc = lax.reduce_precision(acc, 8, 7)
        send = jnp.concatenate([send, bias_rows(high, low)], axis=0)
        if k < 2:
            send, d_low = lax.optimization_barrier((send, d_low))
        got = exchange(send, even, odd)
        if k < 2:
            piece = enc[k * (frames // 2) : (k + 1) * (frames // 2)]
            grad_rows, grad_pred = input_gradients(
                piece, pred, d_low, out_weight, grad_pred, rows, k * (blocks // 2)
            )
            got, grad_rows, grad_pred = lax.optimization_barrier((got, grad_rows, grad_pred))
            grad_enc.append(grad_rows)
        acc = acc + got[:count].astype(F32)
        bias = (high + low) + got_bias(got[count:])
    have = acc.astype(BF16)
    for (even, odd), side in list(zip(orders, sides))[::-1]:
        got = exchange(have, even, odd)
        have = jnp.where(
            side, jnp.concatenate([got, have], axis=0), jnp.concatenate([have, got], axis=0)
        )
    high, low = split_two(bias)
    got = exchange(jnp.concatenate([have, bias_rows(high, low)], axis=0), 1, 1)
    other = got[:width]
    grad_weight = jnp.where(
        core == 0, jnp.concatenate([have, other], axis=1), jnp.concatenate([other, have], axis=1)
    ).astype(F32)
    bias, other_bias = high + low, got_bias(got[width:])
    grad_bias = jnp.where(
        core == 0,
        jnp.concatenate([bias, other_bias], axis=1),
        jnp.concatenate([other_bias, bias], axis=1),
    ).reshape(vocab)
    return (
        loss[0, 0:1], grad_weight, grad_bias, jnp.concatenate(grad_enc, axis=0)[None],
        grad_pred.astype(BF16)[None],
    )


def solution(mesh):
    in_specs = (
        P(("groups", "dp"), None, None),
        P("groups"),
        P(("groups", "dp"), None, None),
        P(("groups", "dp"), None, None),
        P(("groups", "dp")),
        P(("groups", "dp")),
        P(("groups", "dp"), None),
        P(),
        P(),
    )
    out_specs = (
        P(("groups", "dp")),
        P("groups", None),
        P("groups"),
        P(("groups", "dp"), None, None),
        P(("groups", "dp"), None, None),
    )
    return jax.shard_map(
        functools.partial(on_device, mesh.shape["dp"]),
        mesh=mesh, in_specs=in_specs, out_specs=out_specs, check_vma=False,
    )
```

```python
import functools

import jax
import jax.numpy as jnp
from jax import lax
from jax.experimental import pallas as pl
from jax.experimental.pallas import tpu as pltpu
from jax.sharding import PartitionSpec as P

F32 = jnp.float32
BF16 = jnp.bfloat16
LANES = 128
EXTRA = 16


def params(mib):
    return pltpu.CompilerParams(
        dimension_semantics=("arbitrary",), vmem_limit_bytes=mib * 1024 * 1024
    )


def target_column(labels_ref, token_len, tok_slots, reps):
    tok = labels_ref.shape[1]
    row = lax.broadcasted_iota(jnp.int32, (tok_slots, tok), 0)
    lane = lax.broadcasted_iota(jnp.int32, (tok_slots, tok), 1)
    picked = jnp.where(row == lane, labels_ref[...].astype(F32), 0.0)
    column = jnp.sum(picked, axis=1, keepdims=True)
    token = lax.broadcasted_iota(jnp.int32, (tok_slots, 1), 0)
    column = jnp.where(token < token_len, column, -1.0).astype(jnp.int32)
    whole = jnp.broadcast_to(column[None], (reps, tok_slots, 1))
    return whole.reshape(reps * tok_slots, 1)


def stage_kernel(assignment_ref, *refs):
    count = (len(refs) - 2) // 2
    sources, targets, pick_ref, sems = refs[:count], refs[count : 2 * count], refs[-2], refs[-1]
    copies = [
        pltpu.make_async_copy(source, target, sems.at[k])
        for k, (source, target) in enumerate(zip(sources, targets))
    ]
    for copy in copies:
        copy.start()
    own = lax.axis_index("dp")
    pick_ref[0] = assignment_ref[own] ^ own
    pick_ref[1] = assignment_ref.shape[0] // 2
    pick_ref[2] = own & 1
    for copy in copies:
        copy.wait()


def stage(assignment, *arrays):
    anywhere = pl.BlockSpec(memory_space=pl.ANY)
    smem = pl.BlockSpec(memory_space=pltpu.SMEM)
    return pl.pallas_call(
        stage_kernel,
        in_specs=[smem] + [anywhere] * len(arrays),
        out_specs=[anywhere] * len(arrays) + [smem],
        out_shape=[jax.ShapeDtypeStruct(x.shape, x.dtype) for x in arrays]
        + [jax.ShapeDtypeStruct((3,), jnp.int32)],
        scratch_shapes=[pltpu.SemaphoreType.DMA((len(arrays),))],
        compiler_params=pltpu.CompilerParams(vmem_limit_bytes=4 * 1024 * 1024),
    )(assignment, *[pltpu.with_memory_space_constraint(x, pltpu.HBM) for x in arrays])


def in_vmem(x):
    return x


SUB = 256


def forward_kernel(begin, tlen_ref, labels_ref, enc_ref, pred_ref, w_ref, b_ref, *refs):
    e_ref, st_ref, jt_ref, enc_scr, logit_scr = refs[-5:]
    step = pl.program_id(0)
    rows, vocab = e_ref.shape
    tok_slots, width = pred_ref.shape
    block_frames = rows // tok_slots

    @pl.when(step == 0)
    def _():
        enc_scr[...] = enc_ref[...].astype(F32)

    first = pl.multiple_of((begin + step) * block_frames, block_frames)
    enc = enc_scr[pl.ds(first, block_frames), :]
    pred = pred_ref[...].astype(F32)
    sub_frames = SUB // tok_slots
    target = target_column(labels_ref, tlen_ref[0], tok_slots, sub_frames)
    lane = lax.broadcasted_iota(jnp.int32, (SUB, LANES), 1)
    parts = rows // SUB

    def multiply(k):
        place = slice(k * SUB, (k + 1) * SUB)
        act = jnp.tanh(enc[k * sub_frames : (k + 1) * sub_frames, None, :] + pred[None, :, :])
        joint_in = act.reshape(SUB, width).astype(BF16)
        jt_ref[:, place] = joint_in.T
        logit_scr[k % 2] = jnp.dot(joint_in, w_ref[...], preferred_element_type=F32)

    def collapse(k):
        place = slice(k * SUB, (k + 1) * SUB)
        tops = jnp.full((SUB, LANES), -jnp.inf, F32)
        for j in range(vocab // LANES):
            cols = slice(j * LANES, (j + 1) * LANES)
            tops = jnp.maximum(tops, logit_scr[k % 2, :, cols] + b_ref[:, cols])
        row_max = jnp.max(tops, axis=1, keepdims=True)
        rest_acc = jnp.zeros((SUB, LANES), F32)
        label_acc = jnp.zeros((SUB, LANES), F32)
        for j in range(vocab // LANES):
            cols = slice(j * LANES, (j + 1) * LANES)
            shifted = logit_scr[k % 2, :, cols] + b_ref[:, cols] - row_max
            e = jnp.exp(shifted)
            e_ref[place, cols] = e
            hot = lane == target - j * LANES
            rest = jnp.where(hot, 0.0, e)
            if j == 0:
                z_blank = shifted[:, 0:1]
                rest = jnp.where(lane == 0, 0.0, rest)
            rest_acc = rest_acc + rest
            label_acc = label_acc + jnp.where(hot, shifted, 0.0)
        rest_sum = jnp.sum(rest_acc, axis=1, keepdims=True)
        z_label = jnp.sum(label_acc, axis=1, keepdims=True)
        packed = jnp.where(lane == 0, rest_sum, jnp.where(lane == 1, z_blank, z_label))
        st_ref[:, place] = packed.T[:8]

    multiply(0)
    for k in range(parts):
        if k + 1 < parts:
            multiply(k + 1)
        collapse(k)


def grad_kernel(
    pick_ref, flen_ref, tlen_ref, labels_ref, qa_ref, qb_ref, e_ref, st_ref, jt_ref,
    d_ref, loss_ref, send_ref, keep_ref, d_scr, gb_scr, loss_scr, target_scr,
):
    step = pl.program_id(0)
    steps = pl.num_programs(0)
    rows, vocab = e_ref.shape
    tok_slots = labels_ref.shape[1] + 1
    block_frames = rows // tok_slots
    width = jt_ref.shape[0]
    frame_len, token_len = flen_ref[0], tlen_ref[0]

    @pl.when(step == 0)
    def _():
        gb_scr[...] = jnp.zeros_like(gb_scr)
        loss_scr[...] = jnp.zeros_like(loss_scr)
        column = target_column(labels_ref, token_len, tok_slots, block_frames)
        target_scr[...] = jnp.broadcast_to(column, (rows, LANES))

    half_count = pick_ref[1]
    q = jnp.where(pick_ref[0] < half_count, qa_ref[0].astype(F32), qb_ref[0].astype(F32))
    cell = lax.broadcasted_iota(jnp.int32, (1, rows), 1)
    frame = lax.div(cell, tok_slots) + step * block_frames
    token = lax.rem(cell, tok_slots)
    has_label = token < token_len
    count = jnp.full((1, rows), frame_len * (token_len + 1), jnp.int32).astype(F32)
    weight = jnp.where((frame < frame_len) & (token <= token_len), 1.0 / count, 0.0)
    q_blank = q[0:1]
    q_label = jnp.where(has_label, q[1:2], 0.0)
    q_rest = q[2:3]
    rest_sum = st_ref[0:1]
    z_blank = st_ref[1:2]
    z_label = st_ref[2:3]
    e_blank = jnp.exp(z_blank)
    e_label = jnp.exp(z_label)
    total = rest_sum + e_blank + jnp.where(has_label, e_label, 0.0)
    log_total = jnp.log(total)
    cell_loss = -(
        q_blank * (z_blank - log_total)
        + q_label * (z_label - log_total)
        + q_rest * (jnp.log(rest_sum) - log_total)
    )
    loss_scr[...] += cell_loss * weight
    soft = weight * (q_blank + q_label + q_rest) / total
    scale = soft - weight * q_rest / rest_sum
    d_blank = soft * e_blank - weight * q_blank
    d_label = soft * e_label - weight * q_label
    place = lax.broadcasted_iota(jnp.int32, (8, rows), 0)
    packed = jnp.where(place == 0, scale, jnp.where(place == 1, d_label, d_blank))
    columns = packed.T
    scale = jnp.broadcast_to(columns[:, 0:1], (rows, LANES))
    d_label = jnp.broadcast_to(columns[:, 1:2], (rows, LANES))
    lane = lax.broadcasted_iota(jnp.int32, (rows, LANES), 1)
    base = pl.multiple_of(step * rows, rows)
    for j in range(vocab // LANES):
        cols = slice(j * LANES, (j + 1) * LANES)
        d = jnp.where(lane + j * LANES == target_scr[...], d_label, e_ref[:, cols] * scale)
        if j == 0:
            d = jnp.where(lane == 0, columns[:, 2:3], d)
        low = d.astype(BF16)
        d_ref[:, cols] = low
        d_scr[pl.ds(base, rows), cols] = low
        gb_scr[:, cols] += jnp.sum(d.reshape(rows // 8, 8, LANES), axis=0)

    @pl.when(step == steps - 1)
    def _():
        loss_ref[...] = jnp.sum(loss_scr[...], axis=1, keepdims=True)
        part = vocab // 2
        core = pick_ref[2]
        col = pl.multiple_of((1 - core) * part, part)
        dw = jnp.dot(jt_ref[...], d_scr[:, pl.ds(col, part)], preferred_element_type=F32)
        send_ref[:width, :] = dw.astype(BF16)
        col = pl.multiple_of(core * part, part)
        keep_ref[:width, :] = jnp.dot(jt_ref[...], d_scr[:, pl.ds(col, part)], preferred_element_type=F32)
        bias = jnp.sum(gb_scr[...], axis=0, keepdims=True)
        first, second = bias[:, :part], bias[:, part:]
        mine = jnp.where(core == 0, first, second)
        other = jnp.where(core == 0, second, first)
        keep_ref[width:, :] = jnp.broadcast_to(mine, (EXTRA, part))
        high = other.astype(BF16)
        low = (other - high.astype(F32)).astype(BF16)
        place = lax.broadcasted_iota(jnp.int32, (EXTRA, part), 0)
        packed = jnp.where(place == 0, high.astype(F32), jnp.where(place == 1, low.astype(F32), 0.0))
        send_ref[width:, :] = packed.astype(BF16)


def input_kernel(begin, last, enc_ref, pred_ref, d_ref, w_ref, *refs):
    ge_ref, gp_ref, enc_scr, ge_scr, gp_scr = refs[-5:]
    step = pl.program_id(0)
    steps = pl.num_programs(0)
    rows = d_ref.shape[0]
    tok_slots, width = pred_ref.shape
    block_frames = rows // tok_slots

    @pl.when(step == 0)
    def _():
        enc_scr[...] = enc_ref[...].astype(F32)
        gp_scr[...] = jnp.zeros_like(gp_scr) if begin == 0 else refs[0][...]

    first = pl.multiple_of(step * block_frames, block_frames)
    d_hidden = lax.dot_general(
        d_ref[...], w_ref[...], (((1,), (1,)), ((), ())), preferred_element_type=F32
    )
    enc = enc_scr[pl.ds(begin * block_frames + first, block_frames), :]
    act = jnp.tanh(enc[:, None, :] + pred_ref[...].astype(F32)[None, :, :])
    d_pre = d_hidden.reshape(block_frames, tok_slots, width) * (1.0 - act * act)
    ge_scr[pl.ds(first, block_frames), :] = jnp.sum(d_pre, axis=1)
    gp_scr[...] += jnp.sum(d_pre, axis=0)

    @pl.when(step == steps - 1)
    def _():
        ge_ref[...] = ge_scr[...].astype(BF16)
        gp_ref[...] = gp_scr[...].astype(gp_ref.dtype)


def final_kernel(with_bias, core_ref, have_ref, *refs):
    out_ref = refs[-2] if with_bias else refs[-1]
    out_ref[...] = have_ref[...].astype(F32)
    if with_bias:
        mine_ref, rows_ref, bias_ref = refs[1], refs[2], refs[-1]
        mine = mine_ref[...]
        other = rows_ref[0:1, :].astype(F32) + rows_ref[1:2, :].astype(F32)
        core = core_ref[2]
        bias_ref[...] = jnp.concatenate(
            [jnp.where(core == 0, mine, other), jnp.where(core == 0, other, mine)], axis=1
        )


def widen(pick, have, width, before=(), mine=None):
    part = have.shape[1]
    rows = width // 2
    with_bias = mine is not None
    if with_bias:
        place = lambda i, pick: (i, 1 - pick[2])
    else:
        place = lambda i, pick: (i, pick[2])
    in_specs = [pl.BlockSpec((rows, part), lambda i, pick: (i, 0))]
    out_specs = [pl.BlockSpec((rows, part), place)]
    out_shape = [jax.ShapeDtypeStruct((width, 2 * part), F32)]
    extra = ()
    if with_bias:
        in_specs += [
            pl.BlockSpec(memory_space=pl.ANY), whole(mine.shape),
            pl.BlockSpec((EXTRA, part), lambda i, pick: (width // EXTRA, 0)),
        ]
        out_specs += [whole((1, 2 * part))]
        out_shape += [jax.ShapeDtypeStruct((1, 2 * part), F32)]
        extra = (*before, mine, have)
    return pl.pallas_call(
        functools.partial(final_kernel, with_bias),
        grid_spec=pltpu.PrefetchScalarGridSpec(
            num_scalar_prefetch=1, grid=(width // rows,), in_specs=in_specs, out_specs=out_specs
        ),
        out_shape=out_shape,
        input_output_aliases={2: 0} if with_bias else {},
        compiler_params=params(8),
    )(pick, have, *extra)


def whole(shape):
    return pl.BlockSpec(shape, lambda *_: (0,) * len(shape))


SMEM_SPEC = pl.BlockSpec(memory_space=pltpu.SMEM)


def forward(tlen, labels, enc, pred, w, bias, rows, begin, blocks, before):
    frames, width = enc.shape
    tok_slots = pred.shape[0]
    vocab = w.shape[1]
    cells = frames * tok_slots
    return pl.pallas_call(
        functools.partial(forward_kernel, begin),
        grid=(blocks,),
        in_specs=[
            SMEM_SPEC, whole(labels.shape), whole(enc.shape), whole(pred.shape),
            whole(w.shape), whole(bias.shape),
        ] + [pl.BlockSpec(memory_space=pl.ANY)] * len(before),
        out_specs=[
            pl.BlockSpec((rows, vocab), lambda i: (i + begin, 0)),
            pl.BlockSpec((8, rows), lambda i: (0, i + begin)),
            pl.BlockSpec((width, rows), lambda i: (0, i + begin)),
        ],
        out_shape=[
            jax.ShapeDtypeStruct((cells, vocab), F32),
            jax.ShapeDtypeStruct((8, cells), F32),
            jax.ShapeDtypeStruct((width, cells), BF16),
        ],
        scratch_shapes=[pltpu.VMEM((frames, width), F32), pltpu.VMEM((2, SUB, vocab), F32)],
        input_output_aliases={6 + k: k for k in range(len(before))},
        compiler_params=params(16),
    )(tlen, in_vmem(labels), in_vmem(enc), in_vmem(pred), in_vmem(w), in_vmem(bias), *before)


def gradients(pick, flen, tlen, labels, qa, qb, e, st, jt, rows):
    cells, vocab = e.shape
    width = jt.shape[0]
    part = vocab // 2
    smem = pl.BlockSpec(memory_space=pltpu.SMEM)
    grid_spec = pltpu.PrefetchScalarGridSpec(
        num_scalar_prefetch=1,
        grid=(cells // rows,),
        in_specs=[
            smem, smem, whole(labels.shape),
            pl.BlockSpec((1, 3, rows), lambda i, pick: (lax.rem(pick[0], pick[1]), 0, i)),
            pl.BlockSpec((1, 3, rows), lambda i, pick: (lax.rem(pick[0], pick[1]), 0, i)),
            pl.BlockSpec((rows, vocab), lambda i, pick: (i, 0)),
            pl.BlockSpec((8, rows), lambda i, pick: (0, i)),
            whole(jt.shape),
        ],
        out_specs=[
            pl.BlockSpec((rows, vocab), lambda i, pick: (i, 0)),
            whole((1, 1)),
            whole((width + EXTRA, part)),
            whole((width + EXTRA, part)),
        ],
        scratch_shapes=[
            pltpu.VMEM((cells, vocab), BF16),
            pltpu.VMEM((8, vocab), F32),
            pltpu.VMEM((1, rows), F32),
            pltpu.VMEM((rows, LANES), jnp.int32),
        ],
    )
    return pl.pallas_call(
        grad_kernel,
        grid_spec=grid_spec,
        out_shape=[
            pltpu.HBM((cells, vocab), BF16),
            jax.ShapeDtypeStruct((1, 1), F32),
            jax.ShapeDtypeStruct((width + EXTRA, part), BF16),
            jax.ShapeDtypeStruct((width + EXTRA, part), F32),
        ],
        compiler_params=params(20),
    )(pick, flen, tlen, in_vmem(labels), qa, qb, e, st, jt)


def input_gradients(enc, pred, d_low, w, rows, begin, last, before):
    frames, width = enc.shape
    vocab = d_low.shape[1]
    cells = frames // 2 * pred.shape[0]
    half = (frames // 2, width)
    extra = () if not before else (before[1], before[0])
    return pl.pallas_call(
        functools.partial(input_kernel, begin, last),
        grid=(cells // rows,),
        in_specs=[
            whole(enc.shape), whole(pred.shape),
            pl.BlockSpec((rows, vocab), lambda i: (i + begin, 0)), whole(w.shape),
        ] + ([whole(pred.shape), pl.BlockSpec(memory_space=pl.ANY)] if before else []),
        out_specs=[pl.BlockSpec(half, lambda i: (1 if last else 0, 0)), whole(pred.shape)],
        out_shape=[
            jax.ShapeDtypeStruct(enc.shape, BF16),
            jax.ShapeDtypeStruct(pred.shape, BF16 if last else F32),
        ],
        scratch_shapes=[
            pltpu.VMEM(enc.shape, F32), pltpu.VMEM(half, F32), pltpu.VMEM(pred.shape, F32)
        ],
        input_output_aliases={5: 0} if before else {},
        compiler_params=params(12),
    )(in_vmem(enc), in_vmem(pred), pltpu.with_memory_space_constraint(d_low, pltpu.HBM), in_vmem(w), *extra)


def split_two(value):
    high = lax.reduce_precision(value, 8, 7)
    return high, lax.reduce_precision(value - high, 8, 7)


def on_device(
    dp, teacher_post, assignment, encoder_out, predictor_out, frame_lengths, token_lengths,
    labels, out_weight, out_bias,
):
    own = lax.axis_index("dp")
    core = own & 1
    masks = [1 << k for k in range(dp.bit_length() - 1)]
    tok_slots = predictor_out.shape[1]
    rows = 16 * tok_slots
    width, vocab = out_weight.shape
    part = vocab // 2

    def exchange(value, even, odd):
        pairs = [(k, k ^ (odd if k & 1 else even)) for k in range(dp)]
        return lax.ppermute(value, "dp", pairs)

    blocks = encoder_out.shape[1] * tok_slots // rows
    quarter = blocks // 4
    shares = [(0, quarter), (quarter, quarter), (2 * quarter, blocks - 2 * quarter)]
    held, made = teacher_post, ()
    staged = stage(
        assignment, out_weight, encoder_out[0], predictor_out[0], out_bias.reshape(1, vocab), labels
    )
    for k, mask in enumerate(masks):
        got = exchange(held, mask, mask)
        part_no = k - (len(masks) - len(shares))
        if part_no >= 0:
            begin, number = shares[part_no]
            made = tuple(forward(
                token_lengths, label_row, enc, pred, weight, bias_row, rows, begin, number, made
            ))
        if k < len(masks) - 1:
            held = jnp.concatenate([held, got], axis=0)
            held, made, staged = lax.optimization_barrier((held, made, staged))
            weight, enc, pred, bias_row, label_row, pick = staged
    far = got
    e, st, jt = made
    d_low, loss, send, keep = gradients(
        pick, frame_lengths, token_lengths, label_row, held, far, e, st, jt, rows
    )
    got = exchange(send, 1, 1)

    def got_bias(rows_of):
        return rows_of[0:1].astype(F32) + rows_of[1:2].astype(F32)

    def bias_rows(high, low):
        filler = jnp.zeros((EXTRA - 2, part), BF16)
        return jnp.concatenate([high.astype(BF16), low.astype(BF16), filler], axis=0)

    acc = keep[:width] + got[:width].astype(F32)
    bias = keep[width : width + 1] + got_bias(got[width:])
    rest = masks[1:]
    even_order = rest
    odd_order = rest[1:2] + rest[:1] + rest[2:]
    orders = list(zip(even_order, odd_order))
    sides = []
    count = width
    done = ()
    for k, (even, odd) in enumerate(orders):
        high, low = split_two(bias)
        if k < len(orders) - 1:
            side = (own & jnp.where(core == 0, even, odd)) != 0
            sides.append(side)
            count //= 2
            top, bottom = acc[:count], acc[count:]
            send = jnp.where(side, top, bottom).astype(BF16)
            acc = jnp.where(side, bottom, top)
        else:
            send = acc.astype(BF16)
            acc = lax.reduce_precision(acc, 8, 7)
        send = jnp.concatenate([send, bias_rows(high, low)], axis=0)
        if k < 2:
            send, acc, d_low = lax.optimization_barrier((send, acc, d_low))
        got = exchange(send, even, odd)
        if k < 2:
            done = input_gradients(
                enc, pred, d_low, weight, rows, k * (blocks // 2), k == 1, done
            )
            got, done = lax.optimization_barrier((got, done))
        acc = acc + got[:count].astype(F32)
        bias = (high + low) + got_bias(got[count:])
    have = acc.astype(BF16)
    for (even, odd), side in list(zip(orders, sides))[::-1]:
        got = exchange(have, even, odd)
        have = jnp.where(
            side, jnp.concatenate([got, have], axis=0), jnp.concatenate([have, got], axis=0)
        )
    high, low = split_two(bias)
    got = exchange(jnp.concatenate([have, bias_rows(high, low)], axis=0), 1, 1)
    half = widen(pick, have, width)
    got, half = lax.optimization_barrier((got, half))
    grad_weight, grad_bias = widen(pick, got, width, half, high + low)
    return (loss.reshape(1), grad_weight, grad_bias.reshape(vocab), done[0][None], done[1][None])


def solution(mesh):
    in_specs = (
        P(("groups", "dp"), None, None),
        P("groups"),
        P(("groups", "dp"), None, None),
        P(("groups", "dp"), None, None),
        P(("groups", "dp")),
        P(("groups", "dp")),
        P(("groups", "dp"), None),
        P(),
        P(),
    )
    out_specs = (
        P(("groups", "dp")),
        P("groups", None),
        P("groups"),
        P(("groups", "dp"), None, None),
        P(("groups", "dp"), None, None),
    )
    return jax.shard_map(
        functools.partial(on_device, mesh.shape["dp"]),
        mesh=mesh, in_specs=in_specs, out_specs=out_specs, check_vma=False,
    )
```

```python
import functools

import jax
import jax.numpy as jnp
from jax import lax
from jax.experimental import pallas as pl
from jax.experimental.pallas import tpu as pltpu
from jax.sharding import PartitionSpec as P

F32 = jnp.float32
BF16 = jnp.bfloat16
LANES = 128
EXTRA = 16
CHAINS = 2


def params(mib):
    return pltpu.CompilerParams(
        dimension_semantics=("arbitrary",), vmem_limit_bytes=mib * 1024 * 1024
    )


def target_column(labels_ref, token_len, tok_slots, reps):
    tok = labels_ref.shape[1]
    row = lax.broadcasted_iota(jnp.int32, (tok_slots, tok), 0)
    lane = lax.broadcasted_iota(jnp.int32, (tok_slots, tok), 1)
    picked = jnp.where(row == lane, labels_ref[...].astype(F32), 0.0)
    column = jnp.sum(picked, axis=1, keepdims=True)
    token = lax.broadcasted_iota(jnp.int32, (tok_slots, 1), 0)
    column = jnp.where(token < token_len, column, -1.0).astype(jnp.int32)
    whole = jnp.broadcast_to(column[None], (reps, tok_slots, 1))
    return whole.reshape(reps * tok_slots, 1)


def stage_kernel(assignment_ref, *refs):
    count = (len(refs) - 2) // 2
    sources, targets, pick_ref, sems = refs[:count], refs[count : 2 * count], refs[-2], refs[-1]
    copies = [
        pltpu.make_async_copy(source, target, sems.at[k])
        for k, (source, target) in enumerate(zip(sources, targets))
    ]
    for copy in copies:
        copy.start()
    own = lax.axis_index("dp")
    pick_ref[0] = assignment_ref[own] ^ own
    pick_ref[1] = assignment_ref.shape[0] // 2
    pick_ref[2] = own & 1
    for copy in copies:
        copy.wait()


def stage(assignment, *arrays):
    anywhere = pl.BlockSpec(memory_space=pl.ANY)
    smem = pl.BlockSpec(memory_space=pltpu.SMEM)
    return pl.pallas_call(
        stage_kernel,
        in_specs=[smem] + [anywhere] * len(arrays),
        out_specs=[anywhere] * len(arrays) + [smem],
        out_shape=[jax.ShapeDtypeStruct(x.shape, x.dtype) for x in arrays]
        + [jax.ShapeDtypeStruct((3,), jnp.int32)],
        scratch_shapes=[pltpu.SemaphoreType.DMA((len(arrays),))],
        compiler_params=pltpu.CompilerParams(vmem_limit_bytes=4 * 1024 * 1024),
    )(*[pltpu.with_memory_space_constraint(x, pltpu.HBM) for x in (assignment, *arrays)])


def in_vmem(x):
    return x


SUB = 256


def forward_kernel(begin, tlen_ref, labels_ref, enc_ref, pred_ref, w_ref, b_ref, *refs):
    e_ref, st_ref, jt_ref, enc_scr, logit_scr = refs[-5:]
    step = pl.program_id(0)
    rows, vocab = e_ref.shape
    tok_slots, width = pred_ref.shape
    block_frames = rows // tok_slots

    @pl.when(step == 0)
    def _():
        enc_scr[...] = enc_ref[...].astype(F32)

    first = pl.multiple_of((begin + step) * block_frames, block_frames)
    enc = enc_scr[pl.ds(first, block_frames), :]
    pred = pred_ref[...].astype(F32)
    sub_frames = SUB // tok_slots
    target = target_column(labels_ref, tlen_ref[0], tok_slots, sub_frames)
    lane = lax.broadcasted_iota(jnp.int32, (SUB, LANES), 1)
    parts = rows // SUB

    def multiply(k):
        place = slice(k * SUB, (k + 1) * SUB)
        act = jnp.tanh(enc[k * sub_frames : (k + 1) * sub_frames, None, :] + pred[None, :, :])
        joint_in = act.reshape(SUB, width).astype(BF16)
        jt_ref[:, place] = joint_in.T
        logit_scr[k % 2] = jnp.dot(joint_in, w_ref[...], preferred_element_type=F32)

    def collapse(k):
        place = slice(k * SUB, (k + 1) * SUB)
        tops = jnp.full((SUB, LANES), -jnp.inf, F32)
        for j in range(vocab // LANES):
            cols = slice(j * LANES, (j + 1) * LANES)
            tops = jnp.maximum(tops, logit_scr[k % 2, :, cols] + b_ref[:, cols])
        row_max = jnp.max(tops, axis=1, keepdims=True)
        rest_acc = jnp.zeros((SUB, LANES), F32)
        label_acc = jnp.zeros((SUB, LANES), F32)
        for j in range(vocab // LANES):
            cols = slice(j * LANES, (j + 1) * LANES)
            shifted = logit_scr[k % 2, :, cols] + b_ref[:, cols] - row_max
            e = jnp.exp(shifted)
            e_ref[place, cols] = e
            hot = lane == target - j * LANES
            rest = jnp.where(hot, 0.0, e)
            if j == 0:
                z_blank = shifted[:, 0:1]
                rest = jnp.where(lane == 0, 0.0, rest)
            rest_acc = rest_acc + rest
            label_acc = label_acc + jnp.where(hot, shifted, 0.0)
        rest_sum = jnp.sum(rest_acc, axis=1, keepdims=True)
        z_label = jnp.sum(label_acc, axis=1, keepdims=True)
        packed = jnp.where(lane == 0, rest_sum, jnp.where(lane == 1, z_blank, z_label))
        st_ref[:, place] = packed.T[:8]

    multiply(0)
    for k in range(parts):
        if k + 1 < parts:
            multiply(k + 1)
        collapse(k)


def grad_kernel(
    pick_ref, flen_ref, tlen_ref, labels_ref, qa_ref, qb_ref, e_ref, st_ref, jt_ref,
    d_ref, loss_ref, send_ref, keep_ref, d_scr, gb_scr, loss_scr, target_scr,
):
    step = pl.program_id(0)
    steps = pl.num_programs(0)
    rows, vocab = e_ref.shape
    tok_slots = labels_ref.shape[1] + 1
    block_frames = rows // tok_slots
    width = jt_ref.shape[0]
    frame_len, token_len = flen_ref[0], tlen_ref[0]

    @pl.when(step == 0)
    def _():
        gb_scr[...] = jnp.zeros_like(gb_scr)
        loss_scr[...] = jnp.zeros_like(loss_scr)
        column = target_column(labels_ref, token_len, tok_slots, block_frames)
        target_scr[...] = jnp.broadcast_to(column, (rows, LANES))

    half_count = pick_ref[1]
    q = jnp.where(pick_ref[0] < half_count, qa_ref[0].astype(F32), qb_ref[0].astype(F32))
    cell = lax.broadcasted_iota(jnp.int32, (1, rows), 1)
    frame = lax.div(cell, tok_slots) + step * block_frames
    token = lax.rem(cell, tok_slots)
    has_label = token < token_len
    count = jnp.full((1, rows), frame_len * (token_len + 1), jnp.int32).astype(F32)
    weight = jnp.where((frame < frame_len) & (token <= token_len), 1.0 / count, 0.0)
    q_blank = q[0:1]
    q_label = jnp.where(has_label, q[1:2], 0.0)
    q_rest = q[2:3]
    rest_sum = st_ref[0:1]
    z_blank = st_ref[1:2]
    z_label = st_ref[2:3]
    e_blank = jnp.exp(z_blank)
    e_label = jnp.exp(z_label)
    total = rest_sum + e_blank + jnp.where(has_label, e_label, 0.0)
    log_total = jnp.log(total)
    cell_loss = -(
        q_blank * (z_blank - log_total)
        + q_label * (z_label - log_total)
        + q_rest * (jnp.log(rest_sum) - log_total)
    )
    loss_scr[...] += cell_loss * weight
    soft = weight * (q_blank + q_label + q_rest) / total
    scale = soft - weight * q_rest / rest_sum
    d_blank = soft * e_blank - weight * q_blank
    d_label = soft * e_label - weight * q_label
    place = lax.broadcasted_iota(jnp.int32, (8, rows), 0)
    packed = jnp.where(place == 0, scale, jnp.where(place == 1, d_label, d_blank))
    columns = packed.T
    scale = jnp.broadcast_to(columns[:, 0:1], (rows, LANES))
    d_label = jnp.broadcast_to(columns[:, 1:2], (rows, LANES))
    lane = lax.broadcasted_iota(jnp.int32, (rows, LANES), 1)
    base = pl.multiple_of(step * rows, rows)
    for j in range(vocab // LANES):
        cols = slice(j * LANES, (j + 1) * LANES)
        d = jnp.where(lane + j * LANES == target_scr[...], d_label, e_ref[:, cols] * scale)
        if j == 0:
            d = jnp.where(lane == 0, columns[:, 2:3], d)
        low = d.astype(BF16)
        d_ref[:, cols] = low
        d_scr[pl.ds(base, rows), cols] = low
        gb_scr[:, cols] += jnp.sum(d.reshape(rows // 8, 8, LANES), axis=0)

    @pl.when(step == steps - 1)
    def _():
        loss_ref[...] = jnp.sum(loss_scr[...], axis=1, keepdims=True)
        part = vocab // 2
        core = pick_ref[2]
        col = pl.multiple_of((1 - core) * part, part)
        dw = jnp.dot(jt_ref[...], d_scr[:, pl.ds(col, part)], preferred_element_type=F32)
        send_ref[:width, :] = dw.astype(BF16)
        col = pl.multiple_of(core * part, part)
        keep_ref[:width, :] = jnp.dot(jt_ref[...], d_scr[:, pl.ds(col, part)], preferred_element_type=F32)
        bias = jnp.sum(gb_scr[...], axis=0, keepdims=True)
        first, second = bias[:, :part], bias[:, part:]
        mine = jnp.where(core == 0, first, second)
        other = jnp.where(core == 0, second, first)
        keep_ref[width:, :] = jnp.broadcast_to(mine, (EXTRA, part))
        high = other.astype(BF16)
        low = (other - high.astype(F32)).astype(BF16)
        place = lax.broadcasted_iota(jnp.int32, (EXTRA, part), 0)
        packed = jnp.where(place == 0, high.astype(F32), jnp.where(place == 1, low.astype(F32), 0.0))
        send_ref[width:, :] = packed.astype(BF16)


def input_kernel(begin, last, enc_ref, pred_ref, d_ref, w_ref, *refs):
    ge_ref, gp_ref, enc_scr, ge_scr, gp_scr = refs[-5:]
    step = pl.program_id(0)
    steps = pl.num_programs(0)
    rows = d_ref.shape[0]
    tok_slots, width = pred_ref.shape
    block_frames = rows // tok_slots

    @pl.when(step == 0)
    def _():
        enc_scr[...] = enc_ref[...].astype(F32)
        gp_scr[...] = jnp.zeros_like(gp_scr) if begin == 0 else refs[0][...]

    first = pl.multiple_of(step * block_frames, block_frames)
    d_hidden = lax.dot_general(
        d_ref[...], w_ref[...], (((1,), (1,)), ((), ())), preferred_element_type=F32
    )
    enc = enc_scr[pl.ds(begin * block_frames + first, block_frames), :]
    act = jnp.tanh(enc[:, None, :] + pred_ref[...].astype(F32)[None, :, :])
    d_pre = d_hidden.reshape(block_frames, tok_slots, width) * (1.0 - act * act)
    ge_scr[pl.ds(first, block_frames), :] = jnp.sum(d_pre, axis=1)
    gp_scr[...] += jnp.sum(d_pre, axis=0)

    @pl.when(step == steps - 1)
    def _():
        ge_ref[...] = ge_scr[...].astype(BF16)
        gp_ref[...] = gp_scr[...].astype(gp_ref.dtype)


def final_kernel(pick_ref, *refs):
    out_ref, bias_ref = refs[-2:]
    for c in range(CHAINS):
        source_ref, rows_ref = refs[2 * c], refs[2 * c + 1]
        span = source_ref.shape[1]
        cols = slice(c * span, (c + 1) * span)
        out_ref[:, cols] = source_ref[...].astype(F32)
        bias_ref[:, cols] = rows_ref[0:1, :].astype(F32) + rows_ref[1:2, :].astype(F32)


def widen(pick, sources, width, vocab, mine, before):
    span = sources[0].shape[1]
    rows = width // 2

    def column(pick):
        return pick[2] if mine else 1 - pick[2]

    pair = [
        pl.BlockSpec((rows, span), lambda i, pick: (i, 0)),
        pl.BlockSpec((EXTRA, span), lambda i, pick: (width // EXTRA, 0)),
    ]
    return pl.pallas_call(
        final_kernel,
        grid_spec=pltpu.PrefetchScalarGridSpec(
            num_scalar_prefetch=1,
            grid=(width // rows,),
            in_specs=pair * CHAINS + [pl.BlockSpec(memory_space=pl.ANY)] * len(before),
            out_specs=[
                pl.BlockSpec((rows, vocab // 2), lambda i, pick: (i, column(pick))),
                pl.BlockSpec((1, vocab // 2), lambda i, pick: (0, column(pick))),
            ],
        ),
        out_shape=[
            jax.ShapeDtypeStruct((width, vocab), F32), jax.ShapeDtypeStruct((1, vocab), F32)
        ],
        input_output_aliases={1 + 2 * CHAINS + k: k for k in range(len(before))},
        compiler_params=params(8),
    )(pick, *[s for source in sources for s in (source, source)], *before)


def whole(shape):
    return pl.BlockSpec(shape, lambda *_: (0,) * len(shape))


SMEM_SPEC = pl.BlockSpec(memory_space=pltpu.SMEM)


def forward(tlen, labels, enc, pred, w, bias, rows, begin, blocks, before):
    frames, width = enc.shape
    tok_slots = pred.shape[0]
    vocab = w.shape[1]
    cells = frames * tok_slots
    return pl.pallas_call(
        functools.partial(forward_kernel, begin),
        grid=(blocks,),
        in_specs=[
            SMEM_SPEC, whole(labels.shape), whole(enc.shape), whole(pred.shape),
            whole(w.shape), whole(bias.shape),
        ] + [pl.BlockSpec(memory_space=pl.ANY)] * len(before),
        out_specs=[
            pl.BlockSpec((rows, vocab), lambda i: (i + begin, 0)),
            pl.BlockSpec((8, rows), lambda i: (0, i + begin)),
            pl.BlockSpec((width, rows), lambda i: (0, i + begin)),
        ],
        out_shape=[
            jax.ShapeDtypeStruct((cells, vocab), F32),
            jax.ShapeDtypeStruct((8, cells), F32),
            jax.ShapeDtypeStruct((width, cells), BF16),
        ],
        scratch_shapes=[pltpu.VMEM((frames, width), F32), pltpu.VMEM((2, SUB, vocab), F32)],
        input_output_aliases={6 + k: k for k in range(len(before))},
        compiler_params=params(16),
    )(tlen, in_vmem(labels), in_vmem(enc), in_vmem(pred), in_vmem(w), in_vmem(bias), *before)


def gradients(pick, flen, tlen, labels, qa, qb, e, st, jt, rows):
    cells, vocab = e.shape
    width = jt.shape[0]
    part = vocab // 2
    smem = pl.BlockSpec(memory_space=pltpu.SMEM)
    grid_spec = pltpu.PrefetchScalarGridSpec(
        num_scalar_prefetch=1,
        grid=(cells // rows,),
        in_specs=[
            smem, smem, whole(labels.shape),
            pl.BlockSpec((1, 3, rows), lambda i, pick: (lax.rem(pick[0], pick[1]), 0, i)),
            pl.BlockSpec((1, 3, rows), lambda i, pick: (lax.rem(pick[0], pick[1]), 0, i)),
            pl.BlockSpec((rows, vocab), lambda i, pick: (i, 0)),
            pl.BlockSpec((8, rows), lambda i, pick: (0, i)),
            whole(jt.shape),
        ],
        out_specs=[
            pl.BlockSpec((rows, vocab), lambda i, pick: (i, 0)),
            whole((1, 1)),
            whole((width + EXTRA, part)),
            whole((width + EXTRA, part)),
        ],
        scratch_shapes=[
            pltpu.VMEM((cells, vocab), BF16),
            pltpu.VMEM((8, vocab), F32),
            pltpu.VMEM((1, rows), F32),
            pltpu.VMEM((rows, LANES), jnp.int32),
        ],
    )
    return pl.pallas_call(
        grad_kernel,
        grid_spec=grid_spec,
        out_shape=[
            pltpu.HBM((cells, vocab), BF16),
            jax.ShapeDtypeStruct((1, 1), F32),
            jax.ShapeDtypeStruct((width + EXTRA, part), BF16),
            jax.ShapeDtypeStruct((width + EXTRA, part), F32),
        ],
        compiler_params=params(20),
    )(pick, flen, tlen, in_vmem(labels), qa, qb, e, st, jt)


def input_gradients(enc, pred, d_low, w, rows, begin, last, before):
    frames, width = enc.shape
    vocab = d_low.shape[1]
    cells = frames // 2 * pred.shape[0]
    half = (frames // 2, width)
    extra = () if not before else (before[1], before[0])
    return pl.pallas_call(
        functools.partial(input_kernel, begin, last),
        grid=(cells // rows,),
        in_specs=[
            whole(enc.shape), whole(pred.shape),
            pl.BlockSpec((rows, vocab), lambda i: (i + begin, 0)), whole(w.shape),
        ] + ([whole(pred.shape), pl.BlockSpec(memory_space=pl.ANY)] if before else []),
        out_specs=[pl.BlockSpec(half, lambda i: (1 if last else 0, 0)), whole(pred.shape)],
        out_shape=[
            jax.ShapeDtypeStruct(enc.shape, BF16),
            jax.ShapeDtypeStruct(pred.shape, BF16 if last else F32),
        ],
        scratch_shapes=[
            pltpu.VMEM(enc.shape, F32), pltpu.VMEM(half, F32), pltpu.VMEM(pred.shape, F32)
        ],
        input_output_aliases={5: 0} if before else {},
        compiler_params=params(12),
    )(in_vmem(enc), in_vmem(pred), pltpu.with_memory_space_constraint(d_low, pltpu.HBM), in_vmem(w), *extra)


def split_two(value):
    high = lax.reduce_precision(value, 8, 7)
    return high, lax.reduce_precision(value - high, 8, 7)


def on_device(
    dp, teacher_post, assignment, encoder_out, predictor_out, frame_lengths, token_lengths,
    labels, out_weight, out_bias,
):
    own = lax.axis_index("dp")
    core = own & 1
    masks = [1 << k for k in range(dp.bit_length() - 1)]
    tok_slots = predictor_out.shape[1]
    rows = 16 * tok_slots
    width, vocab = out_weight.shape
    part = vocab // 2

    def exchange(value, even, odd):
        pairs = [(k, k ^ (odd if k & 1 else even)) for k in range(dp)]
        return lax.ppermute(value, "dp", pairs)

    blocks = encoder_out.shape[1] * tok_slots // rows
    quarter = blocks // 4
    shares = [(0, quarter), (quarter, quarter), (2 * quarter, blocks - 2 * quarter)]
    held, made = teacher_post, ()
    staged = stage(
        assignment, out_weight, encoder_out[0], predictor_out[0], out_bias.reshape(1, vocab), labels
    )
    for k, mask in enumerate(masks):
        got = exchange(held, mask, mask)
        part_no = k - (len(masks) - len(shares))
        if part_no >= 0:
            begin, number = shares[part_no]
            made = tuple(forward(
                token_lengths, label_row, enc, pred, weight, bias_row, rows, begin, number, made
            ))
        if k < len(masks) - 1:
            held = jnp.concatenate([held, got], axis=0)
            held, made, staged = lax.optimization_barrier((held, made, staged))
            weight, enc, pred, bias_row, label_row, pick = staged
    far = got
    e, st, jt = made
    d_low, loss, send, keep = gradients(
        pick, frame_lengths, token_lengths, label_row, held, far, e, st, jt, rows
    )
    got = exchange(send, 1, 1)

    def got_bias(rows_of):
        return rows_of[0:1].astype(F32) + rows_of[1:2].astype(F32)

    def bias_rows(high, low):
        filler = jnp.zeros((EXTRA - 2, high.shape[1]), BF16)
        return jnp.concatenate([high.astype(BF16), low.astype(BF16), filler], axis=0)

    acc = keep[:width] + got[:width].astype(F32)
    bias = keep[width : width + 1] + got_bias(got[width:])
    rest = masks[1:]
    even_order = rest
    odd_order = rest[1:2] + rest[:1] + rest[2:]
    orders = list(zip(even_order, odd_order))
    sides = []
    count = width
    done = ()
    for k, (even, odd) in enumerate(orders[:-1]):
        high, low = split_two(bias)
        side = (own & jnp.where(core == 0, even, odd)) != 0
        sides.append(side)
        count //= 2
        top, bottom = acc[:count], acc[count:]
        send = jnp.where(side, top, bottom).astype(BF16)
        acc = jnp.where(side, bottom, top)
        send = jnp.concatenate([send, bias_rows(high, low)], axis=0)
        if k < 2:
            send, acc, d_low = lax.optimization_barrier((send, acc, d_low))
        got = exchange(send, even, odd)
        if k < 2:
            done = input_gradients(
                enc, pred, d_low, weight, rows, k * (blocks // 2), k == 1, done
            )
            got, done = lax.optimization_barrier((got, done))
        acc = acc + got[:count].astype(F32)
        bias = (high + low) + got_bias(got[count:])
    chains = range(CHAINS)
    span = part // CHAINS
    even, odd = orders[-1]
    sums, kept, parts = [], [], []
    for c in chains:
        cols = slice(c * span, (c + 1) * span)
        high, low = split_two(bias[:, cols])
        sums.append((high, low))
        sent = acc[:, cols].astype(BF16)
        kept.append(lax.reduce_precision(acc[:, cols], 8, 7))
        parts.append(exchange(jnp.concatenate([sent, bias_rows(high, low)], axis=0), even, odd))
    have = []
    for c in chains:
        got = parts[c]
        if c:
            got, have = lax.optimization_barrier((got, have))
        have.append((kept[c] + got[:count].astype(F32)).astype(BF16))
        high, low = sums[c]
        sums[c] = split_two((high + low) + got_bias(got[count:]))
    for (even, odd), side in list(zip(orders, sides))[::-1]:
        parts = [exchange(have[c], even, odd) for c in chains]
        joined = []
        for c in chains:
            if c:
                parts[c], joined = lax.optimization_barrier((parts[c], joined))
            joined.append(jnp.where(
                side,
                jnp.concatenate([parts[c], have[c]], axis=0),
                jnp.concatenate([have[c], parts[c]], axis=0),
            ))
        have = joined
    sent = [jnp.concatenate([have[c], bias_rows(*sums[c])], axis=0) for c in chains]
    others = [exchange(sent[c], 1, 1) for c in chains]
    result = tuple(widen(pick, sent, width, vocab, True, ()))
    others, result = lax.optimization_barrier((others, result))
    result = tuple(widen(pick, others, width, vocab, False, result))
    grad_weight, grad_bias = result
    return (loss.reshape(1), grad_weight, grad_bias.reshape(vocab), done[0][None], done[1][None])


def solution(mesh):
    in_specs = (
        P(("groups", "dp"), None, None),
        P("groups"),
        P(("groups", "dp"), None, None),
        P(("groups", "dp"), None, None),
        P(("groups", "dp")),
        P(("groups", "dp")),
        P(("groups", "dp"), None),
        P(),
        P(),
    )
    out_specs = (
        P(("groups", "dp")),
        P("groups", None),
        P("groups"),
        P(("groups", "dp"), None, None),
        P(("groups", "dp"), None, None),
    )
    return jax.shard_map(
        functools.partial(on_device, mesh.shape["dp"]),
        mesh=mesh, in_specs=in_specs, out_specs=out_specs, check_vma=False,
    )
```

```python
import functools

import jax
import jax.numpy as jnp
from jax import lax
from jax.experimental import pallas as pl
from jax.experimental.pallas import tpu as pltpu
from jax.sharding import PartitionSpec as P

F32 = jnp.float32
BF16 = jnp.bfloat16
LANES = 128
EXTRA = 16
CHAINS = 2


def params(mib):
    return pltpu.CompilerParams(
        dimension_semantics=("arbitrary",), vmem_limit_bytes=mib * 1024 * 1024
    )


def target_column(labels_ref, token_len, tok_slots, reps):
    tok = labels_ref.shape[1]
    row = lax.broadcasted_iota(jnp.int32, (tok_slots, tok), 0)
    lane = lax.broadcasted_iota(jnp.int32, (tok_slots, tok), 1)
    picked = jnp.where(row == lane, labels_ref[...].astype(F32), 0.0)
    column = jnp.sum(picked, axis=1, keepdims=True)
    token = lax.broadcasted_iota(jnp.int32, (tok_slots, 1), 0)
    column = jnp.where(token < token_len, column, -1.0).astype(jnp.int32)
    whole = jnp.broadcast_to(column[None], (reps, tok_slots, 1))
    return whole.reshape(reps * tok_slots, 1)


def stage_kernel(assignment_ref, *refs):
    count = (len(refs) - 2) // 2
    sources, targets, pick_ref, sems = refs[:count], refs[count : 2 * count], refs[-2], refs[-1]
    copies = [
        pltpu.make_async_copy(source, target, sems.at[k])
        for k, (source, target) in enumerate(zip(sources, targets))
    ]
    for copy in copies:
        copy.start()
    own = lax.axis_index("dp")
    pick_ref[0] = assignment_ref[own] ^ own
    pick_ref[1] = assignment_ref.shape[0] // 2
    pick_ref[2] = own & 1
    for copy in copies:
        copy.wait()


def stage(assignment, *arrays):
    anywhere = pl.BlockSpec(memory_space=pl.ANY)
    smem = pl.BlockSpec(memory_space=pltpu.SMEM)
    return pl.pallas_call(
        stage_kernel,
        in_specs=[smem] + [anywhere] * len(arrays),
        out_specs=[anywhere] * len(arrays) + [smem],
        out_shape=[jax.ShapeDtypeStruct(x.shape, x.dtype) for x in arrays]
        + [jax.ShapeDtypeStruct((3,), jnp.int32)],
        scratch_shapes=[pltpu.SemaphoreType.DMA((len(arrays),))],
        compiler_params=pltpu.CompilerParams(vmem_limit_bytes=4 * 1024 * 1024),
    )(*[pltpu.with_memory_space_constraint(x, pltpu.HBM) for x in (assignment, *arrays)])


def in_vmem(x):
    return x


SUB = 256


def forward_kernel(begin, tlen_ref, labels_ref, enc_ref, pred_ref, w_ref, b_ref, *refs):
    e_ref, st_ref, jt_ref, enc_scr, logit_scr = refs[-5:]
    step = pl.program_id(0)
    rows, vocab = e_ref.shape
    tok_slots, width = pred_ref.shape
    block_frames = rows // tok_slots

    @pl.when(step == 0)
    def _():
        enc_scr[...] = enc_ref[...].astype(F32)

    first = pl.multiple_of((begin + step) * block_frames, block_frames)
    enc = enc_scr[pl.ds(first, block_frames), :]
    pred = pred_ref[...].astype(F32)
    sub_frames = SUB // tok_slots
    target = target_column(labels_ref, tlen_ref[0], tok_slots, sub_frames)
    lane = lax.broadcasted_iota(jnp.int32, (SUB, LANES), 1)
    parts = rows // SUB

    def multiply(k):
        place = slice(k * SUB, (k + 1) * SUB)
        act = jnp.tanh(enc[k * sub_frames : (k + 1) * sub_frames, None, :] + pred[None, :, :])
        joint_in = act.reshape(SUB, width).astype(BF16)
        jt_ref[:, place] = joint_in.T
        logit_scr[k % 2] = jnp.dot(joint_in, w_ref[...], preferred_element_type=F32)

    def collapse(k):
        place = slice(k * SUB, (k + 1) * SUB)
        tops = jnp.full((SUB, LANES), -jnp.inf, F32)
        for j in range(vocab // LANES):
            cols = slice(j * LANES, (j + 1) * LANES)
            tops = jnp.maximum(tops, logit_scr[k % 2, :, cols] + b_ref[:, cols])
        row_max = jnp.max(tops, axis=1, keepdims=True)
        rest_acc = jnp.zeros((SUB, LANES), F32)
        label_acc = jnp.zeros((SUB, LANES), F32)
        for j in range(vocab // LANES):
            cols = slice(j * LANES, (j + 1) * LANES)
            shifted = logit_scr[k % 2, :, cols] + b_ref[:, cols] - row_max
            e = jnp.exp(shifted)
            e_ref[place, cols] = e
            hot = lane == target - j * LANES
            rest = jnp.where(hot, 0.0, e)
            if j == 0:
                z_blank = shifted[:, 0:1]
                rest = jnp.where(lane == 0, 0.0, rest)
            rest_acc = rest_acc + rest
            label_acc = label_acc + jnp.where(hot, shifted, 0.0)
        rest_sum = jnp.sum(rest_acc, axis=1, keepdims=True)
        z_label = jnp.sum(label_acc, axis=1, keepdims=True)
        packed = jnp.where(lane == 0, rest_sum, jnp.where(lane == 1, z_blank, z_label))
        st_ref[:, place] = packed.T[:8]

    multiply(0)
    for k in range(parts):
        if k + 1 < parts:
            multiply(k + 1)
        collapse(k)


def grad_kernel(
    blocks, pick_ref, flen_ref, tlen_ref, labels_ref, qa_ref, qb_ref, e_ref, st_ref, jt_ref,
    d_ref, loss_ref, send_ref, keep_ref, low_scr, high_scr, dw_scr, gb_scr, loss_scr, target_scr,
):
    step = pl.program_id(0)
    steps = pl.num_programs(0)
    rows, vocab = e_ref.shape
    tok_slots = labels_ref.shape[1] + 1
    block_frames = rows // tok_slots
    width = jt_ref.shape[0]
    frame_len, token_len = flen_ref[0], tlen_ref[0]

    @pl.when(step == 0)
    def _():
        gb_scr[...] = jnp.zeros_like(gb_scr)
        loss_scr[...] = jnp.zeros_like(loss_scr)
        column = target_column(labels_ref, token_len, tok_slots, block_frames)
        target_scr[...] = jnp.broadcast_to(column, (rows, LANES))

    def collapse(held_ref):
        half_count = pick_ref[1]
        q = jnp.where(pick_ref[0] < half_count, qa_ref[0].astype(F32), qb_ref[0].astype(F32))
        cell = lax.broadcasted_iota(jnp.int32, (1, rows), 1)
        frame = lax.div(cell, tok_slots) + step * block_frames
        token = lax.rem(cell, tok_slots)
        has_label = token < token_len
        count = jnp.full((1, rows), frame_len * (token_len + 1), jnp.int32).astype(F32)
        weight = jnp.where((frame < frame_len) & (token <= token_len), 1.0 / count, 0.0)
        q_blank = q[0:1]
        q_label = jnp.where(has_label, q[1:2], 0.0)
        q_rest = q[2:3]
        rest_sum = st_ref[0:1]
        z_blank = st_ref[1:2]
        z_label = st_ref[2:3]
        e_blank = jnp.exp(z_blank)
        e_label = jnp.exp(z_label)
        total = rest_sum + e_blank + jnp.where(has_label, e_label, 0.0)
        log_total = jnp.log(total)
        cell_loss = -(
            q_blank * (z_blank - log_total)
            + q_label * (z_label - log_total)
            + q_rest * (jnp.log(rest_sum) - log_total)
        )
        loss_scr[...] += cell_loss * weight
        soft = weight * (q_blank + q_label + q_rest) / total
        scale = soft - weight * q_rest / rest_sum
        d_blank = soft * e_blank - weight * q_blank
        d_label = soft * e_label - weight * q_label
        place = lax.broadcasted_iota(jnp.int32, (8, rows), 0)
        packed = jnp.where(place == 0, scale, jnp.where(place == 1, d_label, d_blank))
        columns = packed.T
        scale = jnp.broadcast_to(columns[:, 0:1], (rows, LANES))
        d_label = jnp.broadcast_to(columns[:, 1:2], (rows, LANES))
        lane = lax.broadcasted_iota(jnp.int32, (rows, LANES), 1)
        for j in range(vocab // LANES):
            cols = slice(j * LANES, (j + 1) * LANES)
            d = jnp.where(lane + j * LANES == target_scr[...], d_label, e_ref[:, cols] * scale)
            if j == 0:
                d = jnp.where(lane == 0, columns[:, 2:3], d)
            low = d.astype(BF16)
            d_ref[:, cols] = low
            held_ref[:, cols] = low
            gb_scr[:, cols] += jnp.sum(d.reshape(rows // 8, 8, LANES), axis=0)

    slots = (low_scr, high_scr)
    last_ref = slots[(blocks - 1) % 2]

    @pl.when(step == 0)
    def _():
        collapse(slots[0])

    for block in range(1, blocks):

        @pl.when(step == block)
        def _(block=block):
            dw = jnp.dot(jt_ref[...], slots[(block - 1) % 2][...], preferred_element_type=F32)
            dw_scr[...] = dw if block == 1 else dw_scr[...] + dw
            collapse(slots[block % 2])

    @pl.when(step == steps - 1)
    def _():
        loss_ref[...] = jnp.sum(loss_scr[...], axis=1, keepdims=True)
        part = vocab // 2
        core = pick_ref[2]
        col = pl.multiple_of((1 - core) * part, part)
        dw = dw_scr[:, pl.ds(col, part)] + jnp.dot(
            jt_ref[...], last_ref[:, pl.ds(col, part)], preferred_element_type=F32
        )
        send_ref[:width, :] = dw.astype(BF16)
        col = pl.multiple_of(core * part, part)
        keep_ref[:width, :] = dw_scr[:, pl.ds(col, part)] + jnp.dot(
            jt_ref[...], last_ref[:, pl.ds(col, part)], preferred_element_type=F32
        )
        bias = jnp.sum(gb_scr[...], axis=0, keepdims=True)
        first, second = bias[:, :part], bias[:, part:]
        mine = jnp.where(core == 0, first, second)
        other = jnp.where(core == 0, second, first)
        keep_ref[width:, :] = jnp.broadcast_to(mine, (EXTRA, part))
        high = other.astype(BF16)
        low = (other - high.astype(F32)).astype(BF16)
        place = lax.broadcasted_iota(jnp.int32, (EXTRA, part), 0)
        packed = jnp.where(place == 0, high.astype(F32), jnp.where(place == 1, low.astype(F32), 0.0))
        send_ref[width:, :] = packed.astype(BF16)


def input_kernel(begin, last, enc_ref, pred_ref, d_ref, w_ref, *refs):
    ge_ref, gp_ref, enc_scr, ge_scr, gp_scr = refs[-5:]
    step = pl.program_id(0)
    steps = pl.num_programs(0)
    rows = d_ref.shape[0]
    tok_slots, width = pred_ref.shape
    block_frames = rows // tok_slots

    @pl.when(step == 0)
    def _():
        enc_scr[...] = enc_ref[...].astype(F32)
        gp_scr[...] = jnp.zeros_like(gp_scr) if begin == 0 else refs[0][...]

    first = pl.multiple_of(step * block_frames, block_frames)
    d_hidden = lax.dot_general(
        d_ref[...], w_ref[...], (((1,), (1,)), ((), ())), preferred_element_type=F32
    )
    enc = enc_scr[pl.ds(begin * block_frames + first, block_frames), :]
    act = jnp.tanh(enc[:, None, :] + pred_ref[...].astype(F32)[None, :, :])
    d_pre = d_hidden.reshape(block_frames, tok_slots, width) * (1.0 - act * act)
    ge_scr[pl.ds(first, block_frames), :] = jnp.sum(d_pre, axis=1)
    gp_scr[...] += jnp.sum(d_pre, axis=0)

    @pl.when(step == steps - 1)
    def _():
        ge_ref[...] = ge_scr[...].astype(BF16)
        gp_ref[...] = gp_scr[...].astype(gp_ref.dtype)


def final_kernel(pick_ref, *refs):
    out_ref, bias_ref = refs[-2:]
    for c in range(CHAINS):
        source_ref, rows_ref = refs[2 * c], refs[2 * c + 1]
        span = source_ref.shape[1]
        cols = slice(c * span, (c + 1) * span)
        out_ref[:, cols] = source_ref[...].astype(F32)
        bias_ref[:, cols] = rows_ref[0:1, :].astype(F32) + rows_ref[1:2, :].astype(F32)


def widen(pick, sources, width, vocab, mine, before):
    span = sources[0].shape[1]
    rows = width // 2

    def column(pick):
        return pick[2] if mine else 1 - pick[2]

    pair = [
        pl.BlockSpec((rows, span), lambda i, pick: (i, 0)),
        pl.BlockSpec((EXTRA, span), lambda i, pick: (width // EXTRA, 0)),
    ]
    return pl.pallas_call(
        final_kernel,
        grid_spec=pltpu.PrefetchScalarGridSpec(
            num_scalar_prefetch=1,
            grid=(width // rows,),
            in_specs=pair * CHAINS + [pl.BlockSpec(memory_space=pl.ANY)] * len(before),
            out_specs=[
                pl.BlockSpec((rows, vocab // 2), lambda i, pick: (i, column(pick))),
                pl.BlockSpec((1, vocab // 2), lambda i, pick: (0, column(pick))),
            ],
        ),
        out_shape=[
            jax.ShapeDtypeStruct((width, vocab), F32), jax.ShapeDtypeStruct((1, vocab), F32)
        ],
        input_output_aliases={1 + 2 * CHAINS + k: k for k in range(len(before))},
        compiler_params=params(8),
    )(pick, *[s for source in sources for s in (source, source)], *before)


def whole(shape):
    return pl.BlockSpec(shape, lambda *_: (0,) * len(shape))


SMEM_SPEC = pl.BlockSpec(memory_space=pltpu.SMEM)


def forward(tlen, labels, enc, pred, w, bias, rows, begin, blocks, before):
    frames, width = enc.shape
    tok_slots = pred.shape[0]
    vocab = w.shape[1]
    cells = frames * tok_slots
    return pl.pallas_call(
        functools.partial(forward_kernel, begin),
        grid=(blocks,),
        in_specs=[
            SMEM_SPEC, whole(labels.shape), whole(enc.shape), whole(pred.shape),
            whole(w.shape), whole(bias.shape),
        ] + [pl.BlockSpec(memory_space=pl.ANY)] * len(before),
        out_specs=[
            pl.BlockSpec((rows, vocab), lambda i: (i + begin, 0)),
            pl.BlockSpec((8, rows), lambda i: (0, i + begin)),
            pl.BlockSpec((width, rows), lambda i: (0, i + begin)),
        ],
        out_shape=[
            jax.ShapeDtypeStruct((cells, vocab), F32),
            jax.ShapeDtypeStruct((8, cells), F32),
            jax.ShapeDtypeStruct((width, cells), BF16),
        ],
        scratch_shapes=[pltpu.VMEM((frames, width), F32), pltpu.VMEM((2, SUB, vocab), F32)],
        input_output_aliases={6 + k: k for k in range(len(before))},
        compiler_params=params(16),
    )(tlen, in_vmem(labels), in_vmem(enc), in_vmem(pred), in_vmem(w), in_vmem(bias), *before)


def gradients(pick, flen, tlen, labels, qa, qb, e, st, jt, rows):
    cells, vocab = e.shape
    width = jt.shape[0]
    part = vocab // 2
    blocks = cells // rows

    def at(i):
        return jnp.minimum(i, blocks - 1)

    smem = pl.BlockSpec(memory_space=pltpu.SMEM)
    grid_spec = pltpu.PrefetchScalarGridSpec(
        num_scalar_prefetch=1,
        grid=(blocks + 1,),
        in_specs=[
            smem, smem, whole(labels.shape),
            pl.BlockSpec((1, 3, rows), lambda i, pick: (lax.rem(pick[0], pick[1]), 0, at(i))),
            pl.BlockSpec((1, 3, rows), lambda i, pick: (lax.rem(pick[0], pick[1]), 0, at(i))),
            pl.BlockSpec((rows, vocab), lambda i, pick: (at(i), 0)),
            pl.BlockSpec((8, rows), lambda i, pick: (0, at(i))),
            pl.BlockSpec((width, rows), lambda i, pick: (0, jnp.maximum(i - 1, 0))),
        ],
        out_specs=[
            pl.BlockSpec((rows, vocab), lambda i, pick: (at(i), 0)),
            whole((1, 1)),
            whole((width + EXTRA, part)),
            whole((width + EXTRA, part)),
        ],
        scratch_shapes=[
            pltpu.VMEM((rows, vocab), BF16),
            pltpu.VMEM((rows, vocab), BF16),
            pltpu.VMEM((width, vocab), F32),
            pltpu.VMEM((8, vocab), F32),
            pltpu.VMEM((1, rows), F32),
            pltpu.VMEM((rows, LANES), jnp.int32),
        ],
    )
    return pl.pallas_call(
        functools.partial(grad_kernel, blocks),
        grid_spec=grid_spec,
        out_shape=[
            pltpu.HBM((cells, vocab), BF16),
            jax.ShapeDtypeStruct((1, 1), F32),
            jax.ShapeDtypeStruct((width + EXTRA, part), BF16),
            jax.ShapeDtypeStruct((width + EXTRA, part), F32),
        ],
        compiler_params=params(20),
    )(pick, flen, tlen, in_vmem(labels), qa, qb, e, st, jt)


def input_gradients(enc, pred, d_low, w, rows, begin, last, before):
    frames, width = enc.shape
    vocab = d_low.shape[1]
    cells = frames // 2 * pred.shape[0]
    half = (frames // 2, width)
    extra = () if not before else (before[1], before[0])
    return pl.pallas_call(
        functools.partial(input_kernel, begin, last),
        grid=(cells // rows,),
        in_specs=[
            whole(enc.shape), whole(pred.shape),
            pl.BlockSpec((rows, vocab), lambda i: (i + begin, 0)), whole(w.shape),
        ] + ([whole(pred.shape), pl.BlockSpec(memory_space=pl.ANY)] if before else []),
        out_specs=[pl.BlockSpec(half, lambda i: (1 if last else 0, 0)), whole(pred.shape)],
        out_shape=[
            jax.ShapeDtypeStruct(enc.shape, BF16),
            jax.ShapeDtypeStruct(pred.shape, BF16 if last else F32),
        ],
        scratch_shapes=[
            pltpu.VMEM(enc.shape, F32), pltpu.VMEM(half, F32), pltpu.VMEM(pred.shape, F32)
        ],
        input_output_aliases={5: 0} if before else {},
        compiler_params=params(12),
    )(in_vmem(enc), in_vmem(pred), pltpu.with_memory_space_constraint(d_low, pltpu.HBM), in_vmem(w), *extra)


def merge_kernel(even, odd, keep_ref, got_ref, acc_ref, send_ref, bias_ref):
    own = lax.axis_index("dp")
    mask = jnp.where((own & 1) == 0, even, odd)
    side = jnp.where((own & mask) != 0, 1, 0)
    count, part = acc_ref.shape
    stay = pl.ds(pl.multiple_of(side * count, count), count)
    leave = pl.ds(pl.multiple_of((1 - side) * count, count), count)
    send_ref[:count, :] = (keep_ref[leave, :] + got_ref[leave, :].astype(F32)).astype(BF16)
    acc_ref[...] = keep_ref[stay, :] + got_ref[stay, :].astype(F32)
    rows = got_ref[2 * count :, :].astype(F32)
    bias = keep_ref[2 * count : 2 * count + 1, :] + rows[0:1] + rows[1:2]
    high = bias.astype(BF16).astype(F32)
    low = (bias - high).astype(BF16).astype(F32)
    bias_ref[...] = high + low
    place = lax.broadcasted_iota(jnp.int32, (EXTRA, part), 0)
    packed = jnp.where(place == 0, high, jnp.where(place == 1, low, 0.0))
    send_ref[count:, :] = packed.astype(BF16)


def merge(keep, got, even, odd):
    rows, part = got.shape
    count = (rows - EXTRA) // 2
    return pl.pallas_call(
        functools.partial(merge_kernel, even, odd),
        grid=(1,),
        in_specs=[whole(keep.shape), whole(got.shape)],
        out_specs=[whole((count, part)), whole((count + EXTRA, part)), whole((1, part))],
        out_shape=[
            jax.ShapeDtypeStruct((count, part), F32),
            jax.ShapeDtypeStruct((count + EXTRA, part), BF16),
            jax.ShapeDtypeStruct((1, part), F32),
        ],
        compiler_params=params(12),
    )(keep, got)


def split_two(value):
    high = lax.reduce_precision(value, 8, 7)
    return high, lax.reduce_precision(value - high, 8, 7)


def on_device(
    dp, teacher_post, assignment, encoder_out, predictor_out, frame_lengths, token_lengths,
    labels, out_weight, out_bias,
):
    own = lax.axis_index("dp")
    core = own & 1
    masks = [1 << k for k in range(dp.bit_length() - 1)]
    tok_slots = predictor_out.shape[1]
    rows = 16 * tok_slots
    width, vocab = out_weight.shape
    part = vocab // 2

    def exchange(value, even, odd):
        pairs = [(k, k ^ (odd if k & 1 else even)) for k in range(dp)]
        return lax.ppermute(value, "dp", pairs)

    blocks = encoder_out.shape[1] * tok_slots // rows
    quarter = blocks // 4
    shares = [(0, quarter), (quarter, quarter), (2 * quarter, blocks - 2 * quarter)]
    held, made = teacher_post, ()
    staged = stage(
        assignment, out_weight, encoder_out[0], predictor_out[0], out_bias.reshape(1, vocab), labels
    )
    for k, mask in enumerate(masks):
        got = exchange(held, mask, mask)
        part_no = k - (len(masks) - len(shares))
        if part_no >= 0:
            begin, number = shares[part_no]
            made = tuple(forward(
                token_lengths, label_row, enc, pred, weight, bias_row, rows, begin, number, made
            ))
        if k < len(masks) - 1:
            held = jnp.concatenate([held, got], axis=0)
            held, made, staged = lax.optimization_barrier((held, made, staged))
            weight, enc, pred, bias_row, label_row, pick = staged
    far = got
    e, st, jt = made
    d_low, loss, send, keep = gradients(
        pick, frame_lengths, token_lengths, label_row, held, far, e, st, jt, rows
    )
    got = exchange(send, 1, 1)

    def got_bias(rows_of):
        return rows_of[0:1].astype(F32) + rows_of[1:2].astype(F32)

    def bias_rows(high, low):
        filler = jnp.zeros((EXTRA - 2, high.shape[1]), BF16)
        return jnp.concatenate([high.astype(BF16), low.astype(BF16), filler], axis=0)

    rest = masks[1:]
    even_order = rest
    odd_order = rest[1:2] + rest[:1] + rest[2:]
    orders = list(zip(even_order, odd_order))
    sides = []
    count = width
    done = ()
    acc, send, bias = merge(keep, got, *orders[0])
    for k, (even, odd) in enumerate(orders[:-1]):
        side = (own & jnp.where(core == 0, even, odd)) != 0
        sides.append(side)
        count //= 2
        if k:
            high, low = split_two(bias)
            top, bottom = acc[:count], acc[count:]
            send = jnp.where(side, top, bottom).astype(BF16)
            acc = jnp.where(side, bottom, top)
            send = jnp.concatenate([send, bias_rows(high, low)], axis=0)
            bias = high + low
        if k < 2:
            send, acc, d_low = lax.optimization_barrier((send, acc, d_low))
        got = exchange(send, even, odd)
        if k < 2:
            done = input_gradients(
                enc, pred, d_low, weight, rows, k * (blocks // 2), k == 1, done
            )
            got, done = lax.optimization_barrier((got, done))
        acc = acc + got[:count].astype(F32)
        bias = bias + got_bias(got[count:])
    chains = range(CHAINS)
    span = part // CHAINS
    even, odd = orders[-1]
    sums, kept, parts = [], [], []
    for c in chains:
        cols = slice(c * span, (c + 1) * span)
        high, low = split_two(bias[:, cols])
        sums.append((high, low))
        sent = acc[:, cols].astype(BF16)
        kept.append(lax.reduce_precision(acc[:, cols], 8, 7))
        parts.append(exchange(jnp.concatenate([sent, bias_rows(high, low)], axis=0), even, odd))
    have = []
    for c in chains:
        got = parts[c]
        if c:
            got, have = lax.optimization_barrier((got, have))
        have.append((kept[c] + got[:count].astype(F32)).astype(BF16))
        high, low = sums[c]
        sums[c] = split_two((high + low) + got_bias(got[count:]))
    for (even, odd), side in list(zip(orders, sides))[::-1]:
        parts = [exchange(have[c], even, odd) for c in chains]
        joined = []
        for c in chains:
            if c:
                parts[c], joined = lax.optimization_barrier((parts[c], joined))
            joined.append(jnp.where(
                side,
                jnp.concatenate([parts[c], have[c]], axis=0),
                jnp.concatenate([have[c], parts[c]], axis=0),
            ))
        have = joined
    sent = [jnp.concatenate([have[c], bias_rows(*sums[c])], axis=0) for c in chains]
    others = [exchange(sent[c], 1, 1) for c in chains]
    result = tuple(widen(pick, sent, width, vocab, True, ()))
    others, result = lax.optimization_barrier((others, result))
    result = tuple(widen(pick, others, width, vocab, False, result))
    grad_weight, grad_bias = result
    return (loss.reshape(1), grad_weight, grad_bias.reshape(vocab), done[0][None], done[1][None])


def solution(mesh):
    in_specs = (
        P(("groups", "dp"), None, None),
        P("groups"),
        P(("groups", "dp"), None, None),
        P(("groups", "dp"), None, None),
        P(("groups", "dp")),
        P(("groups", "dp")),
        P(("groups", "dp"), None),
        P(),
        P(),
    )
    out_specs = (
        P(("groups", "dp")),
        P("groups", None),
        P("groups"),
        P(("groups", "dp"), None, None),
        P(("groups", "dp"), None, None),
    )
    return jax.shard_map(
        functools.partial(on_device, mesh.shape["dp"]),
        mesh=mesh, in_specs=in_specs, out_specs=out_specs, check_vma=False,
    )
```

```python
import functools

import jax
import jax.numpy as jnp
from jax import lax
from jax.experimental import pallas as pl
from jax.experimental.pallas import tpu as pltpu
from jax.sharding import PartitionSpec as P

F32 = jnp.float32
BF16 = jnp.bfloat16
LANES = 128
EXTRA = 16
CHAINS = 2


def params(mib):
    return pltpu.CompilerParams(
        dimension_semantics=("arbitrary",), vmem_limit_bytes=mib * 1024 * 1024
    )


def target_column(labels_ref, token_len, tok_slots, reps):
    tok = labels_ref.shape[1]
    row = lax.broadcasted_iota(jnp.int32, (tok_slots, tok), 0)
    lane = lax.broadcasted_iota(jnp.int32, (tok_slots, tok), 1)
    picked = jnp.where(row == lane, labels_ref[...].astype(F32), 0.0)
    column = jnp.sum(picked, axis=1, keepdims=True)
    token = lax.broadcasted_iota(jnp.int32, (tok_slots, 1), 0)
    column = jnp.where(token < token_len, column, -1.0).astype(jnp.int32)
    whole = jnp.broadcast_to(column[None], (reps, tok_slots, 1))
    return whole.reshape(reps * tok_slots, 1)


def stage_kernel(assignment_ref, *refs):
    count = (len(refs) - 3) // 2
    sources, targets = refs[:count], refs[count : 2 * count]
    pick_ref, order_ref, sems = refs[2 * count :]
    copies = [
        pltpu.make_async_copy(source, target, sems.at[k])
        for k, (source, target) in enumerate(
            zip((assignment_ref, *sources), (order_ref, *targets))
        )
    ]
    for copy in copies:
        copy.start()
    own = lax.axis_index("dp")
    copies[0].wait()
    pick_ref[0] = order_ref[own] ^ own
    pick_ref[1] = assignment_ref.shape[0] // 2
    pick_ref[2] = own & 1
    for copy in copies[1:]:
        copy.wait()


def stage(assignment, *arrays):
    anywhere = pl.BlockSpec(memory_space=pl.ANY)
    smem = pl.BlockSpec(memory_space=pltpu.SMEM)
    return pl.pallas_call(
        stage_kernel,
        in_specs=[anywhere] * (1 + len(arrays)),
        out_specs=[anywhere] * len(arrays) + [smem],
        out_shape=[jax.ShapeDtypeStruct(x.shape, x.dtype) for x in arrays]
        + [jax.ShapeDtypeStruct((3,), jnp.int32)],
        scratch_shapes=[
            pltpu.SMEM(assignment.shape, jnp.int32), pltpu.SemaphoreType.DMA((1 + len(arrays),))
        ],
        compiler_params=pltpu.CompilerParams(vmem_limit_bytes=4 * 1024 * 1024),
    )(*[pltpu.with_memory_space_constraint(x, pltpu.HBM) for x in (assignment, *arrays)])


def in_vmem(x):
    return x


SUB = 256


def forward_kernel(begin, tlen_ref, labels_ref, enc_ref, pred_ref, w_ref, b_ref, *refs):
    e_ref, st_ref, jt_ref, enc_scr, logit_scr = refs[-5:]
    step = pl.program_id(0)
    rows, vocab = e_ref.shape
    tok_slots, width = pred_ref.shape
    block_frames = rows // tok_slots

    @pl.when(step == 0)
    def _():
        enc_scr[...] = enc_ref[...].astype(F32)

    first = pl.multiple_of((begin + step) * block_frames, block_frames)
    enc = enc_scr[pl.ds(first, block_frames), :]
    pred = pred_ref[...].astype(F32)
    sub_frames = SUB // tok_slots
    target = target_column(labels_ref, tlen_ref[0], tok_slots, sub_frames)
    lane = lax.broadcasted_iota(jnp.int32, (SUB, LANES), 1)
    parts = rows // SUB

    def multiply(k):
        place = slice(k * SUB, (k + 1) * SUB)
        act = jnp.tanh(enc[k * sub_frames : (k + 1) * sub_frames, None, :] + pred[None, :, :])
        joint_in = act.reshape(SUB, width).astype(BF16)
        jt_ref[:, place] = joint_in.T
        logit_scr[k % 2] = jnp.dot(joint_in, w_ref[...], preferred_element_type=F32)

    def collapse(k):
        place = slice(k * SUB, (k + 1) * SUB)
        tops = jnp.full((SUB, LANES), -jnp.inf, F32)
        for j in range(vocab // LANES):
            cols = slice(j * LANES, (j + 1) * LANES)
            tops = jnp.maximum(tops, logit_scr[k % 2, :, cols] + b_ref[:, cols])
        row_max = jnp.max(tops, axis=1, keepdims=True)
        rest_acc = jnp.zeros((SUB, LANES), F32)
        label_acc = jnp.zeros((SUB, LANES), F32)
        for j in range(vocab // LANES):
            cols = slice(j * LANES, (j + 1) * LANES)
            shifted = logit_scr[k % 2, :, cols] + b_ref[:, cols] - row_max
            e = jnp.exp(shifted)
            e_ref[place, cols] = e
            hot = lane == target - j * LANES
            rest = jnp.where(hot, 0.0, e)
            if j == 0:
                z_blank = shifted[:, 0:1]
                rest = jnp.where(lane == 0, 0.0, rest)
            rest_acc = rest_acc + rest
            label_acc = label_acc + jnp.where(hot, shifted, 0.0)
        rest_sum = jnp.sum(rest_acc, axis=1, keepdims=True)
        z_label = jnp.sum(label_acc, axis=1, keepdims=True)
        packed = jnp.where(lane == 0, rest_sum, jnp.where(lane == 1, z_blank, z_label))
        st_ref[:, place] = packed.T[:8]

    multiply(0)
    for k in range(parts):
        if k + 1 < parts:
            multiply(k + 1)
        collapse(k)


def grad_kernel(
    blocks, pick_ref, flen_ref, tlen_ref, labels_ref, qa_ref, qb_ref, e_ref, st_ref, jt_ref,
    d_ref, loss_ref, send_ref, keep_ref, low_scr, high_scr, dw_scr, gb_scr, loss_scr, target_scr,
):
    step = pl.program_id(0)
    steps = pl.num_programs(0)
    rows, vocab = e_ref.shape
    tok_slots = labels_ref.shape[1] + 1
    block_frames = rows // tok_slots
    width = jt_ref.shape[0]
    frame_len, token_len = flen_ref[0], tlen_ref[0]

    @pl.when(step == 0)
    def _():
        gb_scr[...] = jnp.zeros_like(gb_scr)
        loss_scr[...] = jnp.zeros_like(loss_scr)
        column = target_column(labels_ref, token_len, tok_slots, block_frames)
        target_scr[...] = jnp.broadcast_to(column, (rows, LANES))

    def collapse(held_ref):
        half_count = pick_ref[1]
        q = jnp.where(pick_ref[0] < half_count, qa_ref[0].astype(F32), qb_ref[0].astype(F32))
        cell = lax.broadcasted_iota(jnp.int32, (1, rows), 1)
        frame = lax.div(cell, tok_slots) + step * block_frames
        token = lax.rem(cell, tok_slots)
        has_label = token < token_len
        count = jnp.full((1, rows), frame_len * (token_len + 1), jnp.int32).astype(F32)
        weight = jnp.where((frame < frame_len) & (token <= token_len), 1.0 / count, 0.0)
        q_blank = q[0:1]
        q_label = jnp.where(has_label, q[1:2], 0.0)
        q_rest = q[2:3]
        rest_sum = st_ref[0:1]
        z_blank = st_ref[1:2]
        z_label = st_ref[2:3]
        e_blank = jnp.exp(z_blank)
        e_label = jnp.exp(z_label)
        total = rest_sum + e_blank + jnp.where(has_label, e_label, 0.0)
        log_total = jnp.log(total)
        cell_loss = -(
            q_blank * (z_blank - log_total)
            + q_label * (z_label - log_total)
            + q_rest * (jnp.log(rest_sum) - log_total)
        )
        loss_scr[...] += cell_loss * weight
        soft = weight * (q_blank + q_label + q_rest) / total
        scale = soft - weight * q_rest / rest_sum
        d_blank = soft * e_blank - weight * q_blank
        d_label = soft * e_label - weight * q_label
        place = lax.broadcasted_iota(jnp.int32, (8, rows), 0)
        packed = jnp.where(place == 0, scale, jnp.where(place == 1, d_label, d_blank))
        columns = packed.T
        scale = jnp.broadcast_to(columns[:, 0:1], (rows, LANES))
        d_label = jnp.broadcast_to(columns[:, 1:2], (rows, LANES))
        lane = lax.broadcasted_iota(jnp.int32, (rows, LANES), 1)
        for j in range(vocab // LANES):
            cols = slice(j * LANES, (j + 1) * LANES)
            d = jnp.where(lane + j * LANES == target_scr[...], d_label, e_ref[:, cols] * scale)
            if j == 0:
                d = jnp.where(lane == 0, columns[:, 2:3], d)
            low = d.astype(BF16)
            d_ref[:, cols] = low
            held_ref[:, cols] = low
            gb_scr[:, cols] += jnp.sum(d.reshape(rows // 8, 8, LANES), axis=0)

    slots = (low_scr, high_scr)
    last_ref = slots[(blocks - 1) % 2]

    @pl.when(step == 0)
    def _():
        collapse(slots[0])

    for block in range(1, blocks):

        @pl.when(step == block)
        def _(block=block):
            dw = jnp.dot(jt_ref[...], slots[(block - 1) % 2][...], preferred_element_type=F32)
            dw_scr[...] = dw if block == 1 else dw_scr[...] + dw
            collapse(slots[block % 2])

    @pl.when(step == steps - 1)
    def _():
        loss_ref[...] = jnp.sum(loss_scr[...], axis=1, keepdims=True)
        part = vocab // 2
        core = pick_ref[2]
        col = pl.multiple_of((1 - core) * part, part)
        dw = dw_scr[:, pl.ds(col, part)] + jnp.dot(
            jt_ref[...], last_ref[:, pl.ds(col, part)], preferred_element_type=F32
        )
        send_ref[:width, :] = dw.astype(BF16)
        col = pl.multiple_of(core * part, part)
        keep_ref[:width, :] = dw_scr[:, pl.ds(col, part)] + jnp.dot(
            jt_ref[...], last_ref[:, pl.ds(col, part)], preferred_element_type=F32
        )
        bias = jnp.sum(gb_scr[...], axis=0, keepdims=True)
        first, second = bias[:, :part], bias[:, part:]
        mine = jnp.where(core == 0, first, second)
        other = jnp.where(core == 0, second, first)
        keep_ref[width:, :] = jnp.broadcast_to(mine, (EXTRA, part))
        high = other.astype(BF16)
        low = (other - high.astype(F32)).astype(BF16)
        place = lax.broadcasted_iota(jnp.int32, (EXTRA, part), 0)
        packed = jnp.where(place == 0, high.astype(F32), jnp.where(place == 1, low.astype(F32), 0.0))
        send_ref[width:, :] = packed.astype(BF16)


def input_kernel(begin, last, enc_ref, pred_ref, d_ref, w_ref, *refs):
    ge_ref, gp_ref, enc_scr, ge_scr, gp_scr = refs[-5:]
    step = pl.program_id(0)
    steps = pl.num_programs(0)
    rows = d_ref.shape[0]
    tok_slots, width = pred_ref.shape
    block_frames = rows // tok_slots

    @pl.when(step == 0)
    def _():
        enc_scr[...] = enc_ref[...].astype(F32)
        gp_scr[...] = jnp.zeros_like(gp_scr) if begin == 0 else refs[0][...]

    first = pl.multiple_of(step * block_frames, block_frames)
    d_hidden = lax.dot_general(
        d_ref[...], w_ref[...], (((1,), (1,)), ((), ())), preferred_element_type=F32
    )
    enc = enc_scr[pl.ds(begin * block_frames + first, block_frames), :]
    act = jnp.tanh(enc[:, None, :] + pred_ref[...].astype(F32)[None, :, :])
    d_pre = d_hidden.reshape(block_frames, tok_slots, width) * (1.0 - act * act)
    ge_scr[pl.ds(first, block_frames), :] = jnp.sum(d_pre, axis=1)
    gp_scr[...] += jnp.sum(d_pre, axis=0)

    @pl.when(step == steps - 1)
    def _():
        ge_ref[...] = ge_scr[...].astype(BF16)
        gp_ref[...] = gp_scr[...].astype(gp_ref.dtype)


def final_kernel(pick_ref, *refs):
    out_ref, bias_ref = refs[-2:]
    for c in range(CHAINS):
        source_ref, rows_ref = refs[2 * c], refs[2 * c + 1]
        span = source_ref.shape[1]
        cols = slice(c * span, (c + 1) * span)
        out_ref[:, cols] = source_ref[...].astype(F32)
        bias_ref[:, cols] = rows_ref[0:1, :].astype(F32) + rows_ref[1:2, :].astype(F32)


def widen(pick, sources, width, vocab, mine, before):
    span = sources[0].shape[1]
    rows = width // 2

    def column(pick):
        return pick[2] if mine else 1 - pick[2]

    pair = [
        pl.BlockSpec((rows, span), lambda i, pick: (i, 0)),
        pl.BlockSpec((EXTRA, span), lambda i, pick: (width // EXTRA, 0)),
    ]
    return pl.pallas_call(
        final_kernel,
        grid_spec=pltpu.PrefetchScalarGridSpec(
            num_scalar_prefetch=1,
            grid=(width // rows,),
            in_specs=pair * CHAINS + [pl.BlockSpec(memory_space=pl.ANY)] * len(before),
            out_specs=[
                pl.BlockSpec((rows, vocab // 2), lambda i, pick: (i, column(pick))),
                pl.BlockSpec((1, vocab // 2), lambda i, pick: (0, column(pick))),
            ],
        ),
        out_shape=[
            jax.ShapeDtypeStruct((width, vocab), F32), jax.ShapeDtypeStruct((1, vocab), F32)
        ],
        input_output_aliases={1 + 2 * CHAINS + k: k for k in range(len(before))},
        compiler_params=params(8),
    )(pick, *[s for source in sources for s in (source, source)], *before)


def whole(shape):
    return pl.BlockSpec(shape, lambda *_: (0,) * len(shape))


SMEM_SPEC = pl.BlockSpec(memory_space=pltpu.SMEM)


def forward(tlen, labels, enc, pred, w, bias, rows, begin, blocks, before):
    frames, width = enc.shape
    tok_slots = pred.shape[0]
    vocab = w.shape[1]
    cells = frames * tok_slots
    return pl.pallas_call(
        functools.partial(forward_kernel, begin),
        grid=(blocks,),
        in_specs=[
            SMEM_SPEC, whole(labels.shape), whole(enc.shape), whole(pred.shape),
            whole(w.shape), whole(bias.shape),
        ] + [pl.BlockSpec(memory_space=pl.ANY)] * len(before),
        out_specs=[
            pl.BlockSpec((rows, vocab), lambda i: (i + begin, 0)),
            pl.BlockSpec((8, rows), lambda i: (0, i + begin)),
            pl.BlockSpec((width, rows), lambda i: (0, i + begin)),
        ],
        out_shape=[
            jax.ShapeDtypeStruct((cells, vocab), F32),
            jax.ShapeDtypeStruct((8, cells), F32),
            jax.ShapeDtypeStruct((width, cells), BF16),
        ],
        scratch_shapes=[pltpu.VMEM((frames, width), F32), pltpu.VMEM((2, SUB, vocab), F32)],
        input_output_aliases={6 + k: k for k in range(len(before))},
        compiler_params=params(16),
    )(tlen, in_vmem(labels), in_vmem(enc), in_vmem(pred), in_vmem(w), in_vmem(bias), *before)


def gradients(pick, flen, tlen, labels, qa, qb, e, st, jt, rows):
    cells, vocab = e.shape
    width = jt.shape[0]
    part = vocab // 2
    blocks = cells // rows

    def at(i):
        return jnp.minimum(i, blocks - 1)

    smem = pl.BlockSpec(memory_space=pltpu.SMEM)
    grid_spec = pltpu.PrefetchScalarGridSpec(
        num_scalar_prefetch=1,
        grid=(blocks + 1,),
        in_specs=[
            smem, smem, whole(labels.shape),
            pl.BlockSpec((1, 3, rows), lambda i, pick: (lax.rem(pick[0], pick[1]), 0, at(i))),
            pl.BlockSpec((1, 3, rows), lambda i, pick: (lax.rem(pick[0], pick[1]), 0, at(i))),
            pl.BlockSpec((rows, vocab), lambda i, pick: (at(i), 0)),
            pl.BlockSpec((8, rows), lambda i, pick: (0, at(i))),
            pl.BlockSpec((width, rows), lambda i, pick: (0, jnp.maximum(i - 1, 0))),
        ],
        out_specs=[
            pl.BlockSpec((rows, vocab), lambda i, pick: (at(i), 0)),
            whole((1, 1)),
            whole((width + EXTRA, part)),
            whole((width + EXTRA, part)),
        ],
        scratch_shapes=[
            pltpu.VMEM((rows, vocab), BF16),
            pltpu.VMEM((rows, vocab), BF16),
            pltpu.VMEM((width, vocab), F32),
            pltpu.VMEM((8, vocab), F32),
            pltpu.VMEM((1, rows), F32),
            pltpu.VMEM((rows, LANES), jnp.int32),
        ],
    )
    return pl.pallas_call(
        functools.partial(grad_kernel, blocks),
        grid_spec=grid_spec,
        out_shape=[
            pltpu.HBM((cells, vocab), BF16),
            jax.ShapeDtypeStruct((1, 1), F32),
            jax.ShapeDtypeStruct((width + EXTRA, part), BF16),
            jax.ShapeDtypeStruct((width + EXTRA, part), F32),
        ],
        compiler_params=params(20),
    )(pick, flen, tlen, in_vmem(labels), qa, qb, e, st, jt)


def input_gradients(enc, pred, d_low, w, rows, begin, last, before):
    frames, width = enc.shape
    vocab = d_low.shape[1]
    cells = frames // 2 * pred.shape[0]
    half = (frames // 2, width)
    extra = () if not before else (before[1], before[0])
    return pl.pallas_call(
        functools.partial(input_kernel, begin, last),
        grid=(cells // rows,),
        in_specs=[
            whole(enc.shape), whole(pred.shape),
            pl.BlockSpec((rows, vocab), lambda i: (i + begin, 0)), whole(w.shape),
        ] + ([whole(pred.shape), pl.BlockSpec(memory_space=pl.ANY)] if before else []),
        out_specs=[pl.BlockSpec(half, lambda i: (1 if last else 0, 0)), whole(pred.shape)],
        out_shape=[
            jax.ShapeDtypeStruct(enc.shape, BF16),
            jax.ShapeDtypeStruct(pred.shape, BF16 if last else F32),
        ],
        scratch_shapes=[
            pltpu.VMEM(enc.shape, F32), pltpu.VMEM(half, F32), pltpu.VMEM(pred.shape, F32)
        ],
        input_output_aliases={5: 0} if before else {},
        compiler_params=params(12),
    )(in_vmem(enc), in_vmem(pred), pltpu.with_memory_space_constraint(d_low, pltpu.HBM), in_vmem(w), *extra)


def merge_kernel(even, odd, keep_ref, got_ref, acc_ref, send_ref, bias_ref):
    own = lax.axis_index("dp")
    mask = jnp.where((own & 1) == 0, even, odd)
    side = jnp.where((own & mask) != 0, 1, 0)
    count, part = acc_ref.shape
    stay = pl.ds(pl.multiple_of(side * count, count), count)
    leave = pl.ds(pl.multiple_of((1 - side) * count, count), count)
    send_ref[:count, :] = (keep_ref[leave, :] + got_ref[leave, :].astype(F32)).astype(BF16)
    acc_ref[...] = keep_ref[stay, :] + got_ref[stay, :].astype(F32)
    rows = got_ref[2 * count :, :].astype(F32)
    bias = keep_ref[2 * count : 2 * count + 1, :] + rows[0:1] + rows[1:2]
    high = bias.astype(BF16).astype(F32)
    low = (bias - high).astype(BF16).astype(F32)
    bias_ref[...] = high + low
    place = lax.broadcasted_iota(jnp.int32, (EXTRA, part), 0)
    packed = jnp.where(place == 0, high, jnp.where(place == 1, low, 0.0))
    send_ref[count:, :] = packed.astype(BF16)


def merge(keep, got, even, odd):
    rows, part = got.shape
    count = (rows - EXTRA) // 2
    return pl.pallas_call(
        functools.partial(merge_kernel, even, odd),
        grid=(1,),
        in_specs=[whole(keep.shape), whole(got.shape)],
        out_specs=[whole((count, part)), whole((count + EXTRA, part)), whole((1, part))],
        out_shape=[
            jax.ShapeDtypeStruct((count, part), F32),
            jax.ShapeDtypeStruct((count + EXTRA, part), BF16),
            jax.ShapeDtypeStruct((1, part), F32),
        ],
        compiler_params=params(12),
    )(keep, got)


def split_two(value):
    high = lax.reduce_precision(value, 8, 7)
    return high, lax.reduce_precision(value - high, 8, 7)


def on_device(
    dp, teacher_post, assignment, encoder_out, predictor_out, frame_lengths, token_lengths,
    labels, out_weight, out_bias,
):
    own = lax.axis_index("dp")
    core = own & 1
    masks = [1 << k for k in range(dp.bit_length() - 1)]
    tok_slots = predictor_out.shape[1]
    rows = 16 * tok_slots
    width, vocab = out_weight.shape
    part = vocab // 2

    def exchange(value, even, odd):
        pairs = [(k, k ^ (odd if k & 1 else even)) for k in range(dp)]
        return lax.ppermute(value, "dp", pairs)

    blocks = encoder_out.shape[1] * tok_slots // rows
    quarter = blocks // 4
    shares = [(0, quarter), (quarter, quarter), (2 * quarter, blocks - 2 * quarter)]
    held, made = teacher_post, ()
    staged = stage(
        assignment, out_weight, encoder_out[0], predictor_out[0], out_bias.reshape(1, vocab), labels,
        teacher_post,
    )
    for k, mask in enumerate(masks):
        got = exchange(held, mask, mask)
        part_no = k - (len(masks) - len(shares))
        if part_no >= 0:
            begin, number = shares[part_no]
            made = tuple(forward(
                token_lengths, label_row, enc, pred, weight, bias_row, rows, begin, number, made
            ))
        if k == 0:
            got, staged = lax.optimization_barrier((got, staged))
            held = staged[5]
        if k < len(masks) - 1:
            held = jnp.concatenate([held, got], axis=0)
            held, made, staged = lax.optimization_barrier((held, made, staged))
            weight, enc, pred, bias_row, label_row, _, pick = staged
    far = got
    e, st, jt = made
    d_low, loss, send, keep = gradients(
        pick, frame_lengths, token_lengths, label_row, held, far, e, st, jt, rows
    )
    got = exchange(send, 1, 1)

    def got_bias(rows_of):
        return rows_of[0:1].astype(F32) + rows_of[1:2].astype(F32)

    def bias_rows(high, low):
        filler = jnp.zeros((EXTRA - 2, high.shape[1]), BF16)
        return jnp.concatenate([high.astype(BF16), low.astype(BF16), filler], axis=0)

    rest = masks[1:]
    even_order = rest
    odd_order = rest[1:2] + rest[:1] + rest[2:]
    orders = list(zip(even_order, odd_order))
    sides = []
    count = width
    done = ()
    acc, send, bias = merge(keep, got, *orders[0])
    for k, (even, odd) in enumerate(orders[:-1]):
        side = (own & jnp.where(core == 0, even, odd)) != 0
        sides.append(side)
        count //= 2
        if k:
            high, low = split_two(bias)
            top, bottom = acc[:count], acc[count:]
            send = jnp.where(side, top, bottom).astype(BF16)
            acc = jnp.where(side, bottom, top)
            send = jnp.concatenate([send, bias_rows(high, low)], axis=0)
            bias = high + low
        if k < 2:
            send, acc, d_low = lax.optimization_barrier((send, acc, d_low))
        got = exchange(send, even, odd)
        if k < 2:
            done = input_gradients(
                enc, pred, d_low, weight, rows, k * (blocks // 2), k == 1, done
            )
            got, done = lax.optimization_barrier((got, done))
        acc = acc + got[:count].astype(F32)
        bias = bias + got_bias(got[count:])
    chains = range(CHAINS)
    span = part // CHAINS
    even, odd = orders[-1]
    sums, kept, parts = [], [], []
    for c in chains:
        cols = slice(c * span, (c + 1) * span)
        high, low = split_two(bias[:, cols])
        sums.append((high, low))
        sent = acc[:, cols].astype(BF16)
        kept.append(lax.reduce_precision(acc[:, cols], 8, 7))
        parts.append(exchange(jnp.concatenate([sent, bias_rows(high, low)], axis=0), even, odd))
    have = []
    for c in chains:
        got = parts[c]
        if c:
            got, have = lax.optimization_barrier((got, have))
        have.append((kept[c] + got[:count].astype(F32)).astype(BF16))
        high, low = sums[c]
        sums[c] = split_two((high + low) + got_bias(got[count:]))
    for (even, odd), side in list(zip(orders, sides))[::-1]:
        parts = [exchange(have[c], even, odd) for c in chains]
        joined = []
        for c in chains:
            if c:
                parts[c], joined = lax.optimization_barrier((parts[c], joined))
            joined.append(jnp.where(
                side,
                jnp.concatenate([parts[c], have[c]], axis=0),
                jnp.concatenate([have[c], parts[c]], axis=0),
            ))
        have = joined
    sent = [jnp.concatenate([have[c], bias_rows(*sums[c])], axis=0) for c in chains]
    others = [exchange(sent[c], 1, 1) for c in chains]
    result = tuple(widen(pick, sent, width, vocab, True, ()))
    others, result = lax.optimization_barrier((others, result))
    result = tuple(widen(pick, others, width, vocab, False, result))
    grad_weight, grad_bias = result
    return (loss.reshape(1), grad_weight, grad_bias.reshape(vocab), done[0][None], done[1][None])


def solution(mesh):
    in_specs = (
        P(("groups", "dp"), None, None),
        P("groups"),
        P(("groups", "dp"), None, None),
        P(("groups", "dp"), None, None),
        P(("groups", "dp")),
        P(("groups", "dp")),
        P(("groups", "dp"), None),
        P(),
        P(),
    )
    out_specs = (
        P(("groups", "dp")),
        P("groups", None),
        P("groups"),
        P(("groups", "dp"), None, None),
        P(("groups", "dp"), None, None),
    )
    return jax.shard_map(
        functools.partial(on_device, mesh.shape["dp"]),
        mesh=mesh, in_specs=in_specs, out_specs=out_specs, check_vma=False,
    )
```

```python
import functools

import jax
import jax.numpy as jnp
from jax import lax
from jax.experimental import pallas as pl
from jax.experimental.pallas import tpu as pltpu
from jax.sharding import PartitionSpec as P

F32 = jnp.float32
BF16 = jnp.bfloat16
LANES = 128
EXTRA = 16
CHAINS = 2


def params(mib):
    return pltpu.CompilerParams(
        dimension_semantics=("arbitrary",), vmem_limit_bytes=mib * 1024 * 1024
    )


def target_column(labels_ref, token_len, tok_slots, reps):
    tok = labels_ref.shape[1]
    row = lax.broadcasted_iota(jnp.int32, (tok_slots, tok), 0)
    lane = lax.broadcasted_iota(jnp.int32, (tok_slots, tok), 1)
    picked = jnp.where(row == lane, labels_ref[...].astype(F32), 0.0)
    column = jnp.sum(picked, axis=1, keepdims=True)
    token = lax.broadcasted_iota(jnp.int32, (tok_slots, 1), 0)
    column = jnp.where(token < token_len, column, -1.0).astype(jnp.int32)
    whole = jnp.broadcast_to(column[None], (reps, tok_slots, 1))
    return whole.reshape(reps * tok_slots, 1)


def stage_kernel(assignment_ref, *refs):
    count = (len(refs) - 3) // 2
    sources, targets = refs[:count], refs[count : 2 * count]
    pick_ref, order_ref, sems = refs[2 * count :]
    copies = [
        pltpu.make_async_copy(source, target, sems.at[k])
        for k, (source, target) in enumerate(
            zip((assignment_ref, *sources), (order_ref, *targets))
        )
    ]
    for copy in copies:
        copy.start()
    own = lax.axis_index("dp")
    copies[0].wait()
    pick_ref[0] = order_ref[own] ^ own
    pick_ref[1] = assignment_ref.shape[0] // 2
    pick_ref[2] = own & 1
    for copy in copies[1:]:
        copy.wait()


def stage(assignment, *arrays):
    anywhere = pl.BlockSpec(memory_space=pl.ANY)
    smem = pl.BlockSpec(memory_space=pltpu.SMEM)
    return pl.pallas_call(
        stage_kernel,
        in_specs=[anywhere] * (1 + len(arrays)),
        out_specs=[anywhere] * len(arrays) + [smem],
        out_shape=[jax.ShapeDtypeStruct(x.shape, x.dtype) for x in arrays]
        + [jax.ShapeDtypeStruct((3,), jnp.int32)],
        scratch_shapes=[
            pltpu.SMEM(assignment.shape, jnp.int32), pltpu.SemaphoreType.DMA((1 + len(arrays),))
        ],
        compiler_params=pltpu.CompilerParams(vmem_limit_bytes=4 * 1024 * 1024),
    )(*[pltpu.with_memory_space_constraint(x, pltpu.HBM) for x in (assignment, *arrays)])


def in_vmem(x):
    return x


SUB = 256


def forward_kernel(begin, tlen_ref, labels_ref, enc_ref, pred_ref, w_ref, b_ref, *refs):
    e_ref, st_ref, jt_ref, enc_scr, logit_scr = refs[-5:]
    step = pl.program_id(0)
    rows, vocab = e_ref.shape
    tok_slots, width = pred_ref.shape
    block_frames = rows // tok_slots

    @pl.when(step == 0)
    def _():
        enc_scr[...] = enc_ref[...].astype(F32)

    first = pl.multiple_of((begin + step) * block_frames, block_frames)
    enc = enc_scr[pl.ds(first, block_frames), :]
    pred = pred_ref[...].astype(F32)
    sub_frames = SUB // tok_slots
    target = target_column(labels_ref, tlen_ref[0], tok_slots, sub_frames)
    lane = lax.broadcasted_iota(jnp.int32, (SUB, LANES), 1)
    parts = rows // SUB

    def multiply(k):
        place = slice(k * SUB, (k + 1) * SUB)
        act = jnp.tanh(enc[k * sub_frames : (k + 1) * sub_frames, None, :] + pred[None, :, :])
        joint_in = act.reshape(SUB, width).astype(BF16)
        jt_ref[:, place] = joint_in.T
        logit_scr[k % 2] = jnp.dot(joint_in, w_ref[...], preferred_element_type=F32)

    def collapse(k):
        place = slice(k * SUB, (k + 1) * SUB)
        tops = jnp.full((SUB, LANES), -jnp.inf, F32)
        for j in range(vocab // LANES):
            cols = slice(j * LANES, (j + 1) * LANES)
            tops = jnp.maximum(tops, logit_scr[k % 2, :, cols] + b_ref[:, cols])
        row_max = jnp.max(tops, axis=1, keepdims=True)
        rest_acc = jnp.zeros((SUB, LANES), F32)
        label_acc = jnp.zeros((SUB, LANES), F32)
        for j in range(vocab // LANES):
            cols = slice(j * LANES, (j + 1) * LANES)
            shifted = logit_scr[k % 2, :, cols] + b_ref[:, cols] - row_max
            e = jnp.exp(shifted)
            e_ref[place, cols] = e
            hot = lane == target - j * LANES
            rest = jnp.where(hot, 0.0, e)
            if j == 0:
                z_blank = shifted[:, 0:1]
                rest = jnp.where(lane == 0, 0.0, rest)
            rest_acc = rest_acc + rest
            label_acc = label_acc + jnp.where(hot, shifted, 0.0)
        rest_sum = jnp.sum(rest_acc, axis=1, keepdims=True)
        z_label = jnp.sum(label_acc, axis=1, keepdims=True)
        packed = jnp.where(lane == 0, rest_sum, jnp.where(lane == 1, z_blank, z_label))
        st_ref[:, place] = packed.T[:8]

    multiply(0)
    for k in range(parts):
        if k + 1 < parts:
            multiply(k + 1)
        collapse(k)


def grad_kernel(
    blocks, pick_ref, flen_ref, tlen_ref, labels_ref, qa_ref, qb_ref, e_ref, st_ref, jt_ref,
    d_ref, loss_ref, send_ref, keep_ref, low_scr, high_scr, dw_scr, gb_scr, loss_scr, target_scr,
):
    step = pl.program_id(0)
    steps = pl.num_programs(0)
    rows, vocab = e_ref.shape
    tok_slots = labels_ref.shape[1] + 1
    block_frames = rows // tok_slots
    width = jt_ref.shape[0]
    frame_len, token_len = flen_ref[0], tlen_ref[0]

    @pl.when(step == 0)
    def _():
        gb_scr[...] = jnp.zeros_like(gb_scr)
        loss_scr[...] = jnp.zeros_like(loss_scr)
        column = target_column(labels_ref, token_len, tok_slots, block_frames)
        target_scr[...] = jnp.broadcast_to(column, (rows, LANES))

    def collapse(held_ref):
        half_count = pick_ref[1]
        q = jnp.where(pick_ref[0] < half_count, qa_ref[0].astype(F32), qb_ref[0].astype(F32))
        cell = lax.broadcasted_iota(jnp.int32, (1, rows), 1)
        frame = lax.div(cell, tok_slots) + step * block_frames
        token = lax.rem(cell, tok_slots)
        has_label = token < token_len
        count = jnp.full((1, rows), frame_len * (token_len + 1), jnp.int32).astype(F32)
        weight = jnp.where((frame < frame_len) & (token <= token_len), 1.0 / count, 0.0)
        q_blank = q[0:1]
        q_label = jnp.where(has_label, q[1:2], 0.0)
        q_rest = q[2:3]
        rest_sum = st_ref[0:1]
        z_blank = st_ref[1:2]
        z_label = st_ref[2:3]
        e_blank = jnp.exp(z_blank)
        e_label = jnp.exp(z_label)
        total = rest_sum + e_blank + jnp.where(has_label, e_label, 0.0)
        log_total = jnp.log(total)
        cell_loss = -(
            q_blank * (z_blank - log_total)
            + q_label * (z_label - log_total)
            + q_rest * (jnp.log(rest_sum) - log_total)
        )
        loss_scr[...] += cell_loss * weight
        soft = weight * (q_blank + q_label + q_rest) / total
        scale = soft - weight * q_rest / rest_sum
        d_blank = soft * e_blank - weight * q_blank
        d_label = soft * e_label - weight * q_label
        place = lax.broadcasted_iota(jnp.int32, (8, rows), 0)
        packed = jnp.where(place == 0, scale, jnp.where(place == 1, d_label, d_blank))
        columns = packed.T
        scale = jnp.broadcast_to(columns[:, 0:1], (rows, LANES))
        d_label = jnp.broadcast_to(columns[:, 1:2], (rows, LANES))
        lane = lax.broadcasted_iota(jnp.int32, (rows, LANES), 1)
        for j in range(vocab // LANES):
            cols = slice(j * LANES, (j + 1) * LANES)
            d = jnp.where(lane + j * LANES == target_scr[...], d_label, e_ref[:, cols] * scale)
            if j == 0:
                d = jnp.where(lane == 0, columns[:, 2:3], d)
            low = d.astype(BF16)
            d_ref[:, cols] = low
            held_ref[:, cols] = low
            gb_scr[:, cols] += jnp.sum(d.reshape(rows // 8, 8, LANES), axis=0)

    slots = (low_scr, high_scr)
    last_ref = slots[(blocks - 1) % 2]

    @pl.when(step == 0)
    def _():
        collapse(slots[0])

    for block in range(1, blocks):

        @pl.when(step == block)
        def _(block=block):
            dw = jnp.dot(jt_ref[...], slots[(block - 1) % 2][...], preferred_element_type=F32)
            dw_scr[...] = dw if block == 1 else dw_scr[...] + dw
            collapse(slots[block % 2])

    @pl.when(step == steps - 1)
    def _():
        loss_ref[...] = jnp.sum(loss_scr[...], axis=1, keepdims=True)
        part = vocab // 2
        core = pick_ref[2]
        col = pl.multiple_of((1 - core) * part, part)
        dw = dw_scr[:, pl.ds(col, part)] + jnp.dot(
            jt_ref[...], last_ref[:, pl.ds(col, part)], preferred_element_type=F32
        )
        send_ref[:width, :] = dw.astype(BF16)
        col = pl.multiple_of(core * part, part)
        keep_ref[:width, :] = dw_scr[:, pl.ds(col, part)] + jnp.dot(
            jt_ref[...], last_ref[:, pl.ds(col, part)], preferred_element_type=F32
        )
        bias = jnp.sum(gb_scr[...], axis=0, keepdims=True)
        first, second = bias[:, :part], bias[:, part:]
        mine = jnp.where(core == 0, first, second)
        other = jnp.where(core == 0, second, first)
        keep_ref[width:, :] = jnp.broadcast_to(mine, (EXTRA, part))
        high = other.astype(BF16)
        low = (other - high.astype(F32)).astype(BF16)
        place = lax.broadcasted_iota(jnp.int32, (EXTRA, part), 0)
        packed = jnp.where(place == 0, high.astype(F32), jnp.where(place == 1, low.astype(F32), 0.0))
        send_ref[width:, :] = packed.astype(BF16)


def input_kernel(begin, last, enc_ref, pred_ref, d_ref, w_ref, *refs):
    ge_ref, gp_ref, enc_scr, ge_scr, gp_scr = refs[-5:]
    step = pl.program_id(0)
    steps = pl.num_programs(0)
    rows = d_ref.shape[0]
    tok_slots, width = pred_ref.shape
    block_frames = rows // tok_slots

    @pl.when(step == 0)
    def _():
        enc_scr[...] = enc_ref[...].astype(F32)
        gp_scr[...] = jnp.zeros_like(gp_scr) if begin == 0 else refs[0][...]

    first = pl.multiple_of(step * block_frames, block_frames)
    d_hidden = lax.dot_general(
        d_ref[...], w_ref[...], (((1,), (1,)), ((), ())), preferred_element_type=F32
    )
    enc = enc_scr[pl.ds(begin * block_frames + first, block_frames), :]
    act = jnp.tanh(enc[:, None, :] + pred_ref[...].astype(F32)[None, :, :])
    d_pre = d_hidden.reshape(block_frames, tok_slots, width) * (1.0 - act * act)
    ge_scr[pl.ds(first, block_frames), :] = jnp.sum(d_pre, axis=1)
    gp_scr[...] += jnp.sum(d_pre, axis=0)

    @pl.when(step == steps - 1)
    def _():
        ge_ref[...] = ge_scr[...].astype(BF16)
        gp_ref[...] = gp_scr[...].astype(gp_ref.dtype)


PIECES = 4


def final_kernel(mine, *refs):
    sources = refs[:CHAINS]
    out_ref, bias_ref, wide, bias_wide, sems = refs[-5:]
    width, part = wide.shape
    core = lax.axis_index("dp") & 1
    cols = pl.ds(pl.multiple_of((core if mine else 1 - core) * part, part), part)
    span = part // CHAINS
    size = width // PIECES
    copies = []
    for c, source in enumerate(sources):
        extra = source[width:, :].astype(F32)
        bias_wide[:, c * span : (c + 1) * span] = extra[0:1] + extra[1:2]
    copies.append(pltpu.make_async_copy(bias_wide, bias_ref.at[:, cols], sems.at[PIECES]))
    copies[0].start()
    for p in range(PIECES):
        rows = slice(p * size, (p + 1) * size)
        for c, source in enumerate(sources):
            wide[rows, c * span : (c + 1) * span] = source[rows, :].astype(F32)
        copies.append(
            pltpu.make_async_copy(wide.at[rows], out_ref.at[rows, cols], sems.at[p])
        )
        copies[-1].start()
    for copy in copies:
        copy.wait()


def widen(sources, width, vocab, mine, before):
    part = vocab // 2
    anywhere = pl.BlockSpec(memory_space=pl.ANY)
    return pl.pallas_call(
        functools.partial(final_kernel, mine),
        in_specs=[pl.BlockSpec(memory_space=pltpu.VMEM)] * CHAINS + [anywhere] * len(before),
        out_specs=[anywhere, anywhere],
        out_shape=[
            pltpu.HBM((width, vocab), F32), pltpu.HBM((1, vocab), F32)
        ],
        scratch_shapes=[
            pltpu.VMEM((width, part), F32), pltpu.VMEM((1, part), F32),
            pltpu.SemaphoreType.DMA((PIECES + 1,)),
        ],
        input_output_aliases={CHAINS + k: k for k in range(len(before))},
        compiler_params=pltpu.CompilerParams(vmem_limit_bytes=8 * 1024 * 1024),
    )(*sources, *before)


def whole(shape):
    return pl.BlockSpec(shape, lambda *_: (0,) * len(shape))


SMEM_SPEC = pl.BlockSpec(memory_space=pltpu.SMEM)


def forward(tlen, labels, enc, pred, w, bias, rows, begin, blocks, before):
    frames, width = enc.shape
    tok_slots = pred.shape[0]
    vocab = w.shape[1]
    cells = frames * tok_slots
    return pl.pallas_call(
        functools.partial(forward_kernel, begin),
        grid=(blocks,),
        in_specs=[
            SMEM_SPEC, whole(labels.shape), whole(enc.shape), whole(pred.shape),
            whole(w.shape), whole(bias.shape),
        ] + [pl.BlockSpec(memory_space=pl.ANY)] * len(before),
        out_specs=[
            pl.BlockSpec((rows, vocab), lambda i: (i + begin, 0)),
            pl.BlockSpec((8, rows), lambda i: (0, i + begin)),
            pl.BlockSpec((width, rows), lambda i: (0, i + begin)),
        ],
        out_shape=[
            jax.ShapeDtypeStruct((cells, vocab), F32),
            jax.ShapeDtypeStruct((8, cells), F32),
            jax.ShapeDtypeStruct((width, cells), BF16),
        ],
        scratch_shapes=[pltpu.VMEM((frames, width), F32), pltpu.VMEM((2, SUB, vocab), F32)],
        input_output_aliases={6 + k: k for k in range(len(before))},
        compiler_params=params(16),
    )(tlen, in_vmem(labels), in_vmem(enc), in_vmem(pred), in_vmem(w), in_vmem(bias), *before)


def gradients(pick, flen, tlen, labels, qa, qb, e, st, jt, rows):
    cells, vocab = e.shape
    width = jt.shape[0]
    part = vocab // 2
    blocks = cells // rows

    def at(i):
        return jnp.minimum(i, blocks - 1)

    smem = pl.BlockSpec(memory_space=pltpu.SMEM)
    grid_spec = pltpu.PrefetchScalarGridSpec(
        num_scalar_prefetch=1,
        grid=(blocks + 1,),
        in_specs=[
            smem, smem, whole(labels.shape),
            pl.BlockSpec((1, 3, rows), lambda i, pick: (lax.rem(pick[0], pick[1]), 0, at(i))),
            pl.BlockSpec((1, 3, rows), lambda i, pick: (lax.rem(pick[0], pick[1]), 0, at(i))),
            pl.BlockSpec((rows, vocab), lambda i, pick: (at(i), 0)),
            pl.BlockSpec((8, rows), lambda i, pick: (0, at(i))),
            pl.BlockSpec((width, rows), lambda i, pick: (0, jnp.maximum(i - 1, 0))),
        ],
        out_specs=[
            pl.BlockSpec((rows, vocab), lambda i, pick: (at(i), 0)),
            whole((1, 1)),
            whole((width + EXTRA, part)),
            whole((width + EXTRA, part)),
        ],
        scratch_shapes=[
            pltpu.VMEM((rows, vocab), BF16),
            pltpu.VMEM((rows, vocab), BF16),
            pltpu.VMEM((width, vocab), F32),
            pltpu.VMEM((8, vocab), F32),
            pltpu.VMEM((1, rows), F32),
            pltpu.VMEM((rows, LANES), jnp.int32),
        ],
    )
    return pl.pallas_call(
        functools.partial(grad_kernel, blocks),
        grid_spec=grid_spec,
        out_shape=[
            pltpu.HBM((cells, vocab), BF16),
            jax.ShapeDtypeStruct((1, 1), F32),
            jax.ShapeDtypeStruct((width + EXTRA, part), BF16),
            jax.ShapeDtypeStruct((width + EXTRA, part), F32),
        ],
        compiler_params=params(20),
    )(pick, flen, tlen, in_vmem(labels), qa, qb, e, st, jt)


def input_gradients(enc, pred, d_low, w, rows, begin, last, before):
    frames, width = enc.shape
    vocab = d_low.shape[1]
    cells = frames // 2 * pred.shape[0]
    half = (frames // 2, width)
    extra = () if not before else (before[1], before[0])
    return pl.pallas_call(
        functools.partial(input_kernel, begin, last),
        grid=(cells // rows,),
        in_specs=[
            whole(enc.shape), whole(pred.shape),
            pl.BlockSpec((rows, vocab), lambda i: (i + begin, 0)), whole(w.shape),
        ] + ([whole(pred.shape), pl.BlockSpec(memory_space=pl.ANY)] if before else []),
        out_specs=[pl.BlockSpec(half, lambda i: (1 if last else 0, 0)), whole(pred.shape)],
        out_shape=[
            jax.ShapeDtypeStruct(enc.shape, BF16),
            jax.ShapeDtypeStruct(pred.shape, BF16 if last else F32),
        ],
        scratch_shapes=[
            pltpu.VMEM(enc.shape, F32), pltpu.VMEM(half, F32), pltpu.VMEM(pred.shape, F32)
        ],
        input_output_aliases={5: 0} if before else {},
        compiler_params=params(12),
    )(in_vmem(enc), in_vmem(pred), pltpu.with_memory_space_constraint(d_low, pltpu.HBM), in_vmem(w), *extra)


def merge_kernel(even, odd, keep_ref, got_ref, acc_ref, send_ref, bias_ref):
    own = lax.axis_index("dp")
    mask = jnp.where((own & 1) == 0, even, odd)
    side = jnp.where((own & mask) != 0, 1, 0)
    count, part = acc_ref.shape
    stay = pl.ds(pl.multiple_of(side * count, count), count)
    leave = pl.ds(pl.multiple_of((1 - side) * count, count), count)
    send_ref[:count, :] = (keep_ref[leave, :] + got_ref[leave, :].astype(F32)).astype(BF16)
    acc_ref[...] = keep_ref[stay, :] + got_ref[stay, :].astype(F32)
    rows = got_ref[2 * count :, :].astype(F32)
    bias = keep_ref[2 * count : 2 * count + 1, :] + rows[0:1] + rows[1:2]
    high = bias.astype(BF16).astype(F32)
    low = (bias - high).astype(BF16).astype(F32)
    bias_ref[...] = high + low
    place = lax.broadcasted_iota(jnp.int32, (EXTRA, part), 0)
    packed = jnp.where(place == 0, high, jnp.where(place == 1, low, 0.0))
    send_ref[count:, :] = packed.astype(BF16)


def merge(keep, got, even, odd):
    rows, part = got.shape
    count = (rows - EXTRA) // 2
    return pl.pallas_call(
        functools.partial(merge_kernel, even, odd),
        grid=(1,),
        in_specs=[whole(keep.shape), whole(got.shape)],
        out_specs=[whole((count, part)), whole((count + EXTRA, part)), whole((1, part))],
        out_shape=[
            jax.ShapeDtypeStruct((count, part), F32),
            jax.ShapeDtypeStruct((count + EXTRA, part), BF16),
            jax.ShapeDtypeStruct((1, part), F32),
        ],
        compiler_params=params(12),
    )(keep, got)


def split_two(value):
    high = lax.reduce_precision(value, 8, 7)
    return high, lax.reduce_precision(value - high, 8, 7)


def on_device(
    dp, teacher_post, assignment, encoder_out, predictor_out, frame_lengths, token_lengths,
    labels, out_weight, out_bias,
):
    own = lax.axis_index("dp")
    core = own & 1
    masks = [1 << k for k in range(dp.bit_length() - 1)]
    tok_slots = predictor_out.shape[1]
    rows = 16 * tok_slots
    width, vocab = out_weight.shape
    part = vocab // 2

    def exchange(value, even, odd):
        pairs = [(k, k ^ (odd if k & 1 else even)) for k in range(dp)]
        return lax.ppermute(value, "dp", pairs)

    blocks = encoder_out.shape[1] * tok_slots // rows
    quarter = blocks // 4
    shares = [(0, quarter), (quarter, quarter), (2 * quarter, blocks - 2 * quarter)]
    held, made = teacher_post, ()
    staged = stage(
        assignment, out_weight, encoder_out[0], predictor_out[0], out_bias.reshape(1, vocab), labels,
        teacher_post,
    )
    for k, mask in enumerate(masks):
        got = exchange(held, mask, mask)
        part_no = k - (len(masks) - len(shares))
        if part_no >= 0:
            begin, number = shares[part_no]
            made = tuple(forward(
                token_lengths, label_row, enc, pred, weight, bias_row, rows, begin, number, made
            ))
        if k == 0:
            got, staged = lax.optimization_barrier((got, staged))
            held = staged[5]
        if k < len(masks) - 1:
            held = jnp.concatenate([held, got], axis=0)
            held, made, staged = lax.optimization_barrier((held, made, staged))
            weight, enc, pred, bias_row, label_row, _, pick = staged
    far = got
    e, st, jt = made
    d_low, loss, send, keep = gradients(
        pick, frame_lengths, token_lengths, label_row, held, far, e, st, jt, rows
    )
    got = exchange(send, 1, 1)

    def got_bias(rows_of):
        return rows_of[0:1].astype(F32) + rows_of[1:2].astype(F32)

    def bias_rows(high, low):
        filler = jnp.zeros((EXTRA - 2, high.shape[1]), BF16)
        return jnp.concatenate([high.astype(BF16), low.astype(BF16), filler], axis=0)

    rest = masks[1:]
    even_order = rest
    odd_order = rest[1:2] + rest[:1] + rest[2:]
    orders = list(zip(even_order, odd_order))
    sides = []
    count = width
    done = ()
    acc, send, bias = merge(keep, got, *orders[0])
    for k, (even, odd) in enumerate(orders[:-1]):
        side = (own & jnp.where(core == 0, even, odd)) != 0
        sides.append(side)
        count //= 2
        if k:
            high, low = split_two(bias)
            top, bottom = acc[:count], acc[count:]
            send = jnp.where(side, top, bottom).astype(BF16)
            acc = jnp.where(side, bottom, top)
            send = jnp.concatenate([send, bias_rows(high, low)], axis=0)
            bias = high + low
        if k < 2:
            send, acc, d_low = lax.optimization_barrier((send, acc, d_low))
        got = exchange(send, even, odd)
        if k < 2:
            done = input_gradients(
                enc, pred, d_low, weight, rows, k * (blocks // 2), k == 1, done
            )
            got, done = lax.optimization_barrier((got, done))
        acc = acc + got[:count].astype(F32)
        bias = bias + got_bias(got[count:])
    chains = range(CHAINS)
    span = part // CHAINS
    even, odd = orders[-1]
    sums, kept, parts = [], [], []
    for c in chains:
        cols = slice(c * span, (c + 1) * span)
        high, low = split_two(bias[:, cols])
        sums.append((high, low))
        sent = acc[:, cols].astype(BF16)
        kept.append(lax.reduce_precision(acc[:, cols], 8, 7))
        parts.append(exchange(jnp.concatenate([sent, bias_rows(high, low)], axis=0), even, odd))
    have = []
    for c in chains:
        got = parts[c]
        if c:
            got, have = lax.optimization_barrier((got, have))
        have.append((kept[c] + got[:count].astype(F32)).astype(BF16))
        high, low = sums[c]
        sums[c] = split_two((high + low) + got_bias(got[count:]))
    for (even, odd), side in list(zip(orders, sides))[::-1]:
        parts = [exchange(have[c], even, odd) for c in chains]
        joined = []
        for c in chains:
            if c:
                parts[c], joined = lax.optimization_barrier((parts[c], joined))
            joined.append(jnp.where(
                side,
                jnp.concatenate([parts[c], have[c]], axis=0),
                jnp.concatenate([have[c], parts[c]], axis=0),
            ))
        have = joined
    sent = [jnp.concatenate([have[c], bias_rows(*sums[c])], axis=0) for c in chains]
    others = [exchange(sent[c], 1, 1) for c in chains]
    result = tuple(widen(sent, width, vocab, True, ()))
    others, result = lax.optimization_barrier((others, result))
    result = tuple(widen(others, width, vocab, False, result))
    grad_weight, grad_bias = result
    return (loss.reshape(1), grad_weight, grad_bias.reshape(vocab), done[0][None], done[1][None])


def solution(mesh):
    in_specs = (
        P(("groups", "dp"), None, None),
        P("groups"),
        P(("groups", "dp"), None, None),
        P(("groups", "dp"), None, None),
        P(("groups", "dp")),
        P(("groups", "dp")),
        P(("groups", "dp"), None),
        P(),
        P(),
    )
    out_specs = (
        P(("groups", "dp")),
        P("groups", None),
        P("groups"),
        P(("groups", "dp"), None, None),
        P(("groups", "dp"), None, None),
    )
    return jax.shard_map(
        functools.partial(on_device, mesh.shape["dp"]),
        mesh=mesh, in_specs=in_specs, out_specs=out_specs, check_vma=False,
    )
```

```python
import functools

import jax
import jax.numpy as jnp
from jax import lax
from jax.experimental import pallas as pl
from jax.experimental.pallas import tpu as pltpu
from jax.sharding import PartitionSpec as P

F32 = jnp.float32
BF16 = jnp.bfloat16
LANES = 128
EXTRA = 16
CHAINS = 2


def params(mib):
    return pltpu.CompilerParams(
        dimension_semantics=("arbitrary",), vmem_limit_bytes=mib * 1024 * 1024
    )


def target_column(labels_ref, token_len, tok_slots, reps):
    tok = labels_ref.shape[1]
    row = lax.broadcasted_iota(jnp.int32, (tok_slots, tok), 0)
    lane = lax.broadcasted_iota(jnp.int32, (tok_slots, tok), 1)
    picked = jnp.where(row == lane, labels_ref[...].astype(F32), 0.0)
    column = jnp.sum(picked, axis=1, keepdims=True)
    token = lax.broadcasted_iota(jnp.int32, (tok_slots, 1), 0)
    column = jnp.where(token < token_len, column, -1.0).astype(jnp.int32)
    whole = jnp.broadcast_to(column[None], (reps, tok_slots, 1))
    return whole.reshape(reps * tok_slots, 1)


def stage_kernel(assignment_ref, *refs):
    count = (len(refs) - 3) // 2
    sources, targets = refs[:count], refs[count : 2 * count]
    pick_ref, order_ref, sems = refs[2 * count :]
    copies = [
        pltpu.make_async_copy(source, target, sems.at[k])
        for k, (source, target) in enumerate(
            zip((assignment_ref, *sources), (order_ref, *targets))
        )
    ]
    for copy in copies:
        copy.start()
    own = lax.axis_index("dp")
    copies[0].wait()
    pick_ref[0] = order_ref[own] ^ own
    pick_ref[1] = assignment_ref.shape[0] // 2
    pick_ref[2] = own & 1
    for copy in copies[1:]:
        copy.wait()


def stage(assignment, *arrays):
    anywhere = pl.BlockSpec(memory_space=pl.ANY)
    smem = pl.BlockSpec(memory_space=pltpu.SMEM)
    return pl.pallas_call(
        stage_kernel,
        in_specs=[anywhere] * (1 + len(arrays)),
        out_specs=[anywhere] * len(arrays) + [smem],
        out_shape=[jax.ShapeDtypeStruct(x.shape, x.dtype) for x in arrays]
        + [jax.ShapeDtypeStruct((3,), jnp.int32)],
        scratch_shapes=[
            pltpu.SMEM(assignment.shape, jnp.int32), pltpu.SemaphoreType.DMA((1 + len(arrays),))
        ],
        compiler_params=pltpu.CompilerParams(vmem_limit_bytes=4 * 1024 * 1024),
    )(*[pltpu.with_memory_space_constraint(x, pltpu.HBM) for x in (assignment, *arrays)])


def in_vmem(x):
    return x


SUB = 256


def forward_kernel(begin, tlen_ref, labels_ref, enc_ref, pred_ref, w_ref, b_ref, *refs):
    e_ref, st_ref, jt_ref, enc_scr, logit_scr = refs[-5:]
    step = pl.program_id(0)
    rows, vocab = e_ref.shape
    tok_slots, width = pred_ref.shape
    block_frames = rows // tok_slots

    @pl.when(step == 0)
    def _():
        enc_scr[...] = enc_ref[...].astype(F32)

    first = pl.multiple_of((begin + step) * block_frames, block_frames)
    enc = enc_scr[pl.ds(first, block_frames), :]
    pred = pred_ref[...].astype(F32)
    sub_frames = SUB // tok_slots
    target = target_column(labels_ref, tlen_ref[0], tok_slots, sub_frames)
    lane = lax.broadcasted_iota(jnp.int32, (SUB, LANES), 1)
    parts = rows // SUB

    def multiply(k):
        place = slice(k * SUB, (k + 1) * SUB)
        act = jnp.tanh(enc[k * sub_frames : (k + 1) * sub_frames, None, :] + pred[None, :, :])
        joint_in = act.reshape(SUB, width).astype(BF16)
        jt_ref[:, place] = joint_in.T
        logit_scr[k % 2] = jnp.dot(joint_in, w_ref[...], preferred_element_type=F32)

    def collapse(k):
        place = slice(k * SUB, (k + 1) * SUB)
        tops = jnp.full((SUB, LANES), -jnp.inf, F32)
        for j in range(vocab // LANES):
            cols = slice(j * LANES, (j + 1) * LANES)
            tops = jnp.maximum(tops, logit_scr[k % 2, :, cols] + b_ref[:, cols])
        row_max = jnp.max(tops, axis=1, keepdims=True)
        rest_acc = jnp.zeros((SUB, LANES), F32)
        label_acc = jnp.zeros((SUB, LANES), F32)
        for j in range(vocab // LANES):
            cols = slice(j * LANES, (j + 1) * LANES)
            shifted = logit_scr[k % 2, :, cols] + b_ref[:, cols] - row_max
            e = jnp.exp(shifted)
            e_ref[place, cols] = e
            hot = lane == target - j * LANES
            rest = jnp.where(hot, 0.0, e)
            if j == 0:
                z_blank = shifted[:, 0:1]
                rest = jnp.where(lane == 0, 0.0, rest)
            rest_acc = rest_acc + rest
            label_acc = label_acc + jnp.where(hot, shifted, 0.0)
        rest_sum = jnp.sum(rest_acc, axis=1, keepdims=True)
        z_label = jnp.sum(label_acc, axis=1, keepdims=True)
        packed = jnp.where(lane == 0, rest_sum, jnp.where(lane == 1, z_blank, z_label))
        st_ref[:, place] = packed.T[:8]

    multiply(0)
    for k in range(parts):
        if k + 1 < parts:
            multiply(k + 1)
        collapse(k)


def grad_kernel(
    blocks, pick_ref, flen_ref, tlen_ref, labels_ref, qa_ref, qb_ref, e_ref, st_ref, jt_ref,
    d_ref, loss_ref, send_ref, keep_ref, low_scr, high_scr, dw_scr, gb_scr, loss_scr, target_scr,
):
    step = pl.program_id(0)
    steps = pl.num_programs(0)
    rows, vocab = e_ref.shape
    tok_slots = labels_ref.shape[1] + 1
    block_frames = rows // tok_slots
    width = jt_ref.shape[0]
    frame_len, token_len = flen_ref[0], tlen_ref[0]

    @pl.when(step == 0)
    def _():
        gb_scr[...] = jnp.zeros_like(gb_scr)
        loss_scr[...] = jnp.zeros_like(loss_scr)
        column = target_column(labels_ref, token_len, tok_slots, block_frames)
        target_scr[...] = column - lax.broadcasted_iota(jnp.int32, (rows, LANES), 1)

    def collapse(held_ref):
        half_count = pick_ref[1]
        q = jnp.where(pick_ref[0] < half_count, qa_ref[0].astype(F32), qb_ref[0].astype(F32))
        cell = lax.broadcasted_iota(jnp.int32, (1, rows), 1)
        frame = lax.div(cell, tok_slots) + step * block_frames
        token = lax.rem(cell, tok_slots)
        has_label = token < token_len
        count = jnp.full((1, rows), frame_len * (token_len + 1), jnp.int32).astype(F32)
        weight = jnp.where((frame < frame_len) & (token <= token_len), 1.0 / count, 0.0)
        q_blank = q[0:1]
        q_label = jnp.where(has_label, q[1:2], 0.0)
        q_rest = q[2:3]
        rest_sum = st_ref[0:1]
        z_blank = st_ref[1:2]
        z_label = st_ref[2:3]
        e_blank = jnp.exp(z_blank)
        e_label = jnp.exp(z_label)
        total = rest_sum + e_blank + jnp.where(has_label, e_label, 0.0)
        log_total = jnp.log(total)
        cell_loss = -(
            q_blank * (z_blank - log_total)
            + q_label * (z_label - log_total)
            + q_rest * (jnp.log(rest_sum) - log_total)
        )
        loss_scr[...] += cell_loss * weight
        soft = weight * (q_blank + q_label + q_rest) / total
        scale = soft - weight * q_rest / rest_sum
        d_blank = soft * e_blank - weight * q_blank
        d_label = soft * e_label - weight * q_label
        place = lax.broadcasted_iota(jnp.int32, (8, rows), 0)
        packed = jnp.where(place == 0, scale, jnp.where(place == 1, d_label, d_blank))
        columns = packed.T
        scale = jnp.broadcast_to(columns[:, 0:1], (rows, LANES))
        d_label = jnp.broadcast_to(columns[:, 1:2], (rows, LANES))
        lane = lax.broadcasted_iota(jnp.int32, (rows, LANES), 1)
        for j in range(vocab // LANES):
            cols = slice(j * LANES, (j + 1) * LANES)
            d = jnp.where(target_scr[...] == j * LANES, d_label, e_ref[:, cols] * scale)
            if j == 0:
                d = jnp.where(lane == 0, columns[:, 2:3], d)
            low = d.astype(BF16)
            d_ref[:, cols] = low
            held_ref[:, cols] = low
            gb_scr[:, cols] += jnp.sum(d.reshape(rows // 8, 8, LANES), axis=0)

    slots = (low_scr, high_scr)
    last_ref = slots[(blocks - 1) % 2]

    @pl.when(step == 0)
    def _():
        collapse(slots[0])

    for block in range(1, blocks):

        @pl.when(step == block)
        def _(block=block):
            dw = jnp.dot(jt_ref[...], slots[(block - 1) % 2][...], preferred_element_type=F32)
            dw_scr[...] = dw if block == 1 else dw_scr[...] + dw
            collapse(slots[block % 2])

    @pl.when(step == steps - 1)
    def _():
        loss_ref[...] = jnp.sum(loss_scr[...], axis=1, keepdims=True)
        part = vocab // 2
        core = pick_ref[2]
        col = pl.multiple_of((1 - core) * part, part)
        dw = dw_scr[:, pl.ds(col, part)] + jnp.dot(
            jt_ref[...], last_ref[:, pl.ds(col, part)], preferred_element_type=F32
        )
        send_ref[:width, :] = dw.astype(BF16)
        col = pl.multiple_of(core * part, part)
        keep_ref[:width, :] = dw_scr[:, pl.ds(col, part)] + jnp.dot(
            jt_ref[...], last_ref[:, pl.ds(col, part)], preferred_element_type=F32
        )
        bias = jnp.sum(gb_scr[...], axis=0, keepdims=True)
        first, second = bias[:, :part], bias[:, part:]
        mine = jnp.where(core == 0, first, second)
        other = jnp.where(core == 0, second, first)
        keep_ref[width:, :] = jnp.broadcast_to(mine, (EXTRA, part))
        high = other.astype(BF16)
        low = (other - high.astype(F32)).astype(BF16)
        place = lax.broadcasted_iota(jnp.int32, (EXTRA, part), 0)
        packed = jnp.where(place == 0, high.astype(F32), jnp.where(place == 1, low.astype(F32), 0.0))
        send_ref[width:, :] = packed.astype(BF16)


def input_kernel(begin, last, enc_ref, pred_ref, d_ref, w_ref, *refs):
    ge_ref, gp_ref, enc_scr, ge_scr, gp_scr = refs[-5:]
    step = pl.program_id(0)
    steps = pl.num_programs(0)
    rows = d_ref.shape[0]
    tok_slots, width = pred_ref.shape
    block_frames = rows // tok_slots

    @pl.when(step == 0)
    def _():
        enc_scr[...] = enc_ref[...].astype(F32)
        gp_scr[...] = jnp.zeros_like(gp_scr) if begin == 0 else refs[0][...]

    first = pl.multiple_of(step * block_frames, block_frames)
    d_hidden = lax.dot_general(
        d_ref[...], w_ref[...], (((1,), (1,)), ((), ())), preferred_element_type=F32
    )
    enc = enc_scr[pl.ds(begin * block_frames + first, block_frames), :]
    act = jnp.tanh(enc[:, None, :] + pred_ref[...].astype(F32)[None, :, :])
    d_pre = d_hidden.reshape(block_frames, tok_slots, width) * (1.0 - act * act)
    ge_scr[pl.ds(first, block_frames), :] = jnp.sum(d_pre, axis=1)
    gp_scr[...] += jnp.sum(d_pre, axis=0)

    @pl.when(step == steps - 1)
    def _():
        ge_ref[...] = ge_scr[...].astype(BF16)
        gp_ref[...] = gp_scr[...].astype(gp_ref.dtype)


PIECES = 4


def final_kernel(mine, *refs):
    sources = refs[:CHAINS]
    out_ref, bias_ref, wide, bias_wide, sems = refs[-5:]
    width, part = wide.shape
    core = lax.axis_index("dp") & 1
    cols = pl.ds(pl.multiple_of((core if mine else 1 - core) * part, part), part)
    span = part // CHAINS
    size = width // PIECES
    copies = []
    for c, source in enumerate(sources):
        extra = source[width:, :].astype(F32)
        bias_wide[:, c * span : (c + 1) * span] = extra[0:1] + extra[1:2]
    copies.append(pltpu.make_async_copy(bias_wide, bias_ref.at[:, cols], sems.at[PIECES]))
    copies[0].start()
    for p in range(PIECES):
        rows = slice(p * size, (p + 1) * size)
        for c, source in enumerate(sources):
            wide[rows, c * span : (c + 1) * span] = source[rows, :].astype(F32)
        copies.append(
            pltpu.make_async_copy(wide.at[rows], out_ref.at[rows, cols], sems.at[p])
        )
        copies[-1].start()
    for copy in copies:
        copy.wait()


def widen(sources, width, vocab, mine, before):
    part = vocab // 2
    anywhere = pl.BlockSpec(memory_space=pl.ANY)
    return pl.pallas_call(
        functools.partial(final_kernel, mine),
        in_specs=[pl.BlockSpec(memory_space=pltpu.VMEM)] * CHAINS + [anywhere] * len(before),
        out_specs=[anywhere, anywhere],
        out_shape=[
            pltpu.HBM((width, vocab), F32), pltpu.HBM((1, vocab), F32)
        ],
        scratch_shapes=[
            pltpu.VMEM((width, part), F32), pltpu.VMEM((1, part), F32),
            pltpu.SemaphoreType.DMA((PIECES + 1,)),
        ],
        input_output_aliases={CHAINS + k: k for k in range(len(before))},
        compiler_params=pltpu.CompilerParams(vmem_limit_bytes=8 * 1024 * 1024),
    )(*sources, *before)


def whole(shape):
    return pl.BlockSpec(shape, lambda *_: (0,) * len(shape))


SMEM_SPEC = pl.BlockSpec(memory_space=pltpu.SMEM)


def forward(tlen, labels, enc, pred, w, bias, rows, begin, blocks, before):
    frames, width = enc.shape
    tok_slots = pred.shape[0]
    vocab = w.shape[1]
    cells = frames * tok_slots
    return pl.pallas_call(
        functools.partial(forward_kernel, begin),
        grid=(blocks,),
        in_specs=[
            SMEM_SPEC, whole(labels.shape), whole(enc.shape), whole(pred.shape),
            whole(w.shape), whole(bias.shape),
        ] + [pl.BlockSpec(memory_space=pl.ANY)] * len(before),
        out_specs=[
            pl.BlockSpec((rows, vocab), lambda i: (i + begin, 0)),
            pl.BlockSpec((8, rows), lambda i: (0, i + begin)),
            pl.BlockSpec((width, rows), lambda i: (0, i + begin)),
        ],
        out_shape=[
            jax.ShapeDtypeStruct((cells, vocab), F32),
            jax.ShapeDtypeStruct((8, cells), F32),
            jax.ShapeDtypeStruct((width, cells), BF16),
        ],
        scratch_shapes=[pltpu.VMEM((frames, width), F32), pltpu.VMEM((2, SUB, vocab), F32)],
        input_output_aliases={6 + k: k for k in range(len(before))},
        compiler_params=params(16),
    )(tlen, in_vmem(labels), in_vmem(enc), in_vmem(pred), in_vmem(w), in_vmem(bias), *before)


def gradients(pick, flen, tlen, labels, qa, qb, e, st, jt, rows):
    cells, vocab = e.shape
    width = jt.shape[0]
    part = vocab // 2
    blocks = cells // rows

    def at(i):
        return jnp.minimum(i, blocks - 1)

    smem = pl.BlockSpec(memory_space=pltpu.SMEM)
    grid_spec = pltpu.PrefetchScalarGridSpec(
        num_scalar_prefetch=1,
        grid=(blocks + 1,),
        in_specs=[
            smem, smem, whole(labels.shape),
            pl.BlockSpec((1, 3, rows), lambda i, pick: (lax.rem(pick[0], pick[1]), 0, at(i))),
            pl.BlockSpec((1, 3, rows), lambda i, pick: (lax.rem(pick[0], pick[1]), 0, at(i))),
            pl.BlockSpec((rows, vocab), lambda i, pick: (at(i), 0)),
            pl.BlockSpec((8, rows), lambda i, pick: (0, at(i))),
            pl.BlockSpec((width, rows), lambda i, pick: (0, jnp.maximum(i - 1, 0))),
        ],
        out_specs=[
            pl.BlockSpec((rows, vocab), lambda i, pick: (at(i), 0)),
            whole((1, 1)),
            whole((width + EXTRA, part)),
            whole((width + EXTRA, part)),
        ],
        scratch_shapes=[
            pltpu.VMEM((rows, vocab), BF16),
            pltpu.VMEM((rows, vocab), BF16),
            pltpu.VMEM((width, vocab), F32),
            pltpu.VMEM((8, vocab), F32),
            pltpu.VMEM((1, rows), F32),
            pltpu.VMEM((rows, LANES), jnp.int32),
        ],
    )
    return pl.pallas_call(
        functools.partial(grad_kernel, blocks),
        grid_spec=grid_spec,
        out_shape=[
            pltpu.HBM((cells, vocab), BF16),
            jax.ShapeDtypeStruct((1, 1), F32),
            jax.ShapeDtypeStruct((width + EXTRA, part), BF16),
            jax.ShapeDtypeStruct((width + EXTRA, part), F32),
        ],
        compiler_params=params(20),
    )(pick, flen, tlen, in_vmem(labels), qa, qb, e, st, jt)


def input_gradients(enc, pred, d_low, w, rows, begin, last, before):
    frames, width = enc.shape
    vocab = d_low.shape[1]
    cells = frames // 2 * pred.shape[0]
    half = (frames // 2, width)
    extra = () if not before else (before[1], before[0])
    return pl.pallas_call(
        functools.partial(input_kernel, begin, last),
        grid=(cells // rows,),
        in_specs=[
            whole(enc.shape), whole(pred.shape),
            pl.BlockSpec((rows, vocab), lambda i: (i + begin, 0)), whole(w.shape),
        ] + ([whole(pred.shape), pl.BlockSpec(memory_space=pl.ANY)] if before else []),
        out_specs=[pl.BlockSpec(half, lambda i: (1 if last else 0, 0)), whole(pred.shape)],
        out_shape=[
            jax.ShapeDtypeStruct(enc.shape, BF16),
            jax.ShapeDtypeStruct(pred.shape, BF16 if last else F32),
        ],
        scratch_shapes=[
            pltpu.VMEM(enc.shape, F32), pltpu.VMEM(half, F32), pltpu.VMEM(pred.shape, F32)
        ],
        input_output_aliases={5: 0} if before else {},
        compiler_params=params(12),
    )(in_vmem(enc), in_vmem(pred), pltpu.with_memory_space_constraint(d_low, pltpu.HBM), in_vmem(w), *extra)


def merge_kernel(even, odd, keep_ref, got_ref, acc_ref, send_ref, bias_ref):
    own = lax.axis_index("dp")
    mask = jnp.where((own & 1) == 0, even, odd)
    side = jnp.where((own & mask) != 0, 1, 0)
    count, part = acc_ref.shape
    stay = pl.ds(pl.multiple_of(side * count, count), count)
    leave = pl.ds(pl.multiple_of((1 - side) * count, count), count)
    send_ref[:count, :] = (keep_ref[leave, :] + got_ref[leave, :].astype(F32)).astype(BF16)
    acc_ref[...] = keep_ref[stay, :] + got_ref[stay, :].astype(F32)
    rows = got_ref[2 * count :, :].astype(F32)
    bias = keep_ref[2 * count : 2 * count + 1, :] + rows[0:1] + rows[1:2]
    high = bias.astype(BF16).astype(F32)
    low = (bias - high).astype(BF16).astype(F32)
    bias_ref[...] = high + low
    place = lax.broadcasted_iota(jnp.int32, (EXTRA, part), 0)
    packed = jnp.where(place == 0, high, jnp.where(place == 1, low, 0.0))
    send_ref[count:, :] = packed.astype(BF16)


def merge(keep, got, even, odd):
    rows, part = got.shape
    count = (rows - EXTRA) // 2
    return pl.pallas_call(
        functools.partial(merge_kernel, even, odd),
        grid=(1,),
        in_specs=[whole(keep.shape), whole(got.shape)],
        out_specs=[whole((count, part)), whole((count + EXTRA, part)), whole((1, part))],
        out_shape=[
            jax.ShapeDtypeStruct((count, part), F32),
            jax.ShapeDtypeStruct((count + EXTRA, part), BF16),
            jax.ShapeDtypeStruct((1, part), F32),
        ],
        compiler_params=params(12),
    )(keep, got)


def split_two(value):
    high = lax.reduce_precision(value, 8, 7)
    return high, lax.reduce_precision(value - high, 8, 7)


def on_device(
    dp, teacher_post, assignment, encoder_out, predictor_out, frame_lengths, token_lengths,
    labels, out_weight, out_bias,
):
    own = lax.axis_index("dp")
    core = own & 1
    masks = [1 << k for k in range(dp.bit_length() - 1)]
    tok_slots = predictor_out.shape[1]
    rows = 16 * tok_slots
    width, vocab = out_weight.shape
    part = vocab // 2

    def exchange(value, even, odd):
        pairs = [(k, k ^ (odd if k & 1 else even)) for k in range(dp)]
        return lax.ppermute(value, "dp", pairs)

    blocks = encoder_out.shape[1] * tok_slots // rows
    quarter = blocks // 4
    shares = [(0, quarter), (quarter, quarter), (2 * quarter, blocks - 2 * quarter)]
    held, made = teacher_post, ()
    staged = stage(
        assignment, out_weight, encoder_out[0], predictor_out[0], out_bias.reshape(1, vocab), labels,
        teacher_post,
    )
    for k, mask in enumerate(masks):
        got = exchange(held, mask, mask)
        part_no = k - (len(masks) - len(shares))
        if part_no >= 0:
            begin, number = shares[part_no]
            made = tuple(forward(
                token_lengths, label_row, enc, pred, weight, bias_row, rows, begin, number, made
            ))
        if k == 0:
            got, staged = lax.optimization_barrier((got, staged))
            held = staged[5]
        if k < len(masks) - 1:
            held = jnp.concatenate([held, got], axis=0)
            held, made, staged = lax.optimization_barrier((held, made, staged))
            weight, enc, pred, bias_row, label_row, _, pick = staged
    far = got
    e, st, jt = made
    d_low, loss, send, keep = gradients(
        pick, frame_lengths, token_lengths, label_row, held, far, e, st, jt, rows
    )
    got = exchange(send, 1, 1)

    def got_bias(rows_of):
        return rows_of[0:1].astype(F32) + rows_of[1:2].astype(F32)

    def bias_rows(high, low):
        filler = jnp.zeros((EXTRA - 2, high.shape[1]), BF16)
        return jnp.concatenate([high.astype(BF16), low.astype(BF16), filler], axis=0)

    rest = masks[1:]
    even_order = rest
    odd_order = rest[1:2] + rest[:1] + rest[2:]
    orders = list(zip(even_order, odd_order))
    sides = []
    count = width
    done = ()
    acc, send, bias = merge(keep, got, *orders[0])
    for k, (even, odd) in enumerate(orders[:-1]):
        side = (own & jnp.where(core == 0, even, odd)) != 0
        sides.append(side)
        count //= 2
        if k:
            high, low = split_two(bias)
            top, bottom = acc[:count], acc[count:]
            send = jnp.where(side, top, bottom).astype(BF16)
            acc = jnp.where(side, bottom, top)
            send = jnp.concatenate([send, bias_rows(high, low)], axis=0)
            bias = high + low
        if k < 2:
            send, acc, d_low = lax.optimization_barrier((send, acc, d_low))
        got = exchange(send, even, odd)
        if k < 2:
            done = input_gradients(
                enc, pred, d_low, weight, rows, k * (blocks // 2), k == 1, done
            )
            got, done = lax.optimization_barrier((got, done))
        acc = acc + got[:count].astype(F32)
        bias = bias + got_bias(got[count:])
    chains = range(CHAINS)
    span = part // CHAINS
    even, odd = orders[-1]
    sums, kept, parts = [], [], []
    for c in chains:
        cols = slice(c * span, (c + 1) * span)
        high, low = split_two(bias[:, cols])
        sums.append((high, low))
        sent = acc[:, cols].astype(BF16)
        kept.append(lax.reduce_precision(acc[:, cols], 8, 7))
        parts.append(exchange(jnp.concatenate([sent, bias_rows(high, low)], axis=0), even, odd))
    have = []
    for c in chains:
        got = parts[c]
        if c:
            got, have = lax.optimization_barrier((got, have))
        have.append((kept[c] + got[:count].astype(F32)).astype(BF16))
        high, low = sums[c]
        sums[c] = split_two((high + low) + got_bias(got[count:]))
    for (even, odd), side in list(zip(orders, sides))[::-1]:
        parts = [exchange(have[c], even, odd) for c in chains]
        joined = []
        for c in chains:
            if c:
                parts[c], joined = lax.optimization_barrier((parts[c], joined))
            joined.append(jnp.where(
                side,
                jnp.concatenate([parts[c], have[c]], axis=0),
                jnp.concatenate([have[c], parts[c]], axis=0),
            ))
        have = joined
    sent = [jnp.concatenate([have[c], bias_rows(*sums[c])], axis=0) for c in chains]
    others = [exchange(sent[c], 1, 1) for c in chains]
    result = tuple(widen(sent, width, vocab, True, ()))
    others, result = lax.optimization_barrier((others, result))
    result = tuple(widen(others, width, vocab, False, result))
    grad_weight, grad_bias = result
    return (loss.reshape(1), grad_weight, grad_bias.reshape(vocab), done[0][None], done[1][None])


def solution(mesh):
    in_specs = (
        P(("groups", "dp"), None, None),
        P("groups"),
        P(("groups", "dp"), None, None),
        P(("groups", "dp"), None, None),
        P(("groups", "dp")),
        P(("groups", "dp")),
        P(("groups", "dp"), None),
        P(),
        P(),
    )
    out_specs = (
        P(("groups", "dp")),
        P("groups", None),
        P("groups"),
        P(("groups", "dp"), None, None),
        P(("groups", "dp"), None, None),
    )
    return jax.shard_map(
        functools.partial(on_device, mesh.shape["dp"]),
        mesh=mesh, in_specs=in_specs, out_specs=out_specs, check_vma=False,
    )
```

```python
import functools

import jax
import jax.numpy as jnp
from jax import lax
from jax.experimental import pallas as pl
from jax.experimental.pallas import tpu as pltpu
from jax.sharding import PartitionSpec as P

F32 = jnp.float32
BF16 = jnp.bfloat16
LANES = 128
EXTRA = 16
CHAINS = 2


def params(mib):
    return pltpu.CompilerParams(
        dimension_semantics=("arbitrary",), vmem_limit_bytes=mib * 1024 * 1024
    )


def target_column(labels_ref, token_len, tok_slots, reps):
    tok = labels_ref.shape[1]
    row = lax.broadcasted_iota(jnp.int32, (tok_slots, tok), 0)
    lane = lax.broadcasted_iota(jnp.int32, (tok_slots, tok), 1)
    picked = jnp.where(row == lane, labels_ref[...].astype(F32), 0.0)
    column = jnp.sum(picked, axis=1, keepdims=True)
    token = lax.broadcasted_iota(jnp.int32, (tok_slots, 1), 0)
    column = jnp.where(token < token_len, column, -1.0).astype(jnp.int32)
    whole = jnp.broadcast_to(column[None], (reps, tok_slots, 1))
    return whole.reshape(reps * tok_slots, 1)


def stage_kernel(assignment_ref, *refs):
    count = (len(refs) - 3) // 2
    sources, targets = refs[:count], refs[count : 2 * count]
    pick_ref, order_ref, sems = refs[2 * count :]
    copies = [
        pltpu.make_async_copy(source, target, sems.at[k])
        for k, (source, target) in enumerate(
            zip((assignment_ref, *sources), (order_ref, *targets))
        )
    ]
    for copy in copies:
        copy.start()
    own = lax.axis_index("dp")
    copies[0].wait()
    pick_ref[0] = order_ref[own] ^ own
    pick_ref[1] = assignment_ref.shape[0] // 2
    pick_ref[2] = own & 1
    for copy in copies[1:]:
        copy.wait()


def stage(assignment, *arrays):
    anywhere = pl.BlockSpec(memory_space=pl.ANY)
    smem = pl.BlockSpec(memory_space=pltpu.SMEM)
    return pl.pallas_call(
        stage_kernel,
        in_specs=[anywhere] * (1 + len(arrays)),
        out_specs=[anywhere] * len(arrays) + [smem],
        out_shape=[jax.ShapeDtypeStruct(x.shape, x.dtype) for x in arrays]
        + [jax.ShapeDtypeStruct((3,), jnp.int32)],
        scratch_shapes=[
            pltpu.SMEM(assignment.shape, jnp.int32), pltpu.SemaphoreType.DMA((1 + len(arrays),))
        ],
        compiler_params=pltpu.CompilerParams(vmem_limit_bytes=4 * 1024 * 1024),
    )(*[pltpu.with_memory_space_constraint(x, pltpu.HBM) for x in (assignment, *arrays)])


def in_vmem(x):
    return x


SUB = 256


def forward_kernel(begin, tlen_ref, labels_ref, enc_ref, pred_ref, w_ref, b_ref, *refs):
    e_ref, st_ref, jt_ref, enc_scr, logit_scr = refs[-5:]
    step = pl.program_id(0)
    rows, vocab = e_ref.shape
    tok_slots, width = pred_ref.shape
    block_frames = rows // tok_slots

    @pl.when(step == 0)
    def _():
        enc_scr[...] = enc_ref[...].astype(F32)

    first = pl.multiple_of((begin + step) * block_frames, block_frames)
    enc = enc_scr[pl.ds(first, block_frames), :]
    pred = pred_ref[...].astype(F32)
    sub_frames = SUB // tok_slots
    target = target_column(labels_ref, tlen_ref[0], tok_slots, sub_frames)
    lane = lax.broadcasted_iota(jnp.int32, (SUB, LANES), 1)
    offset = target - lane
    parts = rows // SUB

    def multiply(k):
        place = slice(k * SUB, (k + 1) * SUB)
        act = jnp.tanh(enc[k * sub_frames : (k + 1) * sub_frames, None, :] + pred[None, :, :])
        joint_in = act.reshape(SUB, width).astype(BF16)
        jt_ref[:, place] = joint_in.T
        logit_scr[k % 2] = jnp.dot(joint_in, w_ref[...], preferred_element_type=F32)

    def collapse(k):
        place = slice(k * SUB, (k + 1) * SUB)
        tops = jnp.full((SUB, LANES), -jnp.inf, F32)
        for j in range(vocab // LANES):
            cols = slice(j * LANES, (j + 1) * LANES)
            tops = jnp.maximum(tops, logit_scr[k % 2, :, cols] + b_ref[:, cols])
        row_max = jnp.max(tops, axis=1, keepdims=True)
        rest_acc = jnp.zeros((SUB, LANES), F32)
        label_acc = jnp.zeros((SUB, LANES), F32)
        for j in range(vocab // LANES):
            cols = slice(j * LANES, (j + 1) * LANES)
            shifted = logit_scr[k % 2, :, cols] + b_ref[:, cols] - row_max
            e = jnp.exp(shifted)
            e_ref[place, cols] = e
            hot = offset == j * LANES
            rest = jnp.where(hot, 0.0, e)
            if j == 0:
                z_blank = shifted[:, 0:1]
                rest = jnp.where(lane == 0, 0.0, rest)
            rest_acc = rest_acc + rest
            label_acc = jnp.where(hot, shifted, label_acc)
        rest_sum = jnp.sum(rest_acc, axis=1, keepdims=True)
        z_label = jnp.sum(label_acc, axis=1, keepdims=True)
        packed = jnp.where(lane == 0, rest_sum, jnp.where(lane == 1, z_blank, z_label))
        st_ref[:, place] = packed.T[:8]

    multiply(0)
    for k in range(parts):
        if k + 1 < parts:
            multiply(k + 1)
        collapse(k)


def grad_kernel(
    blocks, pick_ref, flen_ref, tlen_ref, labels_ref, qa_ref, qb_ref, e_ref, st_ref, jt_ref,
    d_ref, loss_ref, send_ref, keep_ref, low_scr, high_scr, dw_scr, gb_scr, loss_scr, target_scr,
):
    step = pl.program_id(0)
    steps = pl.num_programs(0)
    rows, vocab = e_ref.shape
    tok_slots = labels_ref.shape[1] + 1
    block_frames = rows // tok_slots
    width = jt_ref.shape[0]
    frame_len, token_len = flen_ref[0], tlen_ref[0]

    @pl.when(step == 0)
    def _():
        gb_scr[...] = jnp.zeros_like(gb_scr)
        loss_scr[...] = jnp.zeros_like(loss_scr)
        column = target_column(labels_ref, token_len, tok_slots, block_frames)
        target_scr[...] = column - lax.broadcasted_iota(jnp.int32, (rows, LANES), 1)

    def collapse(held_ref):
        half_count = pick_ref[1]
        q = jnp.where(pick_ref[0] < half_count, qa_ref[0].astype(F32), qb_ref[0].astype(F32))
        cell = lax.broadcasted_iota(jnp.int32, (1, rows), 1)
        frame = lax.div(cell, tok_slots) + step * block_frames
        token = lax.rem(cell, tok_slots)
        has_label = token < token_len
        count = jnp.full((1, rows), frame_len * (token_len + 1), jnp.int32).astype(F32)
        weight = jnp.where((frame < frame_len) & (token <= token_len), 1.0 / count, 0.0)
        q_blank = q[0:1]
        q_label = jnp.where(has_label, q[1:2], 0.0)
        q_rest = q[2:3]
        rest_sum = st_ref[0:1]
        z_blank = st_ref[1:2]
        z_label = st_ref[2:3]
        e_blank = jnp.exp(z_blank)
        e_label = jnp.exp(z_label)
        total = rest_sum + e_blank + jnp.where(has_label, e_label, 0.0)
        log_total = jnp.log(total)
        cell_loss = -(
            q_blank * (z_blank - log_total)
            + q_label * (z_label - log_total)
            + q_rest * (jnp.log(rest_sum) - log_total)
        )
        loss_scr[...] += cell_loss * weight
        soft = weight * (q_blank + q_label + q_rest) / total
        scale = soft - weight * q_rest / rest_sum
        d_blank = soft * e_blank - weight * q_blank
        d_label = soft * e_label - weight * q_label
        place = lax.broadcasted_iota(jnp.int32, (8, rows), 0)
        packed = jnp.where(place == 0, scale, jnp.where(place == 1, d_label, d_blank))
        columns = packed.T
        scale = jnp.broadcast_to(columns[:, 0:1], (rows, LANES))
        d_label = jnp.broadcast_to(columns[:, 1:2], (rows, LANES))
        lane = lax.broadcasted_iota(jnp.int32, (rows, LANES), 1)
        for j in range(vocab // LANES):
            cols = slice(j * LANES, (j + 1) * LANES)
            d = jnp.where(target_scr[...] == j * LANES, d_label, e_ref[:, cols] * scale)
            if j == 0:
                d = jnp.where(lane == 0, columns[:, 2:3], d)
            low = d.astype(BF16)
            d_ref[:, cols] = low
            held_ref[:, cols] = low
            gb_scr[:, cols] += jnp.sum(d.reshape(rows // 8, 8, LANES), axis=0)

    slots = (low_scr, high_scr)
    last_ref = slots[(blocks - 1) % 2]

    @pl.when(step == 0)
    def _():
        collapse(slots[0])

    for block in range(1, blocks):

        @pl.when(step == block)
        def _(block=block):
            dw = jnp.dot(jt_ref[...], slots[(block - 1) % 2][...], preferred_element_type=F32)
            dw_scr[...] = dw if block == 1 else dw_scr[...] + dw
            collapse(slots[block % 2])

    @pl.when(step == steps - 1)
    def _():
        loss_ref[...] = jnp.sum(loss_scr[...], axis=1, keepdims=True)
        part = vocab // 2
        core = pick_ref[2]
        col = pl.multiple_of((1 - core) * part, part)
        dw = dw_scr[:, pl.ds(col, part)] + jnp.dot(
            jt_ref[...], last_ref[:, pl.ds(col, part)], preferred_element_type=F32
        )
        send_ref[:width, :] = dw.astype(BF16)
        col = pl.multiple_of(core * part, part)
        keep_ref[:width, :] = dw_scr[:, pl.ds(col, part)] + jnp.dot(
            jt_ref[...], last_ref[:, pl.ds(col, part)], preferred_element_type=F32
        )
        bias = jnp.sum(gb_scr[...], axis=0, keepdims=True)
        first, second = bias[:, :part], bias[:, part:]
        mine = jnp.where(core == 0, first, second)
        other = jnp.where(core == 0, second, first)
        keep_ref[width:, :] = jnp.broadcast_to(mine, (EXTRA, part))
        high = other.astype(BF16)
        low = (other - high.astype(F32)).astype(BF16)
        place = lax.broadcasted_iota(jnp.int32, (EXTRA, part), 0)
        packed = jnp.where(place == 0, high.astype(F32), jnp.where(place == 1, low.astype(F32), 0.0))
        send_ref[width:, :] = packed.astype(BF16)


def input_kernel(begin, last, enc_ref, pred_ref, d_ref, w_ref, *refs):
    ge_ref, gp_ref, enc_scr, ge_scr, gp_scr = refs[-5:]
    step = pl.program_id(0)
    steps = pl.num_programs(0)
    rows = d_ref.shape[0]
    tok_slots, width = pred_ref.shape
    block_frames = rows // tok_slots

    @pl.when(step == 0)
    def _():
        enc_scr[...] = enc_ref[...].astype(F32)
        gp_scr[...] = jnp.zeros_like(gp_scr) if begin == 0 else refs[0][...]

    first = pl.multiple_of(step * block_frames, block_frames)
    d_hidden = lax.dot_general(
        d_ref[...], w_ref[...], (((1,), (1,)), ((), ())), preferred_element_type=F32
    )
    enc = enc_scr[pl.ds(begin * block_frames + first, block_frames), :]
    act = jnp.tanh(enc[:, None, :] + pred_ref[...].astype(F32)[None, :, :])
    d_pre = d_hidden.reshape(block_frames, tok_slots, width) * (1.0 - act * act)
    ge_scr[pl.ds(first, block_frames), :] = jnp.sum(d_pre, axis=1)
    gp_scr[...] += jnp.sum(d_pre, axis=0)

    @pl.when(step == steps - 1)
    def _():
        ge_ref[...] = ge_scr[...].astype(BF16)
        gp_ref[...] = gp_scr[...].astype(gp_ref.dtype)


PIECES = 4


def final_kernel(mine, *refs):
    sources = refs[:CHAINS]
    out_ref, bias_ref, wide, bias_wide, sems = refs[-5:]
    width, part = wide.shape
    core = lax.axis_index("dp") & 1
    cols = pl.ds(pl.multiple_of((core if mine else 1 - core) * part, part), part)
    span = part // CHAINS
    size = width // PIECES
    copies = []
    for c, source in enumerate(sources):
        extra = source[width:, :].astype(F32)
        bias_wide[:, c * span : (c + 1) * span] = extra[0:1] + extra[1:2]
    copies.append(pltpu.make_async_copy(bias_wide, bias_ref.at[:, cols], sems.at[PIECES]))
    copies[0].start()
    for p in range(PIECES):
        rows = slice(p * size, (p + 1) * size)
        for c, source in enumerate(sources):
            wide[rows, c * span : (c + 1) * span] = source[rows, :].astype(F32)
        copies.append(
            pltpu.make_async_copy(wide.at[rows], out_ref.at[rows, cols], sems.at[p])
        )
        copies[-1].start()
    for copy in copies:
        copy.wait()


def widen(sources, width, vocab, mine, before):
    part = vocab // 2
    anywhere = pl.BlockSpec(memory_space=pl.ANY)
    return pl.pallas_call(
        functools.partial(final_kernel, mine),
        in_specs=[pl.BlockSpec(memory_space=pltpu.VMEM)] * CHAINS + [anywhere] * len(before),
        out_specs=[anywhere, anywhere],
        out_shape=[
            pltpu.HBM((width, vocab), F32), pltpu.HBM((1, vocab), F32)
        ],
        scratch_shapes=[
            pltpu.VMEM((width, part), F32), pltpu.VMEM((1, part), F32),
            pltpu.SemaphoreType.DMA((PIECES + 1,)),
        ],
        input_output_aliases={CHAINS + k: k for k in range(len(before))},
        compiler_params=pltpu.CompilerParams(vmem_limit_bytes=8 * 1024 * 1024),
    )(*sources, *before)


def whole(shape):
    return pl.BlockSpec(shape, lambda *_: (0,) * len(shape))


SMEM_SPEC = pl.BlockSpec(memory_space=pltpu.SMEM)


def forward(tlen, labels, enc, pred, w, bias, rows, begin, blocks, before):
    frames, width = enc.shape
    tok_slots = pred.shape[0]
    vocab = w.shape[1]
    cells = frames * tok_slots
    return pl.pallas_call(
        functools.partial(forward_kernel, begin),
        grid=(blocks,),
        in_specs=[
            SMEM_SPEC, whole(labels.shape), whole(enc.shape), whole(pred.shape),
            whole(w.shape), whole(bias.shape),
        ] + [pl.BlockSpec(memory_space=pl.ANY)] * len(before),
        out_specs=[
            pl.BlockSpec((rows, vocab), lambda i: (i + begin, 0)),
            pl.BlockSpec((8, rows), lambda i: (0, i + begin)),
            pl.BlockSpec((width, rows), lambda i: (0, i + begin)),
        ],
        out_shape=[
            jax.ShapeDtypeStruct((cells, vocab), F32),
            jax.ShapeDtypeStruct((8, cells), F32),
            jax.ShapeDtypeStruct((width, cells), BF16),
        ],
        scratch_shapes=[pltpu.VMEM((frames, width), F32), pltpu.VMEM((2, SUB, vocab), F32)],
        input_output_aliases={6 + k: k for k in range(len(before))},
        compiler_params=params(16),
    )(tlen, in_vmem(labels), in_vmem(enc), in_vmem(pred), in_vmem(w), in_vmem(bias), *before)


def gradients(pick, flen, tlen, labels, qa, qb, e, st, jt, rows):
    cells, vocab = e.shape
    width = jt.shape[0]
    part = vocab // 2
    blocks = cells // rows

    def at(i):
        return jnp.minimum(i, blocks - 1)

    smem = pl.BlockSpec(memory_space=pltpu.SMEM)
    grid_spec = pltpu.PrefetchScalarGridSpec(
        num_scalar_prefetch=1,
        grid=(blocks + 1,),
        in_specs=[
            smem, smem, whole(labels.shape),
            pl.BlockSpec((1, 3, rows), lambda i, pick: (lax.rem(pick[0], pick[1]), 0, at(i))),
            pl.BlockSpec((1, 3, rows), lambda i, pick: (lax.rem(pick[0], pick[1]), 0, at(i))),
            pl.BlockSpec((rows, vocab), lambda i, pick: (at(i), 0)),
            pl.BlockSpec((8, rows), lambda i, pick: (0, at(i))),
            pl.BlockSpec((width, rows), lambda i, pick: (0, jnp.maximum(i - 1, 0))),
        ],
        out_specs=[
            pl.BlockSpec((rows, vocab), lambda i, pick: (at(i), 0)),
            whole((1, 1)),
            whole((width + EXTRA, part)),
            whole((width + EXTRA, part)),
        ],
        scratch_shapes=[
            pltpu.VMEM((rows, vocab), BF16),
            pltpu.VMEM((rows, vocab), BF16),
            pltpu.VMEM((width, vocab), F32),
            pltpu.VMEM((8, vocab), F32),
            pltpu.VMEM((1, rows), F32),
            pltpu.VMEM((rows, LANES), jnp.int32),
        ],
    )
    return pl.pallas_call(
        functools.partial(grad_kernel, blocks),
        grid_spec=grid_spec,
        out_shape=[
            pltpu.HBM((cells, vocab), BF16),
            jax.ShapeDtypeStruct((1, 1), F32),
            jax.ShapeDtypeStruct((width + EXTRA, part), BF16),
            jax.ShapeDtypeStruct((width + EXTRA, part), F32),
        ],
        compiler_params=params(20),
    )(pick, flen, tlen, in_vmem(labels), qa, qb, e, st, jt)


def input_gradients(enc, pred, d_low, w, rows, begin, last, before):
    frames, width = enc.shape
    vocab = d_low.shape[1]
    cells = frames // 2 * pred.shape[0]
    half = (frames // 2, width)
    extra = () if not before else (before[1], before[0])
    return pl.pallas_call(
        functools.partial(input_kernel, begin, last),
        grid=(cells // rows,),
        in_specs=[
            whole(enc.shape), whole(pred.shape),
            pl.BlockSpec((rows, vocab), lambda i: (i + begin, 0)), whole(w.shape),
        ] + ([whole(pred.shape), pl.BlockSpec(memory_space=pl.ANY)] if before else []),
        out_specs=[pl.BlockSpec(half, lambda i: (1 if last else 0, 0)), whole(pred.shape)],
        out_shape=[
            jax.ShapeDtypeStruct(enc.shape, BF16),
            jax.ShapeDtypeStruct(pred.shape, BF16 if last else F32),
        ],
        scratch_shapes=[
            pltpu.VMEM(enc.shape, F32), pltpu.VMEM(half, F32), pltpu.VMEM(pred.shape, F32)
        ],
        input_output_aliases={5: 0} if before else {},
        compiler_params=params(12),
    )(in_vmem(enc), in_vmem(pred), pltpu.with_memory_space_constraint(d_low, pltpu.HBM), in_vmem(w), *extra)


def merge_kernel(even, odd, keep_ref, got_ref, acc_ref, send_ref, bias_ref):
    own = lax.axis_index("dp")
    mask = jnp.where((own & 1) == 0, even, odd)
    side = jnp.where((own & mask) != 0, 1, 0)
    count, part = acc_ref.shape
    stay = pl.ds(pl.multiple_of(side * count, count), count)
    leave = pl.ds(pl.multiple_of((1 - side) * count, count), count)
    send_ref[:count, :] = (keep_ref[leave, :] + got_ref[leave, :].astype(F32)).astype(BF16)
    acc_ref[...] = keep_ref[stay, :] + got_ref[stay, :].astype(F32)
    rows = got_ref[2 * count :, :].astype(F32)
    bias = keep_ref[2 * count : 2 * count + 1, :] + rows[0:1] + rows[1:2]
    high = bias.astype(BF16).astype(F32)
    low = (bias - high).astype(BF16).astype(F32)
    bias_ref[...] = high + low
    place = lax.broadcasted_iota(jnp.int32, (EXTRA, part), 0)
    packed = jnp.where(place == 0, high, jnp.where(place == 1, low, 0.0))
    send_ref[count:, :] = packed.astype(BF16)


def merge(keep, got, even, odd):
    rows, part = got.shape
    count = (rows - EXTRA) // 2
    return pl.pallas_call(
        functools.partial(merge_kernel, even, odd),
        grid=(1,),
        in_specs=[whole(keep.shape), whole(got.shape)],
        out_specs=[whole((count, part)), whole((count + EXTRA, part)), whole((1, part))],
        out_shape=[
            jax.ShapeDtypeStruct((count, part), F32),
            jax.ShapeDtypeStruct((count + EXTRA, part), BF16),
            jax.ShapeDtypeStruct((1, part), F32),
        ],
        compiler_params=params(12),
    )(keep, got)


def split_two(value):
    high = lax.reduce_precision(value, 8, 7)
    return high, lax.reduce_precision(value - high, 8, 7)


def on_device(
    dp, teacher_post, assignment, encoder_out, predictor_out, frame_lengths, token_lengths,
    labels, out_weight, out_bias,
):
    own = lax.axis_index("dp")
    core = own & 1
    masks = [1 << k for k in range(dp.bit_length() - 1)]
    tok_slots = predictor_out.shape[1]
    rows = 16 * tok_slots
    width, vocab = out_weight.shape
    part = vocab // 2

    def exchange(value, even, odd):
        pairs = [(k, k ^ (odd if k & 1 else even)) for k in range(dp)]
        return lax.ppermute(value, "dp", pairs)

    blocks = encoder_out.shape[1] * tok_slots // rows
    quarter = blocks // 4
    shares = [(0, quarter), (quarter, quarter), (2 * quarter, blocks - 2 * quarter)]
    held, made = teacher_post, ()
    staged = stage(
        assignment, out_weight, encoder_out[0], predictor_out[0], out_bias.reshape(1, vocab), labels,
        teacher_post,
    )
    for k, mask in enumerate(masks):
        got = exchange(held, mask, mask)
        part_no = k - (len(masks) - len(shares))
        if part_no >= 0:
            begin, number = shares[part_no]
            made = tuple(forward(
                token_lengths, label_row, enc, pred, weight, bias_row, rows, begin, number, made
            ))
        if k == 0:
            got, staged = lax.optimization_barrier((got, staged))
            held = staged[5]
        if k < len(masks) - 1:
            held = jnp.concatenate([held, got], axis=0)
            held, made, staged = lax.optimization_barrier((held, made, staged))
            weight, enc, pred, bias_row, label_row, _, pick = staged
    far = got
    e, st, jt = made
    d_low, loss, send, keep = gradients(
        pick, frame_lengths, token_lengths, label_row, held, far, e, st, jt, rows
    )
    got = exchange(send, 1, 1)

    def got_bias(rows_of):
        return rows_of[0:1].astype(F32) + rows_of[1:2].astype(F32)

    def bias_rows(high, low):
        filler = jnp.zeros((EXTRA - 2, high.shape[1]), BF16)
        return jnp.concatenate([high.astype(BF16), low.astype(BF16), filler], axis=0)

    rest = masks[1:]
    even_order = rest
    odd_order = rest[1:2] + rest[:1] + rest[2:]
    orders = list(zip(even_order, odd_order))
    sides = []
    count = width
    done = ()
    acc, send, bias = merge(keep, got, *orders[0])
    for k, (even, odd) in enumerate(orders[:-1]):
        side = (own & jnp.where(core == 0, even, odd)) != 0
        sides.append(side)
        count //= 2
        if k:
            high, low = split_two(bias)
            top, bottom = acc[:count], acc[count:]
            send = jnp.where(side, top, bottom).astype(BF16)
            acc = jnp.where(side, bottom, top)
            send = jnp.concatenate([send, bias_rows(high, low)], axis=0)
            bias = high + low
        if k < 2:
            send, acc, d_low = lax.optimization_barrier((send, acc, d_low))
        got = exchange(send, even, odd)
        if k < 2:
            done = input_gradients(
                enc, pred, d_low, weight, rows, k * (blocks // 2), k == 1, done
            )
            got, done = lax.optimization_barrier((got, done))
        acc = acc + got[:count].astype(F32)
        bias = bias + got_bias(got[count:])
    chains = range(CHAINS)
    span = part // CHAINS
    even, odd = orders[-1]
    sums, kept, parts = [], [], []
    for c in chains:
        cols = slice(c * span, (c + 1) * span)
        high, low = split_two(bias[:, cols])
        sums.append((high, low))
        sent = acc[:, cols].astype(BF16)
        kept.append(lax.reduce_precision(acc[:, cols], 8, 7))
        parts.append(exchange(jnp.concatenate([sent, bias_rows(high, low)], axis=0), even, odd))
    have = []
    for c in chains:
        got = parts[c]
        if c:
            got, have = lax.optimization_barrier((got, have))
        have.append((kept[c] + got[:count].astype(F32)).astype(BF16))
        high, low = sums[c]
        sums[c] = split_two((high + low) + got_bias(got[count:]))
    for (even, odd), side in list(zip(orders, sides))[::-1]:
        parts = [exchange(have[c], even, odd) for c in chains]
        joined = []
        for c in chains:
            if c:
                parts[c], joined = lax.optimization_barrier((parts[c], joined))
            joined.append(jnp.where(
                side,
                jnp.concatenate([parts[c], have[c]], axis=0),
                jnp.concatenate([have[c], parts[c]], axis=0),
            ))
        have = joined
    sent = [jnp.concatenate([have[c], bias_rows(*sums[c])], axis=0) for c in chains]
    others = [exchange(sent[c], 1, 1) for c in chains]
    result = tuple(widen(sent, width, vocab, True, ()))
    others, result = lax.optimization_barrier((others, result))
    result = tuple(widen(others, width, vocab, False, result))
    grad_weight, grad_bias = result
    return (loss.reshape(1), grad_weight, grad_bias.reshape(vocab), done[0][None], done[1][None])


def solution(mesh):
    in_specs = (
        P(("groups", "dp"), None, None),
        P("groups"),
        P(("groups", "dp"), None, None),
        P(("groups", "dp"), None, None),
        P(("groups", "dp")),
        P(("groups", "dp")),
        P(("groups", "dp"), None),
        P(),
        P(),
    )
    out_specs = (
        P(("groups", "dp")),
        P("groups", None),
        P("groups"),
        P(("groups", "dp"), None, None),
        P(("groups", "dp"), None, None),
    )
    return jax.shard_map(
        functools.partial(on_device, mesh.shape["dp"]),
        mesh=mesh, in_specs=in_specs, out_specs=out_specs, check_vma=False,
    )
```
